32 devices in a mesh: dp: 16 (over z, y, core), chan: 2 (over x).
Axes of the slice: x: 2, y: 2, z: 4, core: 2. Of those that a mesh axis runs over, the one named last changes fastest.
Arguments:
- features: bfloat16 [16, 512, 4096], P('dp', 'chan'), may hold values from -6 to 6
- crop_ids: int32 [16, 64, 64], P('dp'), may hold values from 0 to 15, as said below
- cotangent: bfloat16 [16, 512, 4096], P('dp', 'chan'), may hold values from -6 to 6
- norm1_gain: float32 [512], P('chan'), may hold values from 0.5 to 1.5
- norm1_bias: float32 [512], P('chan'), may hold values from -3 to 3
- conv1_weight: bfloat16 [9, 512, 512], P(None, 'chan'), may hold values from -0.09375 to 0.09375
- conv1_bias: float32 [512], P('chan'), may hold values from -3 to 3
- norm2_gain: float32 [512], P('chan'), may hold values from 0.5 to 1.5
- norm2_bias: float32 [512], P('chan'), may hold values from -3 to 3
- conv2_weight: bfloat16 [9, 512, 512], P(None, 'chan'), may hold values from -0.09375 to 0.09375
- conv2_bias: float32 [512], P('chan'), may hold values from -3 to 3
- norm3_gain: float32 [512], P('chan'), may hold values from 0.5 to 1.5
- norm3_bias: float32 [512], P('chan'), may hold values from -3 to 3
- query_weight: bfloat16 [512, 512], P('chan'), may hold values from -0.25 to 0.25
- query_bias: float32 [512], P('chan'), may hold values from -3 to 3
- key_weight: bfloat16 [512, 512], P('chan'), may hold values from -0.25 to 0.25
- value_weight: bfloat16 [512, 512], P('chan'), may hold values from -0.25 to 0.25
- value_bias: float32 [512], P('chan'), may hold values from -3 to 3
- proj_weight: bfloat16 [512, 512], P('chan'), may hold values from -1 to 1
- proj_bias: float32 [512], P('chan'), may hold values from -3 to 3
Outputs:
- output: bfloat16 [16, 512, 4096], P('dp', 'chan')
- input_grad: float32 [16, 512, 4096], P('dp', 'chan')
- norm1_gain_grad: float32 [512], P('chan')
- norm1_bias_grad: float32 [512], P('chan')
- conv1_weight_grad: float32 [9, 512, 512], P(None, 'chan')
- conv1_bias_grad: float32 [512], P('chan')
- norm2_gain_grad: float32 [512], P('chan')
- norm2_bias_grad: float32 [512], P('chan')
- conv2_weight_grad: float32 [9, 512, 512], P(None, 'chan')
- conv2_bias_grad: float32 [512], P('chan')
- norm3_gain_grad: float32 [512], P('chan')
- norm3_bias_grad: float32 [512], P('chan')
- query_weight_grad: float32 [512, 512], P('chan')
- query_bias_grad: float32 [512], P('chan')
- key_weight_grad: float32 [512, 512], P('chan')
- value_weight_grad: float32 [512, 512], P('chan')
- value_bias_grad: float32 [512], P('chan')
- proj_weight_grad: float32 [512, 512], P('chan')
- proj_bias_grad: float32 [512], P('chan')
The draws below stay inside these ranges and needn't reach their ends.
Inputs may be any that keep to these rules, and one draw needn't show every extreme that they name: `crop_ids`: in each canvas the 16 crops are rectangles laid out as 4 bands of rows by 4 bands of columns, numbered 4 * row band + column band; every band spans a whole multiple of 8 rows or columns, at least 8.
All inputs are finite; a program needn't handle non-finite values.
Results may differ from the reference program's by a relative error of at most 0.023.
Values may be sent and summed in bfloat16 or wider, within the bound.
No kernel may reach another device: no remote copies, remote signals or barrier semaphores. Data moves between devices by JAX's collectives and lax.ppermute only.
A program may use at most 320 MiB of HBM per device.

```python
import jax
import jax.numpy as jnp
from jax import lax

CH = 512
GROUPS = 32
SIDE = 64
CROPS = 16
PIXELS = 4096
CANVASES = 16


def band_index(band_key):
    band_unit = SIDE // 8
    position = jnp.arange(SIDE) // band_unit
    ranking = jax.random.randint(band_key, (CANVASES, 7), 0, 1 << 20) * 8 + jnp.arange(7)[None, :]
    picked = jnp.argsort(ranking, axis=1)[:, :3] + 1
    return jnp.sum((position[None, :, None] >= picked[:, None, :]).astype(jnp.int32), axis=2)


def draw_crop_ids(key, part):
    key = jax.random.fold_in(key, 7)
    row_key, col_key = jax.random.split(key)
    row_band = band_index(row_key)
    col_band = band_index(col_key)
    return (row_band[:, :, None] * 4 + col_band[:, None, :]).astype(jnp.int32)


def levels(stream_key, extent, pieces, smallest, top_value):
    factor_of = 1.0
    for axis_at, shards_of in pieces:
        heights = jax.random.uniform(jax.random.fold_in(jax.random.fold_in(stream_key, 6), axis_at), (shards_of,), jnp.float32, smallest / len(pieces), top_value / len(pieces))
        factor_of = factor_of * jnp.repeat(jnp.exp(heights), extent[axis_at] // shards_of).reshape((-1,) + (1,) * (len(extent) - 1 - axis_at))
    return factor_of


def noise(own_key, dims, scale, reach, pieces=(), kind=jnp.bfloat16):
    values = jax.random.normal(own_key, dims, jnp.float32) * scale
    if len(pieces) > 0:
        values = levels(own_key, dims, pieces, -0.22, 0.18) * values
    return jnp.clip(values, min=-reach, max=reach).astype(kind)


def setup_inputs(seed: int = 0) -> dict:
    streams_of = jax.random.split(jax.random.key(seed), 21)
    return {
        "features": noise(streams_of[0], (CANVASES, CH, PIXELS), 1.0, 6.0, ((0, 16), (1, 2))),
        "crop_ids": draw_crop_ids(jax.random.fold_in(streams_of[20], 71), 0),
        "cotangent": noise(streams_of[2], (CANVASES, CH, PIXELS), 1.0, 6.0, ((0, 16), (1, 2))),
        "norm1_gain": jnp.clip(0.5 + 1.0 * jax.random.uniform(streams_of[3], (CH,), jnp.float32) ** levels(streams_of[3], (CH,), ((0, 2),), -0.2, 0.2), 0.5, 1.5),
        "norm1_bias": noise(streams_of[4], (CH,), 0.5, 3.0, ((0, 2),), jnp.float32),
        "conv1_weight": noise(streams_of[5], (9, CH, CH), (9 * CH) ** -0.5, 0.09375, ((1, 2),)),
        "conv1_bias": noise(streams_of[6], (CH,), 0.5, 3.0, ((0, 2),), jnp.float32),
        "norm2_gain": jnp.clip(0.5 + 1.0 * jax.random.uniform(streams_of[7], (CH,), jnp.float32) ** levels(streams_of[7], (CH,), ((0, 2),), -0.2, 0.2), 0.5, 1.5),
        "norm2_bias": noise(streams_of[8], (CH,), 0.5, 3.0, ((0, 2),), jnp.float32),
        "conv2_weight": noise(streams_of[9], (9, CH, CH), (9 * CH) ** -0.5, 0.09375, ((1, 2),)),
        "conv2_bias": noise(streams_of[10], (CH,), 0.5, 3.0, ((0, 2),), jnp.float32),
        "norm3_gain": jnp.clip(0.5 + 1.0 * jax.random.uniform(streams_of[11], (CH,), jnp.float32) ** levels(streams_of[11], (CH,), ((0, 2),), -0.2, 0.2), 0.5, 1.5),
        "norm3_bias": noise(streams_of[12], (CH,), 0.5, 3.0, ((0, 2),), jnp.float32),
        "query_weight": noise(streams_of[13], (CH, CH), CH ** -0.5, 0.25, ((0, 2),)),
        "query_bias": noise(streams_of[14], (CH,), 0.5, 3.0, ((0, 2),), jnp.float32),
        "key_weight": noise(streams_of[15], (CH, CH), CH ** -0.5, 0.25, ((0, 2),)),
        "value_weight": noise(streams_of[16], (CH, CH), CH ** -0.5, 0.25, ((0, 2),)),
        "value_bias": noise(streams_of[17], (CH,), 0.5, 3.0, ((0, 2),), jnp.float32),
        "proj_weight": noise(streams_of[18], (CH, CH), (CH // 16) ** -0.5, 1.0, ((0, 2),)),
        "proj_bias": noise(streams_of[19], (CH,), 0.5, 3.0, ((0, 2),), jnp.float32),
    }


@jax.custom_vjp
def low(v):
    return lax.optimization_barrier(v.astype(jnp.bfloat16)).astype(jnp.float32)

@jax.custom_vjp
def low_back(v):
    return v

def low_keep(v):
    return (low(v), None)

def low_pass(kept, grad):
    return (grad,)

def back_keep(v):
    return (v, None)

def back_low(kept, grad):
    return (low(grad),)
low.defvjp(low_keep, low_pass)
low_back.defvjp(back_keep, back_low)
epsilon = 1e-06
highest = lax.Precision.HIGHEST

def crop_mean(crop_table, signal):
    group_width = CH // GROUPS
    summed = jnp.dot(crop_table.T, signal, precision=highest)
    grouped = lax.optimization_barrier(jnp.sum(summed.reshape(summed.shape[0], -1, group_width), axis=2))
    counted = lax.optimization_barrier(jnp.sum(crop_table, axis=0))[:, None] * group_width
    spread = jnp.repeat(grouped / counted, group_width, axis=1)
    return jnp.dot(crop_table, spread, precision=highest)

def group_norm(signal, crop_table, norm_gain, offset):
    centred = signal - crop_mean(crop_table, signal)
    scaled = centred * lax.rsqrt(crop_mean(crop_table, centred * centred) + epsilon)
    return scaled * norm_gain + offset

def swish(signal):
    return signal * jax.nn.sigmoid(signal)

def convolve(active, weight, offset, crop_grid):
    canvas_side = crop_grid.shape[0]
    padded = jnp.pad(active, ((1, 1), (1, 1), (0, 0)))
    padded_crops = jnp.pad(crop_grid, 1, constant_values=-1)
    result = offset
    for tap_index in range(9):
        row_step, col_step = (tap_index // 3 - 1, tap_index % 3 - 1)
        nearby = padded[1 + row_step:1 + row_step + canvas_side, 1 + col_step:1 + col_step + canvas_side]
        inside = padded_crops[1 + row_step:1 + row_step + canvas_side, 1 + col_step:1 + col_step + canvas_side] == crop_grid
        masked = jnp.where(inside[:, :, None], nearby, 0.0)
        result = result + jnp.dot(masked.reshape(canvas_side * canvas_side, -1), weight[tap_index].T, precision=highest)
    return result

def forward(params, canvas, crop_grid):
    norm1_gain, norm1_bias, conv1_weight, conv1_bias, norm2_gain, norm2_bias, conv2_weight, conv2_bias, norm3_gain, norm3_bias, query_weight, query_bias, key_weight, value_weight, value_bias, proj_weight, proj_bias = params
    canvas_side = crop_grid.shape[0]
    pixels = canvas_side * canvas_side
    flat_crops = crop_grid.reshape(pixels)
    crop_table = (flat_crops[:, None] == jnp.arange(CROPS)[None, :]).astype(jnp.float32)
    inputs = canvas.T
    active1 = low(swish(group_norm(inputs, crop_table, norm1_gain, norm1_bias)))
    hidden1 = low_back(convolve(active1.reshape(canvas_side, canvas_side, -1), conv1_weight, conv1_bias, crop_grid))
    active2 = low(swish(group_norm(hidden1, crop_table, norm2_gain, norm2_bias)))
    hidden2 = low_back(convolve(active2.reshape(canvas_side, canvas_side, -1), conv2_weight, conv2_bias, crop_grid))
    residual = inputs + hidden2
    normed = low(group_norm(residual, crop_table, norm3_gain, norm3_bias))
    query_rows = low(low_back(jnp.dot(normed, query_weight.T, precision=highest) + query_bias))
    key_rows = low(low_back(jnp.dot(normed, key_weight.T, precision=highest)))
    value_rows = low(low_back(jnp.dot(normed, value_weight.T, precision=highest) + value_bias))
    scores = low_back(jnp.dot(query_rows, key_rows.T, precision=highest) * CH ** (-0.5))
    same_crop = flat_crops[:, None] == flat_crops[None, :]
    scores = jnp.where(same_crop, scores, -1e+30)
    weights = low(jax.nn.softmax(scores, axis=1))
    mixed_rows = low(low_back(jnp.dot(weights, value_rows, precision=highest)))
    output = residual + jnp.dot(mixed_rows, proj_weight.T, precision=highest) + proj_bias
    return output.T

def reference(features, crop_ids, cotangent, norm1_gain, norm1_bias, conv1_weight, conv1_bias, norm2_gain, norm2_bias, conv2_weight, conv2_bias, norm3_gain, norm3_bias, query_weight, query_bias, key_weight, value_weight, value_bias, proj_weight, proj_bias):
    params = tuple((member.astype(jnp.float32) for member in (norm1_gain, norm1_bias, conv1_weight, conv1_bias, norm2_gain, norm2_bias, conv2_weight, conv2_bias, norm3_gain, norm3_bias, query_weight, query_bias, key_weight, value_weight, value_bias, proj_weight, proj_bias)))

    def one_canvas(running, sliced):
        canvas, crop_grid, tangent = sliced
        output, pull_back = jax.vjp(lambda weights, picture: forward(weights, picture, crop_grid), params, canvas.astype(jnp.float32))
        param_grads, input_grad = pull_back(tangent.astype(jnp.float32))
        running = jax.tree.map(jnp.add, running, param_grads)
        return (running, (output.astype(jnp.bfloat16), input_grad))
    starting = tuple((jnp.zeros_like(member) for member in params))
    summed, (outputs, input_grads) = lax.scan(one_canvas, starting, (features, crop_ids, cotangent))
    return (outputs, input_grads, summed[0], summed[1], summed[2], summed[3], summed[4], summed[5], summed[6], summed[7], summed[8], summed[9], summed[10], summed[11], summed[12], summed[13], summed[14], summed[15], summed[16])
```

```python
import functools
import itertools

import jax
import jax.numpy as jnp
import numpy as np
from jax import lax
from jax.experimental import pallas as pl
from jax.experimental.pallas import tpu as pltpu
from jax.sharding import PartitionSpec as P

CH = 512
GROUPS = 32
CROPS = 16
TILE = 8
BANDS = 4
EPS = 1e-06
F32 = jnp.float32
BF16 = jnp.bfloat16
HIGH = lax.Precision.HIGHEST
NN = (((1,), (0,)), ((), ()))
NT = (((1,), (1,)), ((), ()))
TN = (((0,), (0,)), ((), ()))
VMEM = pltpu.VMEM
ANY = pl.ANY
SCALE = CH ** (-0.5)


def band_layouts(units):
    return [
        tuple(np.diff((0,) + cuts + (units,)))
        for cuts in itertools.combinations(range(1, units), BANDS - 1)
    ]


@functools.lru_cache(maxsize=None)
def owner_tables(devices, units, slots):
    layouts = band_layouts(units)
    rank = np.zeros(1 << (units - 1), np.int32)
    for number, sizes in enumerate(layouts):
        cuts = np.cumsum(sizes)[:-1]
        rank[sum(1 << (int(c) - 1) for c in cuts)] = number
    sizes = np.array(
        [[r * c for r in rows for c in cols] for rows in layouts for cols in layouts], np.int32
    )
    owners = np.zeros(sizes.shape, np.int32)
    if devices == 2:
        masks = np.arange(1 << (CROPS - 1), dtype=np.int32)
        bits = ((masks[None, :] >> np.arange(CROPS)[:, None]) & 1).astype(np.float32)
        for at, row in enumerate(sizes.astype(np.float32)):
            filled = row @ bits
            squares = (row * row) @ bits
            cost = np.abs(squares - (row * row).sum() / 2) + 1e6 * np.abs(filled - slots)
            owners[at] = bits[:, int(np.argmin(cost))].astype(np.int32)
    else:
        for at, row in enumerate(sizes):
            loads = [0] * devices
            for crop in sorted(range(CROPS), key=lambda c: -row[c]):
                device = loads.index(min(loads))
                owners[at, crop] = device
                loads[device] += int(row[crop])
    for device in range(devices):
        assert (np.where(owners == device, sizes, 0).sum(axis=1) <= slots).all()
    return rank, owners


def packed_tables(devices, units, slots):
    rank, owners = owner_tables(devices, units, slots)
    shifts = np.arange(0, 32, 4, dtype=np.int64)
    words = (owners.reshape(-1, 2, 8).astype(np.int64) << shifts).sum(axis=2)
    words = np.where(words >= 1 << 31, words - (1 << 32), words)
    return np.concatenate([rank, words.reshape(-1).astype(np.int32)])


WINDOWS = (8, 16, 24, 32)


def write_plan(devices, slots, ids, table, slot_tile, slot_crop, starts, ends):
    units = ids.shape[0] // TILE
    count = units * units
    layouts = len(band_layouts(units))

    def code(at):
        bits = 0
        for step in range(units - 1):
            bits = bits + jnp.where(at(step) != at(step + 1), 1 << step, 0)
        return table[bits]

    def row_id(step):
        return ids[TILE * step, 0]

    def col_id(step):
        return ids[0, TILE * step]

    layout = code(row_id) * layouts + code(col_id)
    words = [table[(1 << (units - 1)) + 2 * layout + half] for half in range(2)]
    heights, widths = [], []
    for band in range(BANDS):
        heights.append(sum(jnp.where(row_id(k) // BANDS == band, 1, 0) for k in range(units)))
        widths.append(sum(jnp.where(col_id(k) % BANDS == band, 1, 0) for k in range(units)))
    if devices * slots > count:

        def clear(at, carry):
            slot_tile[at] = -1
            slot_crop[at] = -1
            return carry

        lax.fori_loop(0, devices * slots, clear, 0)
    filled = [jnp.int32(device * slots) for device in range(devices)]
    for crop in range(CROPS):
        owner = lax.shift_right_logical(words[crop // 8], jnp.int32(4 * (crop % 8))) & 15
        size = heights[crop // BANDS] * widths[crop % BANDS]
        start = filled[0]
        for device in range(1, devices):
            start = jnp.where(owner == device, filled[device], start)
        starts[crop] = start
        ends[crop] = start
        for device in range(devices):
            filled[device] = filled[device] + jnp.where(owner == device, size, 0)

    def place(row, carry):
        for col in range(units):
            crop = ids[row * TILE, col * TILE]
            at = ends[crop]
            slot_tile[at] = row * units + col
            slot_crop[at] = crop
            ends[crop] = at + 1
        return carry

    lax.fori_loop(0, units, place, 0)


class Plan:
    def __init__(self, me, slot_tile, slot_crop, slots):
        self.slots = slots
        base = me * slots
        lane = lax.broadcasted_iota(jnp.int32, (1, 128), 1) % slots
        down = lax.broadcasted_iota(jnp.int32, (slots, 1), 0)
        self.tile_row, self.crop_row = jnp.zeros_like(lane), jnp.zeros_like(lane)
        self.tile_col, self.crop_col = jnp.zeros_like(down), jnp.zeros_like(down)
        for slot in range(slots):
            tile, crop = slot_tile[base + slot], slot_crop[base + slot]
            self.tile_row = jnp.where(lane == slot, tile, self.tile_row)
            self.crop_row = jnp.where(lane == slot, crop, self.crop_row)
            self.tile_col = jnp.where(down == slot, tile, self.tile_col)
            self.crop_col = jnp.where(down == slot, crop, self.crop_col)
        self.same = (self.crop_col == self.crop_row[:, 0:slots]).astype(F32)


def place_of(position):
    return position[0], position[1], position[2], position[3]


def group_total(value):
    width = CH // GROUPS
    lane = lax.broadcasted_iota(jnp.int32, (value.shape[0], 128), 1)
    parts = []
    for at in range(0, CH, 128):
        part = value[:, at : at + 128]
        step = 1
        while step < width:
            up = pltpu.roll(part, 128 - step, 1)
            down = pltpu.roll(part, step, 1)
            part = part + jnp.where((lane & step) == 0, up, down)
            step *= 2
        parts.append(part)
    return jnp.concatenate(parts, axis=1)


def crop_mean(same, value):
    count = jnp.sum(same, axis=1, keepdims=True) * float(TILE * TILE * (CH // GROUPS))
    total = lax.dot_general(same, group_total(value), NN, precision=HIGH, preferred_element_type=F32)
    return total / count


def slab_sum(pixels, slots, term):
    def step(at, total):
        return total + term(at)

    return lax.fori_loop(0, pixels, step, jnp.zeros((slots, CH), F32), unroll=8)


def stats_slabs(ref, same):
    pixels, slots, _ = ref.shape
    mean = crop_mean(same, slab_sum(pixels, slots, lambda at: ref[at]))

    def square(at):
        centred = ref[at] - mean
        return centred * centred

    inverse = lax.rsqrt(crop_mean(same, slab_sum(pixels, slots, square)) + EPS)
    return mean, inverse


def fill_halo(pad, plan):
    slots = plan.slots
    wide = TILE * slots
    tile_c = jnp.concatenate([plan.tile_col] * TILE, axis=0)
    crop_c = jnp.concatenate([plan.crop_col] * TILE, axis=0)
    tile_r = jnp.concatenate([plan.tile_row] * (wide // 128), axis=1)
    crop_r = jnp.concatenate([plan.crop_row] * (wide // 128), axis=1)
    block_c = lax.broadcasted_iota(jnp.int32, (wide, wide), 0) // slots
    block_r = lax.broadcasted_iota(jnp.int32, (wide, wide), 1) // slots
    linked = (crop_c == crop_r) & (tile_c >= 0)

    def near(row_step, col_step):
        return linked & (tile_r == tile_c + (TILE * row_step + col_step))

    def edge(row_step, col_step, source):
        pick = (near(row_step, col_step) & (block_c == block_r)).astype(F32).astype(BF16)
        moved = jnp.dot(pick, source.reshape(wide, CH), preferred_element_type=F32).astype(BF16)
        return moved.reshape(TILE, slots, CH)

    def corner(row_step, col_step, source):
        pick = near(row_step, col_step)[0:slots, 0:slots].astype(F32).astype(BF16)
        return jnp.dot(pick, source, preferred_element_type=F32).astype(BF16)

    low, high, end = 1, TILE, TILE + 1
    pad[0, low:end] = edge(-1, 0, pad[high, low:end])
    pad[end, low:end] = edge(1, 0, pad[low, low:end])
    pad[low:end, 0] = edge(0, -1, pad[low:end, high])
    pad[low:end, end] = edge(0, 1, pad[low:end, low])
    pad[0, 0] = corner(-1, -1, pad[high, high])
    pad[0, end] = corner(-1, 1, pad[high, low])
    pad[end, 0] = corner(1, -1, pad[low, high])
    pad[end, end] = corner(1, 1, pad[low, low])


class WeightLoad:
    def __init__(self, position, pieces, target, sem):
        self.copies = []
        if len(pieces) == 1:
            self.copies.append(pltpu.make_async_copy(pieces[0], target, sem.at[0]))
        else:
            me = position[0]
            half = pieces[0].shape[1]
            width = pieces[1].shape[1]
            mine = position[1] if len(pieces) == 9 else position[2]
            spots = [me * half]
            for at in range(len(pieces) - 1):
                spots.append((1 - me) * half + (mine ^ at) * width)
            for at, (piece, spot) in enumerate(zip(pieces, spots)):
                rows = pl.ds(pl.multiple_of(spot, width), piece.shape[1])
                self.copies.append(
                    pltpu.make_async_copy(piece, target.at[:, rows, :], sem.at[at])
                )

    def start(self):
        for copy in self.copies:
            copy.start()

    def wait(self):
        for copy in self.copies:
            copy.wait()


def weight_sems(pieces):
    return pltpu.SemaphoreType.DMA((len(pieces),))


def store_grad(grad, outs, work, position, number):
    if len(outs) == 1:
        outs[0][number] = grad.astype(BF16)
    else:
        work[...] = grad
        mine = position[3]
        width = CH // 16
        for at in range(16):
            rows = pl.ds(pl.multiple_of((mine ^ at) * width, width), width)
            part = work[rows, :].astype(BF16)
            core, spot = (at // 4) % 2, (at // 8) * 4 + at % 4
            outs[core][number, spot * width : (spot + 1) * width, :] = part


def grad_shapes(count, paired):
    if paired:
        return [shape((count, CH // 2, CH), BF16)] * 2
    return [shape((count, CH, CH), BF16)]


def conv_rows(pad, weight, row, slots, dims, flipped, count=1):
    total = None
    for tap in range(9):
        down, right = tap // 3, tap % 3
        if flipped:
            down, right = 2 - down, 2 - right
        left = pad[pl.ds(row + down, count), right : right + TILE].reshape(count * TILE * slots, CH)
        part = lax.dot_general(left, weight[tap], dims, preferred_element_type=F32)
        total = part if total is None else total + part
    return total


def load_full(parts, me, dtype, store):
    if len(parts) == 1:
        store(slice(None), parts[0][...].astype(dtype))
    else:
        local = parts[0].shape[-1]
        own = pl.ds(pl.multiple_of(me * local, local), local)
        other = pl.ds(pl.multiple_of((1 - me) * local, local), local)
        store(own, parts[0][...].astype(dtype))
        store(other, parts[1][...].astype(dtype))


def vmem(shape, dtype):
    return pltpu.VMEM(shape, dtype)


def specs(kinds):
    table = {
        "v": pl.BlockSpec(memory_space=pltpu.VMEM),
        "s": pl.BlockSpec(memory_space=pltpu.SMEM),
        "h": pl.BlockSpec(memory_space=pl.ANY),
    }
    return [table[k] for k in kinds]


def call(body, ins, outs, shapes, scratch, name, flops, moved):
    return pl.pallas_call(
        body,
        in_specs=specs(ins),
        out_specs=tuple(specs(outs)),
        out_shape=tuple(shapes),
        scratch_shapes=list(scratch),
        compiler_params=pltpu.CompilerParams(vmem_limit_bytes=60 << 20),
        cost_estimate=pl.CostEstimate(
            flops=int(flops), bytes_accessed=int(moved), transcendentals=0
        ),
        name=name,
    )


def shape(dims, dtype):
    return jax.ShapeDtypeStruct(dims, dtype)


def pack_first_kernel(devices, slots, position, ids, table, signal, *rest):
    plan, rest = rest[:4], rest[4:]
    write_plan(devices, slots, ids, table, *plan)
    pack_kernel(True, slots, position, plan[0], signal, *rest)


def pack_kernel(by_pixel, slots, position, slot_tile, signal, *rest):
    outs, (raster, stage) = rest[:-2], rest[-2:]
    local, pixels = signal.shape
    side = int(pixels**0.5)
    chunk = 512
    cols = local // 128
    for at in range(0, pixels, chunk):
        flipped = signal[:, at : at + chunk].astype(F32).T
        for col in range(cols):
            raster[col, at : at + chunk, :] = flipped[:, col * 128 : (col + 1) * 128]
    for number, out in enumerate(outs):

        def step(slot, carry):
            tile = slot_tile[pack_base(position, number, len(outs), slots) + slot]
            keep = tile >= 0
            tile = jnp.maximum(tile, 0)
            start = (tile // TILE) * (TILE * side) + (tile % TILE) * TILE
            for row in range(TILE):
                for col in range(cols):
                    value = raster[col, pl.ds(pl.multiple_of(start + row * side, TILE), TILE), :]
                    value = jnp.where(keep, value, 0.0)
                    if by_pixel:
                        stage[col, pl.ds(row * TILE * slots + slot, TILE, stride=slots), :] = value
                    else:
                        at = pl.multiple_of(slot * (TILE * TILE) + row * TILE, TILE)
                        stage[col, pl.ds(at, TILE), :] = value
            return carry

        lax.fori_loop(0, slots, step, 0)
        for at in range(0, stage.shape[1], chunk):
            for col in range(cols):
                span = slice(col * 128, (col + 1) * 128)
                out[at : at + chunk, span] = stage[col, at : at + chunk, :].astype(BF16)


def pack_base(position, number, devices, slots):
    return (position[0] ^ number if devices == 2 else number) * slots


def pack_first(position, ids, signal, devices, slots, name):
    local, pixels = signal.shape
    rows = slots * TILE * TILE
    table = jnp.asarray(packed_tables(devices, ids.shape[0] // TILE, slots))
    result = call(
        functools.partial(pack_first_kernel, devices, slots),
        "sssv",
        "ssss" + "v" * devices,
        [shape((devices * slots,), jnp.int32)] * 2
        + [shape((CROPS,), jnp.int32)] * 2
        + [shape((rows, local), BF16)] * devices,
        [vmem((local // 128, pixels, 128), F32), vmem((local // 128, rows, 128), F32)],
        name,
        4 << 30,
        6 << 20,
    )(position, ids, table, signal)
    return result[:4], result[4:]


def pack(position, slot_tile, signal, by_pixel, devices, slots, name):
    local, pixels = signal.shape
    rows = slots * TILE * TILE
    return call(
        functools.partial(pack_kernel, by_pixel, slots),
        "ssv",
        "v" * devices,
        [shape((rows, local), BF16)] * devices,
        [vmem((local // 128, pixels, 128), F32), vmem((local // 128, rows, 128), F32)],
        name,
        4 << 30,
        6 << 20,
    )(position, slot_tile, signal)


def unpack_kernel(by_pixel, slots, position, slot_tile, *rest):
    ins, out, (raster, stage) = rest[:-3], rest[-3], rest[-2:]
    local, pixels = out.shape
    side = int(pixels**0.5)
    chunk = 512
    cols = local // 128
    for number, part in enumerate(ins):
        for at in range(0, stage.shape[1], chunk):
            for col in range(cols):
                span = slice(col * 128, (col + 1) * 128)
                stage[col, at : at + chunk, :] = part[at : at + chunk, span].astype(F32)

        def step(slot, carry):
            tile = slot_tile[pack_base(position, number, len(ins), slots) + slot]

            @pl.when(tile >= 0)
            def _():
                start = (tile // TILE) * (TILE * side) + (tile % TILE) * TILE
                for row in range(TILE):
                    to = pl.ds(pl.multiple_of(start + row * side, TILE), TILE)
                    for col in range(cols):
                        if by_pixel:
                            at = pl.ds(row * TILE * slots + slot, TILE, stride=slots)
                        else:
                            first = pl.multiple_of(slot * (TILE * TILE) + row * TILE, TILE)
                            at = pl.ds(first, TILE)
                        raster[col, to, :] = stage[col, at, :]

            return carry

        lax.fori_loop(0, slots, step, 0)
    for at in range(0, pixels, chunk):
        for col in range(cols):
            span = slice(col * 128, (col + 1) * 128)
            out[span, at : at + chunk] = raster[col, at : at + chunk, :].T.astype(out.dtype)


def unpack(position, slot_tile, parts, pixels, by_pixel, dtype, slots, name):
    rows, local = parts[0].shape
    return call(
        functools.partial(unpack_kernel, by_pixel, slots),
        "ss" + "v" * len(parts),
        "v",
        [shape((local, pixels), dtype)],
        [vmem((local // 128, pixels, 128), F32), vmem((local // 128, rows, 128), F32)],
        name,
        4 << 30,
        8 << 20,
    )(position, slot_tile, *parts)[0]


(G1, B1, C1, G2, B2, C2, G3, B3, QB, VB, PB) = range(11)


def norm_swish_pad(source, mean, inverse, gain, bias, pad, slots):
    scaled = inverse * gain

    def step(row, carry):
        for col in range(TILE):
            before = (source[row * TILE + col] - mean) * scaled + bias
            pad[row + 1, col + 1] = (before * jax.nn.sigmoid(before)).astype(BF16)
        return carry

    lax.fori_loop(0, TILE, step, 0)


def first_kernel(parts, count, position, slot_tile, slot_crop, *rest):
    feature_parts, rest = rest[:parts], rest[parts:]
    par_parts, rest = rest[:parts], rest[parts:]
    pieces, rest = rest[:count], rest[count:]
    (par, feats_hbm, pad1_hbm, hidden_hbm, pad2_hbm, stats1, stats2) = rest[:7]
    feats, wide, hidden, pad1, pad2, weight, weight_sem, sem = rest[7:]
    pixels, slots, _ = wide.shape
    load_weight = WeightLoad(position, pieces, weight, weight_sem)
    load_weight.start()

    def put_par(columns, value):
        par[:, columns] = value

    load_full(par_parts, position[0], F32, put_par)

    def put(columns, value):
        feats[:, columns] = value

    load_full(feature_parts, position[0], BF16, put)
    save_feats = pltpu.make_async_copy(feats, feats_hbm, sem.at[1])
    save_feats.start()

    def widen(at, carry):
        wide[at] = feats[pl.ds(pl.multiple_of(at * slots, slots), slots), :].astype(F32)
        return carry

    lax.fori_loop(0, pixels, widen, 0, unroll=4)
    plan = Plan(position[0], slot_tile, slot_crop, slots)
    mean, inverse = stats_slabs(wide, plan.same)
    stats1[0], stats1[1] = mean, inverse
    norm_swish_pad(
        wide, mean, inverse, par[G1 : G1 + 1, :], par[B1 : B1 + 1, :], pad1, slots
    )
    fill_halo(pad1, plan)
    save_pad1 = pltpu.make_async_copy(pad1, pad1_hbm, sem.at[2])
    save_pad1.start()
    load_weight.wait()

    def step(row, carry):
        total = conv_rows(pad1, weight, row, slots, NT, False) + par[C1 : C1 + 1, :]
        hidden[pl.ds(row * TILE, TILE)] = total.reshape(TILE, slots, CH)
        return carry

    lax.fori_loop(0, TILE, step, 0)
    save_hidden = pltpu.make_async_copy(hidden, hidden_hbm, sem.at[3])
    save_hidden.start()
    mean, inverse = stats_slabs(hidden, plan.same)
    stats2[0], stats2[1] = mean, inverse
    norm_swish_pad(
        hidden, mean, inverse, par[G2 : G2 + 1, :], par[B2 : B2 + 1, :], pad2, slots
    )
    fill_halo(pad2, plan)
    save_pad2 = pltpu.make_async_copy(pad2, pad2_hbm, sem.at[4])
    save_pad2.start()
    save_feats.wait()
    save_pad1.wait()
    save_hidden.wait()
    save_pad2.wait()


def first(position, tables, par_parts, parts, weight, slots):
    pixels = TILE * TILE
    rows = pixels * slots
    pad = (TILE + 2, TILE + 2, slots, CH)
    return call(
        functools.partial(first_kernel, len(parts), len(weight)),
        "sss" + "v" * len(parts) + "v" * len(parts) + "h" * len(weight),
        "vhhhhvv",
        [
            shape((16, CH), F32),
            shape((rows, CH), BF16),
            shape(pad, BF16),
            shape((pixels, slots, CH), F32),
            shape(pad, BF16),
            shape((2, slots, CH), F32),
            shape((2, slots, CH), F32),
        ],
        [
            vmem((rows, CH), BF16),
            vmem((pixels, slots, CH), F32),
            vmem((pixels, slots, CH), F32),
            vmem(pad, BF16),
            vmem(pad, BF16),
            vmem((9, CH, CH), BF16),
            weight_sems(weight),
            pltpu.SemaphoreType.DMA((5,)),
        ],
        "conv1_forward",
        2 * rows * CH * CH * 9,
        20 << 20,
    )(position, *tables[:2], *parts, *par_parts, *weight)


def second_kernel(count, position, slot_tile, slot_crop, par, feats, pad_hbm, *rest):
    pieces, rest = rest[:count], rest[count:]
    resid_hbm, normed_hbm, stats3 = rest[:3]
    resid, resid_tile, normed, pad, weight, rows_scr, weight_sem, sem = rest[3:]
    slots = pad.shape[2]
    pixels = TILE * TILE
    load_pad = pltpu.make_async_copy(pad_hbm, pad, sem.at[0])
    load_weight = WeightLoad(position, pieces, weight, weight_sem)
    load_pad.start()
    load_weight.start()
    plan = Plan(position[0], slot_tile, slot_crop, slots)
    same = plan.same
    load_pad.wait()
    load_weight.wait()
    wide = TILE * slots

    def step(row, carry):
        at = pl.ds(pl.multiple_of(row * wide, wide), wide)
        total = conv_rows(pad, weight, row, slots, NT, False) + par[C2 : C2 + 1, :]
        total = total + feats[at, :].astype(F32)
        for col in range(CH // 128):
            resid[col, at, :] = total[:, col * 128 : (col + 1) * 128]
        return carry

    lax.fori_loop(0, TILE, step, 0)

    def slab(at):
        span = pl.ds(pl.multiple_of(at * slots, slots), slots)
        return jnp.concatenate([resid[col, span, :] for col in range(CH // 128)], axis=1)

    mean = crop_mean(same, slab_sum(pixels, slots, slab))

    def square(at):
        centred = slab(at) - mean
        return centred * centred

    inverse = lax.rsqrt(crop_mean(same, slab_sum(pixels, slots, square)) + EPS)
    stats3[0], stats3[1] = mean, inverse
    rows_scr[0], rows_scr[1] = mean, inverse * par[G3 : G3 + 1, :]
    bias = par[B3 : B3 + 1, :]

    def tile_step(slot, carry):
        value = jnp.concatenate(
            [resid[col, pl.ds(slot, pixels, stride=slots), :] for col in range(CH // 128)],
            axis=1,
        )
        at = pl.ds(pl.multiple_of(slot * pixels, pixels), pixels)
        resid_tile[at, :] = value
        row = pl.ds(slot, 1)
        normed[at, :] = ((value - rows_scr[0, row]) * rows_scr[1, row] + bias).astype(BF16)
        return carry

    lax.fori_loop(0, slots, tile_step, 0)
    save_resid = pltpu.make_async_copy(resid_tile, resid_hbm, sem.at[2])
    save_normed = pltpu.make_async_copy(normed, normed_hbm, sem.at[3])
    save_resid.start()
    save_normed.start()
    save_resid.wait()
    save_normed.wait()


def second(position, tables, par, feats, pad, weight, slots):
    pixels = TILE * TILE
    rows = pixels * slots
    return call(
        functools.partial(second_kernel, len(weight)),
        "sssvvh" + "h" * len(weight),
        "hhv",
        [shape((rows, CH), F32), shape((rows, CH), BF16), shape((2, slots, CH), F32)],
        [
            vmem((CH // 128, rows, 128), F32),
            vmem((rows, CH), F32),
            vmem((rows, CH), BF16),
            vmem(pad.shape, BF16),
            vmem((9, CH, CH), BF16),
            vmem((2, slots, CH), F32),
            weight_sems(weight),
            pltpu.SemaphoreType.DMA((4,)),
        ],
        "conv2_forward",
        2 * rows * CH * CH * 9,
        16 << 20,
    )(position, *tables[:2], par, feats, pad, *weight)


def attention_kernel(parts, outs, count, position, slot_tile, slot_crop, starts, ends, *rest):
    par, normed, resid, stats3 = rest[:4]
    tangent_parts, rest = rest[4 : 4 + parts], rest[4 + parts :]
    pieces, rest = rest[:count], rest[count:]
    out_parts, rest = rest[:outs], rest[outs:]
    grad_outs, rest = rest[:outs], rest[outs:]
    vecs, resid_grad, pad = rest[:3]
    (tangent, query, key, value, mixed_grad, mixed, query_grad, key_grad, value_grad) = rest[3:12]
    normed_grad, by_tile, rows_scr, weight, key_crop, work, weight_sem = rest[12:]
    load_weight = WeightLoad(position, pieces, weight, weight_sem)
    load_weight.start()
    wq, wk, wv, wp = (weight.at[k] for k in range(4))
    rows = normed.shape[0]
    pixels = TILE * TILE
    slots = rows // pixels
    me = position[0]
    base = me * slots
    block = 256
    per_block = block // pixels
    plan = Plan(me, slot_tile, slot_crop, slots)
    lane_slot = lax.broadcasted_iota(jnp.int32, (1, rows), 1) // pixels
    crops = jnp.zeros((1, rows), jnp.int32)
    for slot in range(slots):
        crops = jnp.where(lane_slot == slot, slot_crop[base + slot], crops)
    key_crop[...] = crops

    def put(columns, part):
        tangent[:, columns] = part

    load_full(tangent_parts, me, BF16, put)
    load_weight.wait()

    def project(at, carry):
        span = pl.ds(pl.multiple_of(at * block, block), block)
        left = normed[span, :]
        total = lax.dot_general(left, wq[...], NT, preferred_element_type=F32)
        query[span, :] = (total + par[QB : QB + 1, :]).astype(BF16)
        key[span, :] = lax.dot_general(left, wk[...], NT, preferred_element_type=F32).astype(BF16)
        total = lax.dot_general(left, wv[...], NT, preferred_element_type=F32)
        value[span, :] = (total + par[VB : VB + 1, :]).astype(BF16)
        mixed_grad[span, :] = jnp.dot(
            tangent[span, :], wp[...], preferred_element_type=F32
        ).astype(BF16)
        key_grad[span, :] = jnp.zeros((block, CH), F32)
        value_grad[span, :] = jnp.zeros((block, CH), F32)
        return carry

    lax.fori_loop(0, rows // block, project, 0)

    def attend(at, begin, width):
        span = pl.ds(pl.multiple_of(at * block, block), block)
        keys = pl.ds(pl.multiple_of(begin, 128), width)
        q, g = query[span, :], mixed_grad[span, :]
        scores = lax.dot_general(q, key[keys, :], NT, preferred_element_type=F32) * SCALE
        down = lax.broadcasted_iota(jnp.int32, (block, 1), 0) // pixels
        own_crop = jnp.zeros((block, 1), jnp.int32)
        for slot in range(per_block):
            own_crop = jnp.where(down == slot, slot_crop[base + at * per_block + slot], own_crop)
        scores = jnp.where(own_crop == key_crop[:, keys], scores, -1e30)
        top = jnp.max(scores, axis=1, keepdims=True)
        exponent = jnp.exp(scores - top)
        total = jnp.sum(exponent, axis=1, keepdims=True)
        prob = exponent * (1.0 / total)
        rounded = prob.astype(BF16)
        mixed[span, :] = jnp.dot(
            rounded, value[keys, :], preferred_element_type=F32
        ).astype(BF16)
        prob_grad = lax.dot_general(g, value[keys, :], NT, preferred_element_type=F32)
        inner = jnp.sum(prob * prob_grad, axis=1, keepdims=True)
        score_grad = (prob * (prob_grad - inner)).astype(BF16)
        query_grad[span, :] = (
            jnp.dot(score_grad, key[keys, :], preferred_element_type=F32) * SCALE
        ).astype(BF16)
        key_grad[keys, :] += lax.dot_general(score_grad, q, TN, preferred_element_type=F32)
        value_grad[keys, :] += lax.dot_general(rounded, g, TN, preferred_element_type=F32)

    def attend_step(at, carry):
        low_crop = slot_crop[base + at * per_block]
        high_crop = slot_crop[base + at * per_block + per_block - 1]
        low = starts[jnp.maximum(low_crop, 0)] - base
        low = jnp.where(low_crop < 0, at * per_block, low) // 2 * 2
        high = jnp.where(high_crop < 0, slots, ends[jnp.maximum(high_crop, 0)] - base)
        kind = sum(jnp.where(high - low > width, 1, 0) for width in WINDOWS[:-1])
        span = jnp.int32(WINDOWS[0])
        for number, width in enumerate(WINDOWS):
            span = jnp.where(kind == number, width, span)
        begin = jnp.minimum(low, slots - span) * pixels
        for number, width in enumerate(WINDOWS):

            @pl.when(kind == number)
            def _():
                attend(at, begin, width * pixels)

        return carry

    lax.fori_loop(0, rows // block, attend_step, 0)

    def back(at, carry):
        query_bias, value_bias, tangent_sum = carry
        span = pl.ds(pl.multiple_of(at * block, block), block)
        dq = query_grad[span, :]
        dk = (key_grad[span, :] * SCALE).astype(BF16)
        dv = value_grad[span, :].astype(BF16)
        key[span, :] = dk
        value[span, :] = dv
        total = jnp.dot(dq, wq[...], preferred_element_type=F32)
        total += jnp.dot(dk, wk[...], preferred_element_type=F32)
        total += jnp.dot(dv, wv[...], preferred_element_type=F32)
        normed_grad[span, :] = total
        result = lax.dot_general(mixed[span, :], wp[...], NT, preferred_element_type=F32)
        result = (result + par[PB : PB + 1, :] + resid[span, :]).astype(BF16)
        if outs == 1:
            out_parts[0][span, :] = result
        else:
            mixed_scr = query
            mixed_scr[span, :] = result
        query_bias += jnp.sum(dq.astype(F32), axis=0, keepdims=True)
        value_bias += jnp.sum(dv.astype(F32), axis=0, keepdims=True)
        tangent_sum += jnp.sum(tangent[span, :].astype(F32), axis=0, keepdims=True)
        return query_bias, value_bias, tangent_sum

    zero = jnp.zeros((1, CH), F32)
    query_bias, value_bias, tangent_sum = lax.fori_loop(
        0, rows // block, back, (zero, zero, zero)
    )
    if outs == 2:
        local = out_parts[0].shape[1]
        own = pl.ds(pl.multiple_of(me * local, local), local)
        other = pl.ds(pl.multiple_of((1 - me) * local, local), local)
        out_parts[0][...] = query[:, own]
        out_parts[1][...] = query[:, other]
    left = normed[...]
    for number, grad in enumerate((query_grad, key, value)):
        total = lax.dot_general(grad[...], left, TN, preferred_element_type=F32)
        store_grad(total, grad_outs, work, position, number)
    total = lax.dot_general(tangent[...], mixed[...], TN, preferred_element_type=F32)
    store_grad(total, grad_outs, work, position, 3)

    def hat_of(slot, span):
        row = pl.ds(slot, 1)
        return (resid[span, :] - stats3[0, row]) * stats3[1, row]

    def sums(slot, carry):
        span = pl.ds(pl.multiple_of(slot * pixels, pixels), pixels)
        upstream = normed_grad[span, :]
        row = pl.ds(slot, 1)
        rows_scr[0, row] = jnp.sum(upstream, axis=0, keepdims=True)
        rows_scr[1, row] = jnp.sum(upstream * hat_of(slot, span), axis=0, keepdims=True)
        return carry

    lax.fori_loop(0, slots, sums, 0)
    same = plan.same
    gain = par[G3 : G3 + 1, :]
    plain, crossed = rows_scr[0], rows_scr[1]
    vecs[...] = jnp.zeros_like(vecs)
    vecs[G3 : G3 + 1, :] = jnp.sum(crossed, axis=0, keepdims=True)
    vecs[B3 : B3 + 1, :] = jnp.sum(plain, axis=0, keepdims=True)
    vecs[QB : QB + 1, :] = query_bias
    vecs[VB : VB + 1, :] = value_bias
    vecs[PB : PB + 1, :] = tangent_sum
    rows_scr[0] = crop_mean(same, plain * gain)
    rows_scr[1] = crop_mean(same, crossed * gain)

    def apply(slot, carry):
        span = pl.ds(pl.multiple_of(slot * pixels, pixels), pixels)
        row = pl.ds(slot, 1)
        scaled = normed_grad[span, :] * gain
        centred = scaled - rows_scr[0, row] - hat_of(slot, span) * rows_scr[1, row]
        result = tangent[span, :].astype(F32) + stats3[1, row] * centred
        for col in range(CH // 128):
            by_tile[col, span, :] = result[:, col * 128 : (col + 1) * 128]
        return carry

    lax.fori_loop(0, slots, apply, 0)

    def spread(row, carry):
        total = carry
        for col in range(TILE):
            at = row * TILE + col
            slab = jnp.concatenate(
                [
                    by_tile[c, pl.ds(at, slots, stride=pixels), :] for c in range(CH // 128)
                ],
                axis=1,
            )
            resid_grad[at] = slab
            rounded = slab.astype(BF16)
            pad[row + 1, col + 1] = rounded
            total += jnp.sum(rounded.astype(F32), axis=0, keepdims=True)
        return total

    vecs[C2 : C2 + 1, :] = lax.fori_loop(0, TILE, spread, zero)
    fill_halo(pad, plan)


def attention(position, tables, par, normed, resid, stats3, tangent_parts, weight, slots):
    pixels = TILE * TILE
    rows = pixels * slots
    parts = len(tangent_parts)
    pad = (TILE + 2, TILE + 2, slots, CH)
    if parts == 2:
        out_shapes = [shape((rows, CH // 2), BF16)] * 2
    else:
        out_shapes = [shape((rows, CH), BF16)]
    outs = len(out_shapes)
    result = call(
        functools.partial(attention_kernel, parts, outs, len(weight)),
        "sssss" + "v" * (4 + parts) + "h" * len(weight),
        "v" * (2 * outs + 3),
        out_shapes
        + grad_shapes(4, outs == 2)
        + [shape((16, CH), F32), shape((pixels, slots, CH), F32), shape(pad, BF16)],
        [vmem((rows, CH), BF16)] * 7
        + [vmem((rows, CH), F32)] * 3
        + [vmem((CH // 128, rows, 128), F32), vmem((2, slots, CH), F32)]
        + [vmem((4, CH, CH), BF16), vmem((1, rows), jnp.int32), vmem((CH, CH), F32)]
        + [weight_sems(weight)],
        "attention",
        30 << 30,
        24 << 20,
    )(
        position,
        *tables,
        par,
        normed,
        resid,
        stats3,
        *tangent_parts,
        *weight,
    )
    return result[:outs], result[outs : 2 * outs], result[2 * outs :]


def weight_grad_kernel(outs, begin, position, active, grad, *rest):
    out_parts, (flipped, work) = rest[:outs], rest[outs:]
    slots = active.shape[2]
    wide = TILE * slots
    for row in range(TILE):
        left = grad[row + 1, 1 : TILE + 1].reshape(wide, CH)
        flipped[:, row * wide : (row + 1) * wide] = left.T

    def step(number, carry):
        tap = begin + number
        right = active[pl.ds(tap // 3, TILE), pl.ds(tap % 3, TILE)].reshape(TILE * wide, CH)
        total = jnp.dot(flipped[...], right, preferred_element_type=F32)
        store_grad(total, out_parts, work, position, number)
        return carry

    lax.fori_loop(0, out_parts[0].shape[0], step, 0)


def weight_grad(position, active, grad, paired, slots, name, begin=0, count=9):
    rows = TILE * TILE * slots
    shapes = grad_shapes(count, paired)
    return call(
        functools.partial(weight_grad_kernel, len(shapes), begin),
        "svv",
        "v" * len(shapes),
        shapes,
        [vmem((CH, rows), BF16), vmem((CH, CH), F32)],
        name,
        2 * rows * CH * CH * count,
        12 << 20,
    )(position, active, grad)


def swish_back(upstream, before):
    gate = jax.nn.sigmoid(before)
    return upstream * (gate + before * gate * (1.0 - gate))


def norm_back_sums(source, upstream, mean, inverse, gain, bias, slots):
    def step(at, carry):
        plain, crossed = carry
        hat = (source(at) - mean) * inverse
        grad = swish_back(upstream[at], hat * gain + bias)
        upstream[at] = grad
        return plain + grad, crossed + grad * hat

    zero = jnp.zeros((slots, CH), F32)
    return lax.fori_loop(0, TILE * TILE, step, (zero, zero), unroll=2)


def middle_kernel(count, position, slot_tile, slot_crop, par, stats2, pad_hbm, hidden_hbm, *rest):
    pieces, rest = rest[:count], rest[count:]
    pad_out_hbm, vecs = rest[:2]
    pad, weight, hidden, upstream, pad_out, weight_sem, sem = rest[2:]
    slots = pad.shape[2]
    load_pad = pltpu.make_async_copy(pad_hbm, pad, sem.at[0])
    load_weight = WeightLoad(position, pieces, weight, weight_sem)
    load_hidden = pltpu.make_async_copy(hidden_hbm, hidden, sem.at[2])
    load_pad.start()
    load_weight.start()
    load_hidden.start()
    plan = Plan(position[0], slot_tile, slot_crop, slots)
    same = plan.same
    load_pad.wait()
    load_weight.wait()

    def step(row, carry):
        total = conv_rows(pad, weight, row, slots, NN, True)
        upstream[pl.ds(row * TILE, TILE)] = total.reshape(TILE, slots, CH)
        return carry

    lax.fori_loop(0, TILE, step, 0)
    load_hidden.wait()
    mean, inverse = stats2[0], stats2[1]
    gain, bias = par[G2 : G2 + 1, :], par[B2 : B2 + 1, :]
    plain, crossed = norm_back_sums(
        lambda at: hidden[at], upstream, mean, inverse, gain, bias, slots
    )
    vecs[...] = jnp.zeros_like(vecs)
    vecs[G2 : G2 + 1, :] = jnp.sum(crossed, axis=0, keepdims=True)
    vecs[B2 : B2 + 1, :] = jnp.sum(plain, axis=0, keepdims=True)
    plain = crop_mean(same, plain * gain)
    crossed = crop_mean(same, crossed * gain)

    def apply(row, carry):
        total = carry
        for col in range(TILE):
            at = row * TILE + col
            hat = (hidden[at] - mean) * inverse
            grad = inverse * (upstream[at] * gain - plain - hat * crossed)
            rounded = grad.astype(BF16)
            pad_out[row + 1, col + 1] = rounded
            total += rounded.astype(F32)
        return total

    total = lax.fori_loop(0, TILE, apply, jnp.zeros((slots, CH), F32))
    vecs[C1 : C1 + 1, :] = jnp.sum(total, axis=0, keepdims=True)
    fill_halo(pad_out, plan)
    save = pltpu.make_async_copy(pad_out, pad_out_hbm, sem.at[3])
    save.start()
    save.wait()


def middle(position, tables, par, stats2, pad, weight, hidden, slots):
    pixels = TILE * TILE
    rows = pixels * slots
    return call(
        functools.partial(middle_kernel, len(weight)),
        "sssvvhh" + "h" * len(weight),
        "hv",
        [shape(pad.shape, BF16), shape((16, CH), F32)],
        [
            vmem(pad.shape, BF16),
            vmem((9, CH, CH), BF16),
            vmem((pixels, slots, CH), F32),
            vmem((pixels, slots, CH), F32),
            vmem(pad.shape, BF16),
            weight_sems(weight),
            pltpu.SemaphoreType.DMA((4,)),
        ],
        "conv2_input_grad",
        2 * rows * CH * CH * 9,
        16 << 20,
    )(position, *tables[:2], par, stats2, pad, hidden, *weight)


def last_kernel(
    outs, count, position, slot_tile, slot_crop, par, stats1, feats, pad_hbm, resid_hbm, *rest
):
    pieces, rest = rest[:count], rest[count:]
    out_parts, (vecs, pad, weight, resid, upstream, weight_sem, sem) = rest[:outs], rest[outs:]
    slots = pad.shape[2]
    pixels = TILE * TILE
    me = position[0]
    load_pad = pltpu.make_async_copy(pad_hbm, pad, sem.at[0])
    load_weight = WeightLoad(position, pieces, weight, weight_sem)
    load_resid = pltpu.make_async_copy(resid_hbm, resid, sem.at[2])
    load_pad.start()
    load_weight.start()
    load_resid.start()
    plan = Plan(me, slot_tile, slot_crop, slots)
    same = plan.same
    load_pad.wait()
    load_weight.wait()

    def step(row, carry):
        total = conv_rows(pad, weight, row, slots, NN, True)
        upstream[pl.ds(row * TILE, TILE)] = total.reshape(TILE, slots, CH)
        return carry

    lax.fori_loop(0, TILE, step, 0)
    load_resid.wait()
    mean, inverse = stats1[0], stats1[1]
    gain, bias = par[G1 : G1 + 1, :], par[B1 : B1 + 1, :]

    def source(at):
        return feats[pl.ds(pl.multiple_of(at * slots, slots), slots), :].astype(F32)

    plain, crossed = norm_back_sums(source, upstream, mean, inverse, gain, bias, slots)
    vecs[...] = jnp.zeros_like(vecs)
    vecs[G1 : G1 + 1, :] = jnp.sum(crossed, axis=0, keepdims=True)
    vecs[B1 : B1 + 1, :] = jnp.sum(plain, axis=0, keepdims=True)
    plain = crop_mean(same, plain * gain)
    crossed = crop_mean(same, crossed * gain)

    def apply(at, carry):
        hat = (source(at) - mean) * inverse
        grad = resid[at] + inverse * (upstream[at] * gain - plain - hat * crossed)
        if outs == 1:
            span = pl.ds(pl.multiple_of(at * slots, slots), slots)
            out_parts[0][span, :] = grad.astype(BF16)
        else:
            upstream[at] = grad
        return carry

    lax.fori_loop(0, pixels, apply, 0, unroll=2)
    if outs == 2:
        local = out_parts[0].shape[1]
        own = pl.ds(pl.multiple_of(me * local, local), local)
        other = pl.ds(pl.multiple_of((1 - me) * local, local), local)
        out_parts[0][...] = upstream[:, :, own].reshape(pixels * slots, local)
        out_parts[1][...] = upstream[:, :, other].reshape(pixels * slots, local).astype(BF16)


def last(position, tables, par, stats1, feats, pad, weight, resid_grad, parts, slots):
    pixels = TILE * TILE
    rows = pixels * slots
    if parts == 2:
        out_shapes = [shape((rows, CH // 2), F32), shape((rows, CH // 2), BF16)]
    else:
        out_shapes = [shape((rows, CH), BF16)]
    outs = len(out_shapes)
    result = call(
        functools.partial(last_kernel, outs, len(weight)),
        "sssvvvhh" + "h" * len(weight),
        "v" * (outs + 1),
        out_shapes + [shape((16, CH), F32)],
        [
            vmem(pad.shape, BF16),
            vmem((9, CH, CH), BF16),
            vmem((pixels, slots, CH), F32),
            vmem((pixels, slots, CH), F32),
            weight_sems(weight),
            pltpu.SemaphoreType.DMA((3,)),
        ],
        "conv1_input_grad",
        2 * rows * CH * CH * 9,
        16 << 20,
    )(position, *tables[:2], par, stats1, feats, pad, resid_grad, *weight)
    return result[:outs], result[outs]


class Links:
    def flip(self, value, bit):
        return lax.ppermute(value, "dp", [(at, at ^ bit) for at in range(16)])

    def chan(self, value):
        return lax.ppermute(value, "chan", [(0, 1), (1, 0)])

    def core(self, value):
        return self.flip(value, 1)

    def down(self, value):
        return self.flip(value, 2)

    def near(self, value):
        return self.flip(value, 4)

    def far(self, value):
        return self.flip(value, 8)

    def spread(self, value):
        parts = [value, self.near(value), self.down(value)]
        parts.append(self.down(parts[1]))
        return parts + [self.core(part) for part in parts]

    def gather_eighths(self, weight, piece):
        width = weight.shape[1] // 8
        own = lax.dynamic_slice_in_dim(weight, piece * width, width, 1)
        return [weight] + self.spread(self.chan(own))

    def gather_halves(self, weight, core):
        width = weight.shape[1] // 2
        own = self.chan(lax.dynamic_slice_in_dim(weight, core * width, width, 1))
        return [weight, own, self.core(own)]

    def add(self, left, right):
        return (left.astype(F32) + right.astype(F32)).astype(BF16)

    def reduce(self, halves):
        count = halves[0].shape[0]
        value = self.add(halves[0], self.core(halves[1]))
        value = value.reshape(count, 2, 2, 2, CH // 16, CH)
        third = -(-count // 3)
        orders = (("chan", "down", "near"), ("down", "near", "chan"), ("near", "chan", "down"))
        done = []
        for number, order in enumerate(orders):
            part = value[number * third : (number + 1) * third]
            if part.shape[0] == 0:
                continue
            names = ["chan", "down", "near"]
            for name in order:
                at = 1 + names.index(name)
                names.remove(name)
                keep = lax.index_in_dim(part, 0, at, keepdims=False)
                send = lax.index_in_dim(part, 1, at, keepdims=False)
                part = self.add(keep, getattr(self, name)(send))
            done.append(part)
        value = jnp.concatenate(done, axis=0)
        return self.spread(self.add(value, self.far(value)))

    def total(self, value):
        for step in (self.core, self.chan, self.down, self.near, self.far):
            value = value + step(value)
        return value


def assemble_kernel(position, *rest):
    parts, out = rest[:-1], rest[-1]
    width = parts[0].shape[1]
    for at, part in enumerate(parts):
        rows = pl.ds(pl.multiple_of((position[1] ^ at) * width, width), width)
        out[:, rows, :] = part[...].astype(F32)


def assemble(position, parts, name):
    count, width, _ = parts[0].shape
    return call(
        assemble_kernel,
        "s" + "v" * len(parts),
        "v",
        [shape((count, width * len(parts), CH), F32)],
        [],
        name,
        1 << 20,
        6 << 20,
    )(position, *parts)[0]


def body(
    features,
    crop_ids,
    cotangent,
    norm1_gain,
    norm1_bias,
    conv1_weight,
    conv1_bias,
    norm2_gain,
    norm2_bias,
    conv2_weight,
    conv2_bias,
    norm3_gain,
    norm3_bias,
    query_weight,
    query_bias,
    key_weight,
    value_weight,
    value_bias,
    proj_weight,
    proj_bias,
):
    _, local, pixels = features.shape
    devices = lax.axis_size("chan")
    copies = lax.axis_size("dp")
    index = lax.axis_index("chan").astype(jnp.int32)
    tiles = pixels // (TILE * TILE)
    slots = tiles if devices == 1 else tiles // 2
    paired = devices == 2 and copies == 16
    links = Links()
    turn = lax.axis_index("dp").astype(jnp.int32)
    core, down, near = turn & 1, (turn >> 1) & 1, (turn >> 2) & 1
    piece = core * 4 + down * 2 + near
    position = jnp.stack([index, piece, core, index * 8 + piece])

    def exchange(parts):
        if paired:
            return [parts[0], links.chan(parts[1])]
        if devices == 2:
            parts = [jnp.where(index == 0, parts[k], parts[1 - k]) for k in range(2)]
        moved = lax.all_to_all(jnp.stack(parts), "chan", 0, 0)
        return [jnp.transpose(moved, (1, 0, 2)).reshape(moved.shape[1], CH)]

    def give_back(parts):
        if paired:
            return [parts[0], links.chan(parts[1])]
        whole = parts[0].reshape(parts[0].shape[0], devices, local)
        moved = lax.all_to_all(jnp.transpose(whole, (1, 0, 2)), "chan", 0, 0)
        parts = [moved[at] for at in range(devices)]
        if devices == 2:
            parts = [jnp.where(index == 0, parts[k], parts[1 - k]) for k in range(2)]
        return parts

    lanes = -(-local // 128) * 128

    def widened(signal):
        return jnp.pad(signal, ((0, lanes - local), (0, 0))) if lanes > local else signal

    def narrowed(parts):
        return [part[:, :local] for part in parts] if lanes > local else parts

    def unpack_lanes(parts, by_pixel, dtype, name):
        if lanes > local:
            parts = [jnp.pad(part, ((0, 0), (0, lanes - local))) for part in parts]
        whole = unpack(position, tables[0], parts, pixels, by_pixel, dtype, slots, name)
        return whole[:local]

    vectors = jnp.stack(
        [
            norm1_gain,
            norm1_bias,
            conv1_bias,
            norm2_gain,
            norm2_bias,
            conv2_bias,
            norm3_gain,
            norm3_bias,
            query_bias,
            value_bias,
            proj_bias,
        ]
        + [jnp.zeros_like(proj_bias)] * 5
    )
    small = jnp.stack([query_weight, key_weight, value_weight, proj_weight])
    if paired:
        weight1 = links.gather_eighths(conv1_weight, piece)
        weight2 = links.gather_eighths(conv2_weight, piece)
        par_parts = [vectors, links.chan(vectors)]
    else:
        par_parts = [lax.all_gather(vectors, "chan", axis=1, tiled=True)]
        weight1 = [lax.all_gather(conv1_weight, "chan", axis=1, tiled=True)]
        weight2 = [lax.all_gather(conv2_weight, "chan", axis=1, tiled=True)]
    tables, packed = pack_first(
        position, crop_ids[0], widened(features[0]), devices, slots, "pack_features"
    )
    feature_parts = exchange(narrowed(packed))
    packed = pack(
        position, tables[0], widened(cotangent[0]), False, devices, slots, "pack_cotangent"
    )
    packed = list(packed)
    if paired:
        small, packed[1], _ = lax.optimization_barrier((small, packed[1], feature_parts[1]))
        weight3 = links.gather_halves(small, core)
    else:
        weight3 = [lax.all_gather(small, "chan", axis=1, tiled=True)]
    tangent_parts = exchange(narrowed(packed))
    par, feats, pad1, hidden, pad2, stats1, stats2 = first(
        position, tables, par_parts, feature_parts, weight1, slots
    )
    resid, normed, stats3 = second(position, tables, par, feats, pad2, weight2, slots)
    out_parts, small_grads, (vecs3, resid_grad, grad2) = attention(
        position, tables, par, normed, resid, stats3, tangent_parts, weight3, slots
    )
    out_parts = give_back(out_parts)
    output = unpack_lanes(out_parts, False, BF16, "unpack_output")
    grads2 = weight_grad(position, pad2, grad2, paired, slots, "conv2_weight_grad")
    grad1, vecs2 = middle(position, tables, par, stats2, grad2, weight2, hidden, slots)
    grads1 = weight_grad(position, pad1, grad1, paired, slots, "conv1_weight_grad")
    in_parts, vecs1 = last(
        position, tables, par, stats1, feats, grad1, weight1, resid_grad, len(feature_parts), slots
    )
    in_parts = give_back(in_parts)
    input_grad = unpack_lanes(in_parts, True, F32, "unpack_input_grad")

    vecs = vecs1 + vecs2 + vecs3
    if paired:
        small_grads = assemble(position, links.reduce(small_grads), "small_grads")
        weight2_grad = assemble(position, links.reduce(grads2), "conv2_grads")
        weight1_grad = assemble(position, links.reduce(grads1), "conv1_grads")
        vecs = links.total(vecs)
        vecs = lax.dynamic_slice_in_dim(vecs, index * local, local, 1)
    else:

        def total(grad, axis):
            part = lax.psum_scatter(grad, "chan", scatter_dimension=axis, tiled=True)
            return lax.psum(part, "dp").astype(F32)

        small_grads, weight2_grad, weight1_grad = [
            total(g[0], 1) for g in (small_grads, grads2, grads1)
        ]
        vecs = total(vecs, 1)
    gq, gk, gv, gp = [small_grads[k] for k in range(4)]
    return (
        output[None],
        input_grad[None],
        vecs[G1],
        vecs[B1],
        weight1_grad,
        vecs[C1],
        vecs[G2],
        vecs[B2],
        weight2_grad,
        vecs[C2],
        vecs[G3],
        vecs[B3],
        gq,
        vecs[QB],
        gk,
        gv,
        vecs[VB],
        gp,
        vecs[PB],
    )


def solution(mesh):
    canvas = P("dp", "chan", None)
    vector = P("chan")
    conv = P(None, "chan", None)
    matrix = P("chan", None)
    placed = (
        (canvas, P("dp", None, None), canvas)
        + (vector, vector, conv, vector, vector, vector, conv, vector, vector, vector)
        + (matrix, vector, matrix, matrix, vector, matrix, vector)
    )
    results = (
        (canvas, canvas, vector, vector, conv, vector, vector, vector, conv, vector)
        + (vector, vector, matrix, vector, matrix, matrix, vector, matrix, vector)
    )
    return jax.shard_map(body, mesh=mesh, in_specs=placed, out_specs=results, check_vma=False)
```

```python
import functools
import itertools

import jax
import jax.numpy as jnp
import numpy as np
from jax import lax
from jax.experimental import pallas as pl
from jax.experimental.pallas import tpu as pltpu
from jax.sharding import PartitionSpec as P

CH = 512
GROUPS = 32
CROPS = 16
TILE = 8
BANDS = 4
EPS = 1e-06
F32 = jnp.float32
BF16 = jnp.bfloat16
HIGH = lax.Precision.HIGHEST
NN = (((1,), (0,)), ((), ()))
NT = (((1,), (1,)), ((), ()))
TN = (((0,), (0,)), ((), ()))
VMEM = pltpu.VMEM
ANY = pl.ANY
SCALE = CH ** (-0.5)


def band_layouts(units):
    return [
        tuple(np.diff((0,) + cuts + (units,)))
        for cuts in itertools.combinations(range(1, units), BANDS - 1)
    ]


@functools.lru_cache(maxsize=None)
def owner_tables(devices, units, slots):
    layouts = band_layouts(units)
    rank = np.zeros(1 << (units - 1), np.int32)
    for number, sizes in enumerate(layouts):
        cuts = np.cumsum(sizes)[:-1]
        rank[sum(1 << (int(c) - 1) for c in cuts)] = number
    sizes = np.array(
        [[r * c for r in rows for c in cols] for rows in layouts for cols in layouts], np.int32
    )
    owners = np.zeros(sizes.shape, np.int32)
    if devices == 2:
        masks = np.arange(1 << (CROPS - 1), dtype=np.int32)
        bits = ((masks[None, :] >> np.arange(CROPS)[:, None]) & 1).astype(np.float32)
        for at, row in enumerate(sizes.astype(np.float32)):
            filled = row @ bits
            squares = (row * row) @ bits
            cost = np.abs(squares - (row * row).sum() / 2) + 1e6 * np.abs(filled - slots)
            owners[at] = bits[:, int(np.argmin(cost))].astype(np.int32)
    else:
        for at, row in enumerate(sizes):
            loads = [0] * devices
            for crop in sorted(range(CROPS), key=lambda c: -row[c]):
                device = loads.index(min(loads))
                owners[at, crop] = device
                loads[device] += int(row[crop])
    for device in range(devices):
        assert (np.where(owners == device, sizes, 0).sum(axis=1) <= slots).all()
    return rank, owners


def packed_tables(devices, units, slots):
    rank, owners = owner_tables(devices, units, slots)
    shifts = np.arange(0, 32, 4, dtype=np.int64)
    words = (owners.reshape(-1, 2, 8).astype(np.int64) << shifts).sum(axis=2)
    words = np.where(words >= 1 << 31, words - (1 << 32), words)
    return np.concatenate([rank, words.reshape(-1).astype(np.int32)])


WINDOWS = (8, 16, 24, 32)


def write_plan(devices, slots, ids, table, slot_tile, slot_crop, starts, ends):
    units = ids.shape[0] // TILE
    count = units * units
    layouts = len(band_layouts(units))

    def code(at):
        bits = 0
        for step in range(units - 1):
            bits = bits + jnp.where(at(step) != at(step + 1), 1 << step, 0)
        return table[bits]

    def row_id(step):
        return ids[TILE * step, 0]

    def col_id(step):
        return ids[0, TILE * step]

    layout = code(row_id) * layouts + code(col_id)
    words = [table[(1 << (units - 1)) + 2 * layout + half] for half in range(2)]
    heights, widths = [], []
    for band in range(BANDS):
        heights.append(sum(jnp.where(row_id(k) // BANDS == band, 1, 0) for k in range(units)))
        widths.append(sum(jnp.where(col_id(k) % BANDS == band, 1, 0) for k in range(units)))
    if devices * slots > count:

        def clear(at, carry):
            slot_tile[at] = -1
            slot_crop[at] = -1
            return carry

        lax.fori_loop(0, devices * slots, clear, 0)
    filled = [jnp.int32(device * slots) for device in range(devices)]
    for crop in range(CROPS):
        owner = lax.shift_right_logical(words[crop // 8], jnp.int32(4 * (crop % 8))) & 15
        size = heights[crop // BANDS] * widths[crop % BANDS]
        start = filled[0]
        for device in range(1, devices):
            start = jnp.where(owner == device, filled[device], start)
        starts[crop] = start
        ends[crop] = start
        for device in range(devices):
            filled[device] = filled[device] + jnp.where(owner == device, size, 0)

    def place(row, carry):
        for col in range(units):
            crop = ids[row * TILE, col * TILE]
            at = ends[crop]
            slot_tile[at] = row * units + col
            slot_crop[at] = crop
            ends[crop] = at + 1
        return carry

    lax.fori_loop(0, units, place, 0)


class Plan:
    def __init__(self, me, slot_tile, slot_crop, slots):
        self.slots = slots
        base = me * slots
        lane = lax.broadcasted_iota(jnp.int32, (1, 128), 1) % slots
        down = lax.broadcasted_iota(jnp.int32, (slots, 1), 0)
        self.tile_row, self.crop_row = jnp.zeros_like(lane), jnp.zeros_like(lane)
        self.tile_col, self.crop_col = jnp.zeros_like(down), jnp.zeros_like(down)
        for slot in range(slots):
            tile, crop = slot_tile[base + slot], slot_crop[base + slot]
            self.tile_row = jnp.where(lane == slot, tile, self.tile_row)
            self.crop_row = jnp.where(lane == slot, crop, self.crop_row)
            self.tile_col = jnp.where(down == slot, tile, self.tile_col)
            self.crop_col = jnp.where(down == slot, crop, self.crop_col)
        self.same = (self.crop_col == self.crop_row[:, 0:slots]).astype(F32)


def group_total(value):
    width = CH // GROUPS
    lane = lax.broadcasted_iota(jnp.int32, (value.shape[0], 128), 1)
    parts = []
    for at in range(0, value.shape[1], 128):
        part = value[:, at : at + 128]
        step = 1
        while step < width:
            up = pltpu.roll(part, 128 - step, 1)
            down = pltpu.roll(part, step, 1)
            part = part + jnp.where((lane & step) == 0, up, down)
            step *= 2
        parts.append(part)
    return jnp.concatenate(parts, axis=1)


def crop_mean(same, value):
    count = jnp.sum(same, axis=1, keepdims=True) * float(TILE * TILE * (CH // GROUPS))
    total = lax.dot_general(same, group_total(value), NN, precision=HIGH, preferred_element_type=F32)
    return total / count


def lanes_of(width):
    return [slice(at, at + 128) for at in range(0, width, 128)]


def slab_sum(pixels, slots, width, term):
    parts = []
    for lanes in lanes_of(width):

        def step(at, total):
            return total + term(at, lanes)

        parts.append(lax.fori_loop(0, pixels, step, jnp.zeros((slots, 128), F32), unroll=8))
    return jnp.concatenate(parts, axis=1)


def slab_stats(pixels, slots, slab, same):
    mean = crop_mean(same, slab_sum(pixels, slots, CH, slab))

    def square(at, lanes):
        centred = slab(at, lanes) - mean[:, lanes]
        return centred * centred

    return mean, lax.rsqrt(crop_mean(same, slab_sum(pixels, slots, CH, square)) + EPS)


def sigmoid(value):
    return 0.5 * jnp.tanh(0.5 * value) + 0.5


def fill_halo(pad, plan):
    slots = plan.slots
    wide = TILE * slots
    tile_c = jnp.concatenate([plan.tile_col] * TILE, axis=0)
    crop_c = jnp.concatenate([plan.crop_col] * TILE, axis=0)
    tile_r = jnp.concatenate([plan.tile_row] * (wide // 128), axis=1)
    crop_r = jnp.concatenate([plan.crop_row] * (wide // 128), axis=1)
    block_c = lax.broadcasted_iota(jnp.int32, (wide, wide), 0) // slots
    block_r = lax.broadcasted_iota(jnp.int32, (wide, wide), 1) // slots
    linked = (crop_c == crop_r) & (tile_c >= 0)

    def near(row_step, col_step):
        return linked & (tile_r == tile_c + (TILE * row_step + col_step))

    def edge(row_step, col_step, source):
        pick = (near(row_step, col_step) & (block_c == block_r)).astype(F32).astype(BF16)
        moved = jnp.dot(pick, source.reshape(wide, CH), preferred_element_type=F32).astype(BF16)
        return moved.reshape(TILE, slots, CH)

    def corner(row_step, col_step, source):
        pick = near(row_step, col_step)[0:slots, 0:slots].astype(F32).astype(BF16)
        return jnp.dot(pick, source, preferred_element_type=F32).astype(BF16)

    low, high, end = 1, TILE, TILE + 1
    pad[0, low:end] = edge(-1, 0, pad[high, low:end])
    pad[end, low:end] = edge(1, 0, pad[low, low:end])
    pad[low:end, 0] = edge(0, -1, pad[low:end, high])
    pad[low:end, end] = edge(0, 1, pad[low:end, low])
    pad[0, 0] = corner(-1, -1, pad[high, high])
    pad[0, end] = corner(-1, 1, pad[high, low])
    pad[end, 0] = corner(1, -1, pad[low, high])
    pad[end, end] = corner(1, 1, pad[low, low])


class WeightLoad:
    def __init__(self, position, pieces, target, sem, columns=None):
        self.copies = []
        views = [(pieces[0], None)]
        if len(pieces) > 1:
            me, core = position[0], position[1]
            half = pieces[0].shape[1]
            views = [(pieces[0], me * half)]
            part = half // (len(pieces) - 1)
            for number, piece in enumerate(pieces[1:]):
                spot = (1 - me) * half
                if len(pieces) == 3:
                    spot = spot + (core ^ number) * part
                if len(piece.shape) == 3:
                    views.append((piece, spot))
                    continue
                for at in range(piece.shape[0]):
                    views.append((piece.at[at], spot + at * piece.shape[2]))
        for at, (piece, spot) in enumerate(views):
            width = piece.shape[1]
            rows = slice(None)
            if spot is not None:
                rows = pl.ds(pl.multiple_of(spot, 32), width)
            if columns is not None:
                piece = piece.at[:, :, columns]
            self.copies.append(pltpu.make_async_copy(piece, target.at[:, rows, :], sem.at[at]))

    def start(self):
        for copy in self.copies:
            copy.start()

    def wait(self):
        for copy in self.copies:
            copy.wait()


def weight_sems(pieces):
    return pltpu.SemaphoreType.DMA((9,))


BLOCK = CH // 16


def store_grad(grad, outs, work, position, unit, first, count, front=True):
    if len(outs) == 1:
        outs[0][unit] = grad.astype(BF16)
        return
    work[...] = grad
    me, core, quad = position[0], position[1], position[2]
    for half, out in enumerate(outs):
        for c in range(2):
            for q in range(4):
                row = (me ^ c) * (CH // 2) + (core ^ half) * (CH // 4) + (quad ^ q) * BLOCK
                part = work[pl.ds(pl.multiple_of(row, BLOCK), BLOCK), :]
                if front:
                    to = ((c * 4 + q) * first + unit) * BLOCK
                else:
                    to = (8 * first + (q * 2 + c) * (count - first) + unit - first) * BLOCK
                out[pl.ds(pl.multiple_of(to, BLOCK), BLOCK), :] = part.astype(BF16)


def store_vectors(vecs, out, me):
    if len(out.shape) == 2:
        out[...] = vecs[...]
    else:
        half = out.shape[2]
        out[0] = vecs[:, pl.ds(pl.multiple_of(me * half, half), half)]
        out[1] = vecs[:, pl.ds(pl.multiple_of((1 - me) * half, half), half)]


def vector_shape(paired):
    return shape((2, 16, CH // 2) if paired else (16, CH), F32)


def grad_shapes(count, paired):
    if paired:
        return [shape((8 * count * BLOCK, CH), BF16)] * 2
    return [shape((count, CH, CH), BF16)]


def conv_rows(pad, weight, row, slots, dims, flipped, count=1):
    total = None
    for tap in range(9):
        down, right = tap // 3, tap % 3
        if flipped:
            down, right = 2 - down, 2 - right
        left = pad[pl.ds(row + down, count), right : right + TILE].reshape(count * TILE * slots, CH)
        part = lax.dot_general(left, weight[tap], dims, preferred_element_type=F32)
        total = part if total is None else total + part
    return total


def load_full(parts, me, dtype, store):
    if len(parts) == 1:
        store(slice(None), parts[0][...].astype(dtype))
    else:
        local = parts[0].shape[-1]
        own = pl.ds(pl.multiple_of(me * local, local), local)
        other = pl.ds(pl.multiple_of((1 - me) * local, local), local)
        store(own, parts[0][...].astype(dtype))
        store(other, parts[1][...].astype(dtype))


def vmem(shape, dtype):
    return pltpu.VMEM(shape, dtype)


def specs(kinds):
    table = {
        "v": pl.BlockSpec(memory_space=pltpu.VMEM),
        "s": pl.BlockSpec(memory_space=pltpu.SMEM),
        "h": pl.BlockSpec(memory_space=pl.ANY),
    }
    return [table[k] for k in kinds]


ROOM = {
    "unpack_output": 18,
    "unpack_input_grad": 18,
    "conv2_weight_grad": 24,
    "conv1_weight_grad": 22,
    "conv2_input_grad": 24,
    "conv1_input_grad": 20,
    "conv2_grads": 16,
    "conv1_grads": 14,
}


def call(body, ins, outs, shapes, scratch, name, flops, moved):
    return pl.pallas_call(
        body,
        in_specs=specs(ins),
        out_specs=tuple(specs(outs)),
        out_shape=tuple(shapes),
        scratch_shapes=list(scratch),
        compiler_params=pltpu.CompilerParams(vmem_limit_bytes=ROOM.get(name, 60) << 20),
        cost_estimate=pl.CostEstimate(
            flops=int(flops), bytes_accessed=int(moved), transcendentals=0
        ),
        name=name,
    )


def shape(dims, dtype):
    return jax.ShapeDtypeStruct(dims, dtype)


def pack_first_kernel(devices, slots, position, ids, table, signal, *rest):
    plan, rest = rest[:4], rest[4:]
    write_plan(devices, slots, ids, table, *plan)
    pack_kernel(True, slots, position, plan[0], signal, *rest)


def pack_kernel(by_pixel, slots, position, slot_tile, signal, *rest):
    outs, (raster, stage) = rest[:-2], rest[-2:]
    local, pixels = signal.shape
    side = int(pixels**0.5)
    chunk = 512
    cols = local // 128
    for at in range(0, pixels, chunk):
        flipped = signal[:, at : at + chunk].astype(F32).T
        for col in range(cols):
            raster[col, at : at + chunk, :] = flipped[:, col * 128 : (col + 1) * 128]
    for number, out in enumerate(outs):

        def step(slot, carry):
            tile = slot_tile[pack_base(position, number, len(outs), slots) + slot]
            keep = tile >= 0
            tile = jnp.maximum(tile, 0)
            start = (tile // TILE) * (TILE * side) + (tile % TILE) * TILE
            for row in range(TILE):
                for col in range(cols):
                    value = raster[col, pl.ds(pl.multiple_of(start + row * side, TILE), TILE), :]
                    value = jnp.where(keep, value, 0.0)
                    if by_pixel:
                        stage[col, pl.ds(row * TILE * slots + slot, TILE, stride=slots), :] = value
                    else:
                        at = pl.multiple_of(slot * (TILE * TILE) + row * TILE, TILE)
                        stage[col, pl.ds(at, TILE), :] = value
            return carry

        lax.fori_loop(0, slots, step, 0)
        for at in range(0, stage.shape[1], chunk):
            for col in range(cols):
                span = slice(col * 128, (col + 1) * 128)
                out[at : at + chunk, span] = stage[col, at : at + chunk, :].astype(BF16)


def pack_base(position, number, devices, slots):
    return (position[0] ^ number if devices == 2 else number) * slots


def pack_first(position, ids, signal, devices, slots, name):
    local, pixels = signal.shape
    rows = slots * TILE * TILE
    table = jnp.asarray(packed_tables(devices, ids.shape[0] // TILE, slots))
    result = call(
        functools.partial(pack_first_kernel, devices, slots),
        "sssv",
        "ssss" + "v" * devices,
        [shape((devices * slots,), jnp.int32)] * 2
        + [shape((CROPS,), jnp.int32)] * 2
        + [shape((rows, local), BF16)] * devices,
        [vmem((local // 128, pixels, 128), F32), vmem((local // 128, rows, 128), F32)],
        name,
        4 << 30,
        6 << 20,
    )(position, ids, table, signal)
    return result[:4], result[4:]


def pack(position, slot_tile, signal, by_pixel, devices, slots, name):
    local, pixels = signal.shape
    rows = slots * TILE * TILE
    return call(
        functools.partial(pack_kernel, by_pixel, slots),
        "ssv",
        "v" * devices,
        [shape((rows, local), BF16)] * devices,
        [vmem((local // 128, pixels, 128), F32), vmem((local // 128, rows, 128), F32)],
        name,
        40 << 30,
        6 << 20,
    )(position, slot_tile, signal)


def unpack_kernel(by_pixel, slots, position, slot_tile, *rest):
    ins, out, (raster, stage) = rest[:-3], rest[-3], rest[-2:]
    local, pixels = out.shape
    side = int(pixels**0.5)
    chunk = 512
    cols = local // 128
    for number, part in enumerate(ins):
        for at in range(0, stage.shape[1], chunk):
            for col in range(cols):
                span = slice(col * 128, (col + 1) * 128)
                stage[col, at : at + chunk, :] = part[at : at + chunk, span].astype(F32)

        def step(slot, carry):
            tile = slot_tile[pack_base(position, number, len(ins), slots) + slot]

            @pl.when(tile >= 0)
            def _():
                start = (tile // TILE) * (TILE * side) + (tile % TILE) * TILE
                for row in range(TILE):
                    to = pl.ds(pl.multiple_of(start + row * side, TILE), TILE)
                    for col in range(cols):
                        if by_pixel:
                            at = pl.ds(row * TILE * slots + slot, TILE, stride=slots)
                        else:
                            first = pl.multiple_of(slot * (TILE * TILE) + row * TILE, TILE)
                            at = pl.ds(first, TILE)
                        raster[col, to, :] = stage[col, at, :]

            return carry

        lax.fori_loop(0, slots, step, 0)
    for at in range(0, pixels, chunk):
        for col in range(cols):
            span = slice(col * 128, (col + 1) * 128)
            out[span, at : at + chunk] = raster[col, at : at + chunk, :].T.astype(out.dtype)


def unpack(position, slot_tile, parts, pixels, by_pixel, dtype, slots, name):
    rows, local = parts[0].shape
    return call(
        functools.partial(unpack_kernel, by_pixel, slots),
        "ss" + "v" * len(parts),
        "v",
        [shape((local, pixels), dtype)],
        [vmem((local // 128, pixels, 128), F32), vmem((local // 128, rows, 128), F32)],
        name,
        4 << 30,
        8 << 20,
    )(position, slot_tile, *parts)[0]


(G1, B1, C1, G2, B2, C2, G3, B3, QB, VB, PB) = range(11)


def norm_swish_pad(slab, mean, inverse, gain, bias, pad, copy=None):
    scaled = inverse * gain
    for lanes in lanes_of(CH):
        centre, factor, offset = mean[:, lanes], scaled[:, lanes], bias[:, lanes]

        def step(row, carry):
            for col in range(TILE):
                value = slab(row * TILE + col, lanes)
                before = (value - centre) * factor + offset
                pad[row + 1, col + 1, :, lanes] = (before * sigmoid(before)).astype(BF16)
                if copy is not None:
                    copy[row * TILE + col, :, lanes] = value.astype(BF16)
            return carry

        lax.fori_loop(0, TILE, step, 0)


def first_kernel(parts, count, position, slot_tile, slot_crop, *rest):
    feature_parts, rest = rest[:parts], rest[parts:]
    par_parts, rest = rest[:parts], rest[parts:]
    pieces, rest = rest[:count], rest[count:]
    (par, feats_hbm, pad1_hbm, hidden_hbm, pad2_hbm, stats1, stats2) = rest[:7]
    feats, rounded, hidden, pad1, pad2, weight, weight_sem, sem = rest[7:]
    pixels, slots, _ = hidden.shape
    load_weight = WeightLoad(position, pieces, weight, weight_sem)
    load_weight.start()

    def put_par(columns, value):
        par[:, columns] = value

    load_full(par_parts, position[0], F32, put_par)

    def put(columns, value):
        feats[:, columns] = value

    load_full(feature_parts, position[0], BF16, put)
    save_feats = pltpu.make_async_copy(feats, feats_hbm, sem.at[1])
    save_feats.start()

    plan = Plan(position[0], slot_tile, slot_crop, slots)

    def slab1(at, lanes):
        return feats[pl.ds(pl.multiple_of(at * slots, slots), slots), lanes].astype(F32)

    mean, inverse = slab_stats(pixels, slots, slab1, plan.same)
    stats1[0], stats1[1] = mean, inverse
    norm_swish_pad(slab1, mean, inverse, par[G1 : G1 + 1, :], par[B1 : B1 + 1, :], pad1)
    fill_halo(pad1, plan)
    save_pad1 = pltpu.make_async_copy(pad1, pad1_hbm, sem.at[2])
    save_pad1.start()
    load_weight.wait()

    def step(row, carry):
        total = conv_rows(pad1, weight, row, slots, NT, False) + par[C1 : C1 + 1, :]
        hidden[pl.ds(row * TILE, TILE)] = total.reshape(TILE, slots, CH)
        return carry

    lax.fori_loop(0, TILE, step, 0)

    def slab2(at, lanes):
        return hidden[at, :, lanes]

    mean, inverse = slab_stats(pixels, slots, slab2, plan.same)
    stats2[0], stats2[1] = mean, inverse
    norm_swish_pad(
        slab2, mean, inverse, par[G2 : G2 + 1, :], par[B2 : B2 + 1, :], pad2, rounded
    )
    save_hidden = pltpu.make_async_copy(rounded, hidden_hbm, sem.at[3])
    save_hidden.start()
    fill_halo(pad2, plan)
    save_pad2 = pltpu.make_async_copy(pad2, pad2_hbm, sem.at[4])
    save_pad2.start()
    save_feats.wait()
    save_pad1.wait()
    save_hidden.wait()
    save_pad2.wait()


def first(position, tables, par_parts, parts, weight, slots):
    pixels = TILE * TILE
    rows = pixels * slots
    pad = (TILE + 2, TILE + 2, slots, CH)
    return call(
        functools.partial(first_kernel, len(parts), len(weight)),
        "sss" + "v" * len(parts) + "v" * len(parts) + "h" * len(weight),
        "vhhhhvv",
        [
            shape((16, CH), F32),
            shape((rows, CH), BF16),
            shape(pad, BF16),
            shape((pixels, slots, CH), BF16),
            shape(pad, BF16),
            shape((2, slots, CH), F32),
            shape((2, slots, CH), F32),
        ],
        [
            vmem((rows, CH), BF16),
            vmem((pixels, slots, CH), BF16),
            vmem((pixels, slots, CH), F32),
            vmem(pad, BF16),
            vmem(pad, BF16),
            vmem((9, CH, CH), BF16),
            weight_sems(weight),
            pltpu.SemaphoreType.DMA((5,)),
        ],
        "conv1_forward",
        2 * rows * CH * CH * 9,
        20 << 20,
    )(position, *tables[:2], *parts, *par_parts, *weight)


def second_kernel(count, position, slot_tile, slot_crop, par, feats, pad_hbm, *rest):
    pieces, rest = rest[:count], rest[count:]
    resid_hbm, normed_hbm, stats3 = rest[:3]
    resid, resid_tile, normed, pad, weight, rows_scr, weight_sem, sem = rest[3:]
    slots = pad.shape[2]
    pixels = TILE * TILE
    load_pad = pltpu.make_async_copy(pad_hbm, pad, sem.at[0])
    load_weight = WeightLoad(position, pieces, weight, weight_sem)
    load_pad.start()
    load_weight.start()
    plan = Plan(position[0], slot_tile, slot_crop, slots)
    same = plan.same
    load_pad.wait()
    load_weight.wait()
    wide = TILE * slots

    def step(row, carry):
        at = pl.ds(pl.multiple_of(row * wide, wide), wide)
        total = conv_rows(pad, weight, row, slots, NT, False) + par[C2 : C2 + 1, :]
        total = total + feats[at, :].astype(F32)
        for col in range(CH // 128):
            resid[col, at, :] = total[:, col * 128 : (col + 1) * 128]
        return carry

    lax.fori_loop(0, TILE, step, 0)

    def slab(at, lanes):
        return resid[lanes.start // 128, pl.ds(pl.multiple_of(at * slots, slots), slots), :]

    mean, inverse = slab_stats(pixels, slots, slab, same)
    stats3[0], stats3[1] = mean, inverse
    rows_scr[0], rows_scr[1] = mean, inverse * par[G3 : G3 + 1, :]
    bias = par[B3 : B3 + 1, :]

    def tile_step(slot, carry):
        at = pl.ds(pl.multiple_of(slot * pixels, pixels), pixels)
        centre, factor = rows_scr[0, pl.ds(slot, 1)], rows_scr[1, pl.ds(slot, 1)]
        for col, lanes in enumerate(lanes_of(CH)):
            value = resid[col, pl.ds(slot, pixels, stride=slots), :]
            resid_tile[at, lanes] = value.astype(BF16)
            scaled = (value - centre[:, lanes]) * factor[:, lanes]
            normed[at, lanes] = (scaled + bias[:, lanes]).astype(BF16)
        return carry

    lax.fori_loop(0, slots, tile_step, 0, unroll=2)
    save_resid = pltpu.make_async_copy(resid_tile, resid_hbm, sem.at[2])
    save_normed = pltpu.make_async_copy(normed, normed_hbm, sem.at[3])
    save_resid.start()
    save_normed.start()
    save_resid.wait()
    save_normed.wait()


def second(position, tables, par, feats, pad, weight, slots):
    pixels = TILE * TILE
    rows = pixels * slots
    return call(
        functools.partial(second_kernel, len(weight)),
        "sssvvh" + "h" * len(weight),
        "hhv",
        [shape((rows, CH), BF16), shape((rows, CH), BF16), shape((2, slots, CH), F32)],
        [
            vmem((CH // 128, rows, 128), F32),
            vmem((rows, CH), BF16),
            vmem((rows, CH), BF16),
            vmem(pad.shape, BF16),
            vmem((9, CH, CH), BF16),
            vmem((2, slots, CH), F32),
            weight_sems(weight),
            pltpu.SemaphoreType.DMA((4,)),
        ],
        "conv2_forward",
        2 * rows * CH * CH * 9,
        16 << 20,
    )(position, *tables[:2], par, feats, pad, *weight)


def attention_kernel(parts, outs, count, position, slot_tile, slot_crop, starts, ends, *rest):
    par, normed, resid, stats3 = rest[:4]
    tangent_parts, rest = rest[4 : 4 + parts], rest[4 + parts :]
    pieces, rest = rest[:count], rest[count:]
    out_parts, rest = rest[:outs], rest[outs:]
    grad_outs, rest = rest[:outs], rest[outs:]
    vecs_out, pad = rest[:2]
    (tangent, query, key, value, mixed_grad, mixed, query_grad, key_grad, value_grad) = rest[2:11]
    normed_grad, by_tile, rows_scr, weight, key_crop, work, vecs, weight_sem = rest[11:]
    load_weight = WeightLoad(position, pieces, weight, weight_sem)
    load_weight.start()
    wq, wk, wv, wp = (weight.at[k] for k in range(4))
    rows = normed.shape[0]
    pixels = TILE * TILE
    slots = rows // pixels
    me = position[0]
    base = me * slots
    block = 256
    per_block = block // pixels
    plan = Plan(me, slot_tile, slot_crop, slots)
    lane_slot = lax.broadcasted_iota(jnp.int32, (1, rows), 1) // pixels
    crops = jnp.zeros((1, rows), jnp.int32)
    for slot in range(slots):
        crops = jnp.where(lane_slot == slot, slot_crop[base + slot], crops)
    key_crop[...] = crops

    def put(columns, part):
        tangent[:, columns] = part

    load_full(tangent_parts, me, BF16, put)
    load_weight.wait()

    def project(at, carry):
        span = pl.ds(pl.multiple_of(at * block, block), block)
        left = normed[span, :]
        total = lax.dot_general(left, wq[...], NT, preferred_element_type=F32)
        query[span, :] = (total + par[QB : QB + 1, :]).astype(BF16)
        key[span, :] = lax.dot_general(left, wk[...], NT, preferred_element_type=F32).astype(BF16)
        total = lax.dot_general(left, wv[...], NT, preferred_element_type=F32)
        value[span, :] = (total + par[VB : VB + 1, :]).astype(BF16)
        mixed_grad[span, :] = jnp.dot(
            tangent[span, :], wp[...], preferred_element_type=F32
        ).astype(BF16)
        key_grad[span, :] = jnp.zeros((block, CH), F32)
        value_grad[span, :] = jnp.zeros((block, CH), F32)
        return carry

    lax.fori_loop(0, rows // block, project, 0)

    def attend(at, begin, width):
        span = pl.ds(pl.multiple_of(at * block, block), block)
        keys = pl.ds(pl.multiple_of(begin, 128), width)
        q, g = query[span, :], mixed_grad[span, :]
        scores = lax.dot_general(q, key[keys, :], NT, preferred_element_type=F32) * SCALE
        down = lax.broadcasted_iota(jnp.int32, (block, 1), 0) // pixels
        own_crop = jnp.zeros((block, 1), jnp.int32)
        for slot in range(per_block):
            own_crop = jnp.where(down == slot, slot_crop[base + at * per_block + slot], own_crop)
        scores = jnp.where(own_crop == key_crop[:, keys], scores, -1e30)
        top = jnp.max(scores, axis=1, keepdims=True)
        exponent = jnp.exp(scores - top)
        total = jnp.sum(exponent, axis=1, keepdims=True)
        prob = exponent * (1.0 / total)
        rounded = prob.astype(BF16)
        mixed[span, :] = jnp.dot(
            rounded, value[keys, :], preferred_element_type=F32
        ).astype(BF16)
        prob_grad = lax.dot_general(g, value[keys, :], NT, preferred_element_type=F32)
        inner = jnp.sum(prob * prob_grad, axis=1, keepdims=True)
        score_grad = (prob * (prob_grad - inner)).astype(BF16)
        query_grad[span, :] = (
            jnp.dot(score_grad, key[keys, :], preferred_element_type=F32) * SCALE
        ).astype(BF16)
        key_grad[keys, :] += lax.dot_general(score_grad, q, TN, preferred_element_type=F32)
        value_grad[keys, :] += lax.dot_general(rounded, g, TN, preferred_element_type=F32)

    def attend_step(at, carry):
        low_crop = slot_crop[base + at * per_block]
        high_crop = slot_crop[base + at * per_block + per_block - 1]
        low = starts[jnp.maximum(low_crop, 0)] - base
        low = jnp.where(low_crop < 0, at * per_block, low) // 2 * 2
        high = jnp.where(high_crop < 0, slots, ends[jnp.maximum(high_crop, 0)] - base)
        kind = sum(jnp.where(high - low > width, 1, 0) for width in WINDOWS[:-1])
        span = jnp.int32(WINDOWS[0])
        for number, width in enumerate(WINDOWS):
            span = jnp.where(kind == number, width, span)
        begin = jnp.minimum(low, slots - span) * pixels
        for number, width in enumerate(WINDOWS):

            @pl.when(kind == number)
            def _():
                attend(at, begin, width * pixels)

        return carry

    lax.fori_loop(0, rows // block, attend_step, 0)

    def back(at, carry):
        query_bias, value_bias, tangent_sum = carry
        span = pl.ds(pl.multiple_of(at * block, block), block)
        dq = query_grad[span, :]
        dk = (key_grad[span, :] * SCALE).astype(BF16)
        dv = value_grad[span, :].astype(BF16)
        key[span, :] = dk
        value[span, :] = dv
        total = jnp.dot(dq, wq[...], preferred_element_type=F32)
        total += jnp.dot(dk, wk[...], preferred_element_type=F32)
        total += jnp.dot(dv, wv[...], preferred_element_type=F32)
        normed_grad[span, :] = total
        result = lax.dot_general(mixed[span, :], wp[...], NT, preferred_element_type=F32)
        result = (result + par[PB : PB + 1, :] + resid[span, :].astype(F32)).astype(BF16)
        if outs == 1:
            out_parts[0][span, :] = result
        else:
            mixed_scr = query
            mixed_scr[span, :] = result
        query_bias += jnp.sum(dq.astype(F32), axis=0, keepdims=True)
        value_bias += jnp.sum(dv.astype(F32), axis=0, keepdims=True)
        tangent_sum += jnp.sum(tangent[span, :].astype(F32), axis=0, keepdims=True)
        return query_bias, value_bias, tangent_sum

    zero = jnp.zeros((1, CH), F32)
    query_bias, value_bias, tangent_sum = lax.fori_loop(
        0, rows // block, back, (zero, zero, zero)
    )
    if outs == 2:
        local = out_parts[0].shape[1]
        own = pl.ds(pl.multiple_of(me * local, local), local)
        other = pl.ds(pl.multiple_of((1 - me) * local, local), local)
        out_parts[0][...] = query[:, own]
        out_parts[1][...] = query[:, other]
    left = normed[...]
    for number, grad in enumerate((query_grad, key, value)):
        total = lax.dot_general(grad[...], left, TN, preferred_element_type=F32)
        store_grad(total, grad_outs, work, position, number, 4, 4)
    total = lax.dot_general(tangent[...], mixed[...], TN, preferred_element_type=F32)
    store_grad(total, grad_outs, work, position, 3, 4, 4)

    def sums(slot, carry):
        span = pl.ds(pl.multiple_of(slot * pixels, pixels), pixels)
        row = pl.ds(slot, 1)
        centre, factor = stats3[0, row], stats3[1, row]
        plains, crosseds = [], []
        for lanes in lanes_of(CH):
            upstream = normed_grad[span, lanes]
            hat = (resid[span, lanes].astype(F32) - centre[:, lanes]) * factor[:, lanes]
            plains.append(jnp.sum(upstream, axis=0, keepdims=True))
            crosseds.append(jnp.sum(upstream * hat, axis=0, keepdims=True))
        rows_scr[0, row] = jnp.concatenate(plains, axis=1)
        rows_scr[1, row] = jnp.concatenate(crosseds, axis=1)
        return carry

    lax.fori_loop(0, slots, sums, 0)
    same = plan.same
    gain = par[G3 : G3 + 1, :]
    plain, crossed = rows_scr[0], rows_scr[1]
    vecs[...] = jnp.zeros_like(vecs)
    vecs[G3 : G3 + 1, :] = jnp.sum(crossed, axis=0, keepdims=True)
    vecs[B3 : B3 + 1, :] = jnp.sum(plain, axis=0, keepdims=True)
    vecs[QB : QB + 1, :] = query_bias
    vecs[VB : VB + 1, :] = value_bias
    vecs[PB : PB + 1, :] = tangent_sum
    rows_scr[0] = crop_mean(same, plain * gain)
    rows_scr[1] = crop_mean(same, crossed * gain)

    def apply(slot, carry):
        span = pl.ds(pl.multiple_of(slot * pixels, pixels), pixels)
        row = pl.ds(slot, 1)
        centre, factor = stats3[0, row], stats3[1, row]
        slope = factor * gain
        level = factor * rows_scr[0, row]
        tilt = factor * factor * rows_scr[1, row]
        for col, lanes in enumerate(lanes_of(CH)):
            centred = resid[span, lanes].astype(F32) - centre[:, lanes]
            grad = normed_grad[span, lanes] * slope[:, lanes] - level[:, lanes]
            grad = grad - centred * tilt[:, lanes]
            by_tile[col, span, :] = tangent[span, lanes].astype(F32) + grad
        return carry

    lax.fori_loop(0, slots, apply, 0)

    def spread(row, carry):
        total = carry
        for col in range(TILE):
            at = row * TILE + col
            slab = jnp.concatenate(
                [
                    by_tile[c, pl.ds(at, slots, stride=pixels), :] for c in range(CH // 128)
                ],
                axis=1,
            )
            rounded = slab.astype(BF16)
            pad[row + 1, col + 1] = rounded
            total += jnp.sum(rounded.astype(F32), axis=0, keepdims=True)
        return total

    vecs[C2 : C2 + 1, :] = lax.fori_loop(0, TILE, spread, zero)
    store_vectors(vecs, vecs_out, me)
    fill_halo(pad, plan)


def attention(position, tables, par, normed, resid, stats3, tangent_parts, weight, slots):
    pixels = TILE * TILE
    rows = pixels * slots
    parts = len(tangent_parts)
    pad = (TILE + 2, TILE + 2, slots, CH)
    if parts == 2:
        out_shapes = [shape((rows, CH // 2), BF16)] * 2
    else:
        out_shapes = [shape((rows, CH), BF16)]
    outs = len(out_shapes)
    result = call(
        functools.partial(attention_kernel, parts, outs, len(weight)),
        "sssss" + "v" * (4 + parts) + "h" * len(weight),
        "v" * (2 * outs + 2),
        out_shapes
        + grad_shapes(4, outs == 2)
        + [vector_shape(outs == 2), shape(pad, BF16)],
        [vmem((rows, CH), BF16)] * 7
        + [vmem((rows, CH), F32)] * 3
        + [vmem((CH // 128, rows, 128), F32), vmem((2, slots, CH), F32)]
        + [vmem((4, CH, CH), BF16), vmem((1, rows), jnp.int32), vmem((CH, CH), F32)]
        + [vmem((16, CH), F32)]
        + [weight_sems(weight)],
        "attention",
        30 << 30,
        24 << 20,
    )(
        position,
        *tables,
        par,
        normed,
        resid,
        stats3,
        *tangent_parts,
        *weight,
    )
    return result[:outs], result[outs : 2 * outs], result[2 * outs :]


def weight_grad_kernel(paired, first, extra, position, active, grad, *rest):
    outs = 2 if paired else 1
    extras, rest = rest[: outs if extra else 0], rest[outs if extra else 0 :]
    out_parts, (flipped, work, sem) = rest[:outs], rest[outs:]
    copies = []
    for half, part in enumerate(extras):
        for at in range(8):
            source = part.at[pl.ds(at * extra * BLOCK, extra * BLOCK)]
            target = out_parts[half].at[pl.ds(at * first * BLOCK, extra * BLOCK)]
            copies.append(pltpu.make_async_copy(source, target, sem.at[half, at]))
    for copy in copies:
        copy.start()
    slots = active.shape[2]
    wide = TILE * slots
    for row in range(TILE):
        left = grad[row + 1, 1 : TILE + 1].reshape(wide, CH)
        flipped[:, row * wide : (row + 1) * wide] = left.T

    def step(front, tap, carry):
        right = active[pl.ds(tap // 3, TILE), pl.ds(tap % 3, TILE)].reshape(TILE * wide, CH)
        total = jnp.dot(flipped[...], right, preferred_element_type=F32)
        store_grad(total, out_parts, work, position, tap + extra, first, 9 + extra, front)
        return carry

    lax.fori_loop(0, first - extra, functools.partial(step, True), 0)
    if first - extra < 9:
        lax.fori_loop(first - extra, 9, functools.partial(step, False), 0)
    for copy in copies:
        copy.wait()


def weight_grad(position, active, grad, paired, slots, name, first=9, extras=()):
    rows = TILE * TILE * slots
    extra = 4 if extras else 0
    shapes = grad_shapes(9 + extra, paired)
    return call(
        functools.partial(weight_grad_kernel, paired, first, extra),
        "svv" + "h" * len(extras),
        "v" * len(shapes),
        shapes,
        [
            vmem((CH, rows), BF16),
            vmem((CH, CH), F32),
            pltpu.SemaphoreType.DMA((2, 8)),
        ],
        name,
        2 * rows * CH * CH * 9,
        12 << 20,
    )(position, active, grad, *extras)


def swish_back(upstream, before):
    gate = sigmoid(before)
    return upstream * (gate + before * gate * (1.0 - gate))


def norm_back_sums(source, upstream, mean, inverse, gain, bias, slots):
    plains, crosseds = [], []
    for lanes in lanes_of(upstream.shape[2]):
        centre, factor = mean[:, lanes], inverse[:, lanes]
        slope, offset = gain[:, lanes], bias[:, lanes]

        def step(at, carry):
            plain, crossed = carry
            hat = (source(at, lanes) - centre) * factor
            grad = swish_back(upstream[at, :, lanes], hat * slope + offset)
            upstream[at, :, lanes] = grad
            return plain + grad, crossed + grad * hat

        zero = jnp.zeros((slots, 128), F32)
        plain, crossed = lax.fori_loop(0, TILE * TILE, step, (zero, zero), unroll=4)
        plains.append(plain)
        crosseds.append(crossed)
    return jnp.concatenate(plains, axis=1), jnp.concatenate(crosseds, axis=1)


def norm_back_apply(source, upstream, mean, inverse, gain, plain, crossed, put):
    for lanes in lanes_of(upstream.shape[2]):
        centre, factor = mean[:, lanes], inverse[:, lanes]
        slope = factor * gain[:, lanes]
        level = factor * plain[:, lanes]
        tilt = factor * factor * crossed[:, lanes]

        def step(at, carry):
            centred = source(at, lanes) - centre
            put(at, lanes, upstream[at, :, lanes] * slope - level - centred * tilt)
            return carry

        lax.fori_loop(0, TILE * TILE, step, 0, unroll=8)


def middle_kernel(count, position, slot_tile, slot_crop, par, stats2, pad_hbm, hidden_hbm, *rest):
    pieces, rest = rest[:count], rest[count:]
    pad_out_hbm, vecs_out = rest[:2]
    pad, weight, hidden, upstream, pad_out, vecs, totals, weight_sem, sem = rest[2:]
    slots = pad.shape[2]
    load_pad = pltpu.make_async_copy(pad_hbm, pad, sem.at[0])
    load_weight = WeightLoad(position, pieces, weight, weight_sem)
    load_hidden = pltpu.make_async_copy(hidden_hbm, hidden, sem.at[2])
    load_pad.start()
    load_weight.start()
    load_hidden.start()
    plan = Plan(position[0], slot_tile, slot_crop, slots)
    same = plan.same
    load_pad.wait()
    load_weight.wait()

    def step(row, carry):
        total = conv_rows(pad, weight, row, slots, NN, True)
        upstream[pl.ds(row * TILE, TILE)] = total.reshape(TILE, slots, CH)
        return carry

    lax.fori_loop(0, TILE, step, 0)
    load_hidden.wait()
    mean, inverse = stats2[0], stats2[1]
    gain, bias = par[G2 : G2 + 1, :], par[B2 : B2 + 1, :]

    def source(at, lanes):
        return hidden[at, :, lanes].astype(F32)

    plain, crossed = norm_back_sums(
        source, upstream, mean, inverse, gain, bias, slots
    )
    vecs[...] = jnp.zeros_like(vecs)
    vecs[G2 : G2 + 1, :] = jnp.sum(crossed, axis=0, keepdims=True)
    vecs[B2 : B2 + 1, :] = jnp.sum(plain, axis=0, keepdims=True)
    plain = crop_mean(same, plain * gain)
    crossed = crop_mean(same, crossed * gain)

    totals[...] = jnp.zeros_like(totals)

    def put(at, lanes, grad):
        rounded = grad.astype(BF16)
        pad_out[at // TILE + 1, at % TILE + 1, :, lanes] = rounded
        totals[:, lanes] += rounded.astype(F32)

    norm_back_apply(source, upstream, mean, inverse, gain, plain, crossed, put)
    vecs[C1 : C1 + 1, :] = jnp.sum(totals[...], axis=0, keepdims=True)
    store_vectors(vecs, vecs_out, position[0])
    fill_halo(pad_out, plan)
    save = pltpu.make_async_copy(pad_out, pad_out_hbm, sem.at[3])
    save.start()
    save.wait()


def middle(position, tables, par, stats2, pad, weight, hidden, slots):
    pixels = TILE * TILE
    rows = pixels * slots
    return call(
        functools.partial(middle_kernel, len(weight)),
        "sssvvhh" + "h" * len(weight),
        "hv",
        [shape(pad.shape, BF16), vector_shape(len(weight) > 1)],
        [
            vmem(pad.shape, BF16),
            vmem((9, CH, CH), BF16),
            vmem((pixels, slots, CH), BF16),
            vmem((pixels, slots, CH), F32),
            vmem(pad.shape, BF16),
            vmem((16, CH), F32),
            vmem((slots, CH), F32),
            weight_sems(weight),
            pltpu.SemaphoreType.DMA((4,)),
        ],
        "conv2_input_grad",
        2 * rows * CH * CH * 9,
        16 << 20,
    )(position, *tables[:2], par, stats2, pad, hidden, *weight)


def last_kernel(
    whose, count, position, slot_tile, slot_crop, par, stats1, vecs2, vecs3, *rest
):
    feats_hbm, pad_hbm, resid_hbm = rest[:3]
    pieces, rest = rest[3 : 3 + count], rest[3 + count :]
    out, vecs, pad, weight, feats, resid, upstream, weight_sem, sem = rest
    slots = pad.shape[2]
    width = upstream.shape[2]
    pixels = TILE * TILE
    me = position[0]
    columns = None
    span = pl.ds(0, width)
    if width < CH:
        columns = span = pl.ds(pl.multiple_of((me ^ whose) * width, width), width)
    load_weight = WeightLoad(position, pieces, weight, weight_sem, columns)
    load_pad = pltpu.make_async_copy(pad_hbm, pad, sem.at[0])
    inner = pl.ds(1, TILE)
    load_resid = pltpu.make_async_copy(resid_hbm.at[inner, inner, :, span], resid, sem.at[1])
    load_feats = pltpu.make_async_copy(feats_hbm.at[:, span], feats, sem.at[2])
    load_pad.start()
    load_weight.start()
    load_feats.start()
    load_resid.start()
    plan = Plan(me, slot_tile, slot_crop, slots)
    same = plan.same
    load_pad.wait()
    load_weight.wait()

    def step(row, carry):
        total = conv_rows(pad, weight, row, slots, NN, True)
        upstream[pl.ds(row * TILE, TILE)] = total.reshape(TILE, slots, width)
        return carry

    lax.fori_loop(0, TILE, step, 0)
    load_feats.wait()
    load_resid.wait()
    mean, inverse = stats1[0, :, span], stats1[1, :, span]
    gain, bias = par[G1 : G1 + 1, span], par[B1 : B1 + 1, span]

    def source(at, lanes):
        return feats[pl.ds(pl.multiple_of(at * slots, slots), slots), lanes].astype(F32)

    plain, crossed = norm_back_sums(source, upstream, mean, inverse, gain, bias, slots)
    vecs[...] = vecs2[...] + vecs3[...] if width == CH else vecs2[whose] + vecs3[whose]
    vecs[G1 : G1 + 1, :] = jnp.sum(crossed, axis=0, keepdims=True)
    vecs[B1 : B1 + 1, :] = jnp.sum(plain, axis=0, keepdims=True)
    if out.shape[0] > pixels * slots:
        begin = pixels * slots
        out[begin : begin + 16, :] = vecs[...].astype(BF16)
        out[begin + 16 : begin + 32, :] = jnp.zeros((16, width), BF16)
    plain = crop_mean(same, plain * gain)
    crossed = crop_mean(same, crossed * gain)

    def put(at, lanes, grad):
        rows = pl.ds(pl.multiple_of(at * slots, slots), slots)
        grad = resid[at // TILE, at % TILE, :, lanes].astype(F32) + grad
        out[rows, lanes] = grad.astype(out.dtype)

    norm_back_apply(source, upstream, mean, inverse, gain, plain, crossed, put)


def last(position, tables, par, stats1, vecs, feats, pad, weight, resid_grad, whose, slots):
    pixels = TILE * TILE
    rows = pixels * slots
    width = CH // 2 if len(weight) > 1 else CH
    return call(
        functools.partial(last_kernel, whose, len(weight)),
        "sssvvvvhhh" + "h" * len(weight),
        "vv",
        [
            shape((rows + (32 if whose else 0), width), F32 if width < CH and whose == 0 else BF16),
            shape((16, width), F32),
        ],
        [
            vmem(pad.shape, BF16),
            vmem((9, CH, width), BF16),
            vmem((rows, width), BF16),
            vmem((TILE, TILE, slots, width), BF16),
            vmem((pixels, slots, width), F32),
            weight_sems(weight),
            pltpu.SemaphoreType.DMA((3,)),
        ],
        "conv1_input_grad",
        2 * rows * CH * width * 9,
        10 << 20,
    )(position, *tables[:2], par, stats1, *vecs, feats, pad, resid_grad, *weight)


def after(value, *others):
    flat, tree = jax.tree.flatten(value)
    extra = jax.tree.leaves(others)
    held = lax.optimization_barrier(tuple(flat) + tuple(extra))
    return jax.tree.unflatten(tree, list(held[: len(flat)]))


def add(*terms):
    total = terms[0].astype(F32)
    for term in terms[1:]:
        total = total + term.astype(F32)
    return total


def swap(value, axis):
    return lax.ppermute(value, axis, [(0, 1), (1, 0)])


def to_all(value, axes, count):
    return lax.all_to_all(jnp.broadcast_to(value[None], (count,) + value.shape), axes, 0, 0)


QUAD = ("y", "near")


def from_quad(values):
    return [
        lax.ppermute(value, ("near", "y"), [(at, at ^ bits) for at in range(4)])
        for bits, value in zip((2, 1, 3), values)
    ]


def rounded_sum(terms):
    total = terms[0].astype(F32)
    for term in terms[1:]:
        total = total + term.astype(F32)
    return total.astype(BF16)


def vector_rows(vectors):
    rows, width = vectors.shape
    return jnp.pad(vectors.astype(BF16), ((0, BLOCK - rows), (0, CH - width)))


class Reduction:
    def __init__(self, halves, first, count):
        self.stage, self.first, self.count = 0, first, count
        self.state = (halves[0], halves[1], swap(halves[1], "core"))

    def advance(self, *others, vectors=None):
        if others:
            self.state = after(self.state, *others)
        self.stage += 1
        front = self.first * BLOCK
        back = (self.count - self.first) * BLOCK
        state = self.state
        if self.stage == 1:
            mine, _, came = state

            def part(begin, size):
                span = slice(begin, begin + size)
                return rounded_sum([mine[span], came[span]])

            start = 8 * front
            keep = part(0, 4 * front), part(start, 2 * back)
            sent_front = part(4 * front, 4 * front)
            sent_back = [part(start + q * 2 * back, 2 * back) for q in (1, 2, 3)]
            self.state = keep, (swap(sent_front, "chan"), from_quad(sent_back))
            return sent_front, sent_back
        if self.stage == 2:
            (mine_front, mine_back), (came_front, came_back) = state
            piece = [slice(q * front, (q + 1) * front) for q in range(4)]
            sent_front = [rounded_sum([mine_front[piece[q]], came_front[piece[q]]]) for q in (1, 2, 3)]
            sent_back = rounded_sum([mine_back[back:]] + [value[back:] for value in came_back])
            keep_front = [mine_front[:front], came_front[:front]]
            keep_back = [mine_back[:back]] + [value[:back] for value in came_back]
            self.state = keep_front, keep_back, (from_quad(sent_front), swap(sent_back, "chan"))
            return sent_front, sent_back
        if self.stage == 3:
            mine_front, mine_back, (came_front, came_back) = state
            parts = [rounded_sum(mine_front + came_front), rounded_sum(mine_back + [came_back])]
            if vectors is not None:
                parts.append(vector_rows(vectors))
            value = jnp.concatenate(parts, axis=0)
            self.state = value, swap(value, "far")
            return value
        if self.stage == 4:
            value = rounded_sum(list(state))
            self.state = [value] + from_quad([value] * 3)
            return value
        if self.stage == 5:
            mine = jnp.concatenate(state, axis=0)
            self.state = mine, swap(mine, "core")
            return mine

    @property
    def pieces(self):
        return list(self.state)


def assemble_kernel(sizes, position, mine, other, *outs):
    units = mine.shape[0] // (4 * BLOCK)
    vectors = None
    for number, part in enumerate((mine, other)):
        for at in range(4):
            row = ((position[1] ^ number) * 4 + (position[2] ^ at)) * BLOCK
            rows = pl.ds(pl.multiple_of(row, BLOCK), BLOCK)
            unit = 0
            for out, size in zip(outs, sizes):
                for index in range(max(size, 1)):
                    begin = (at * units + unit) * BLOCK
                    value = part[begin : begin + BLOCK, :].astype(F32)
                    if size:
                        out[index, rows, :] = value
                    else:
                        out[rows, :] = value
                    unit += 1
            if unit < units:
                begin = (at * units + unit) * BLOCK
                term = part[begin : begin + BLOCK, :].astype(F32)
                vectors = term if vectors is None else vectors + term
    if vectors is not None:
        outs[-1][...] = vectors


def assemble(position, pieces, sizes, vectors, name):
    shapes = [shape(((size,) if size else ()) + (8 * BLOCK, CH), F32) for size in sizes]
    if vectors:
        shapes.append(shape((BLOCK, CH), F32))
    return call(
        functools.partial(assemble_kernel, sizes),
        "svv",
        "v" * len(shapes),
        shapes,
        [],
        name,
        4 << 30,
        6 << 20,
    )(position, *pieces)


def body(
    paired,
    features,
    crop_ids,
    cotangent,
    norm1_gain,
    norm1_bias,
    conv1_weight,
    conv1_bias,
    norm2_gain,
    norm2_bias,
    conv2_weight,
    conv2_bias,
    norm3_gain,
    norm3_bias,
    query_weight,
    query_bias,
    key_weight,
    value_weight,
    value_bias,
    proj_weight,
    proj_bias,
):
    _, local, pixels = features.shape
    devices = lax.axis_size("chan")
    index = lax.axis_index("chan").astype(jnp.int32)
    tiles = pixels // (TILE * TILE)
    slots = tiles if devices == 1 else tiles // 2
    if paired:
        core, down, near = [lax.axis_index(a).astype(jnp.int32) for a in ("core", "y", "near")]
        quad = down * 2 + near
        piece = core * 4 + quad
    else:
        core = quad = jnp.int32(0)
    position = jnp.stack([index, core, quad])

    def exchange(parts):
        if paired:
            return [parts[0], swap(parts[1], "chan")]
        if devices == 2:
            parts = [jnp.where(index == 0, parts[k], parts[1 - k]) for k in range(2)]
        moved = lax.all_to_all(jnp.stack(parts), "chan", 0, 0)
        return [jnp.transpose(moved, (1, 0, 2)).reshape(moved.shape[1], CH)]

    def give_back(parts):
        if paired:
            return [parts[0], swap(parts[1], "chan")]
        whole = parts[0].reshape(parts[0].shape[0], devices, local)
        moved = lax.all_to_all(jnp.transpose(whole, (1, 0, 2)), "chan", 0, 0)
        parts = [moved[at] for at in range(devices)]
        if devices == 2:
            parts = [jnp.where(index == 0, parts[k], parts[1 - k]) for k in range(2)]
        return parts

    lanes = -(-local // 128) * 128

    def widened(signal):
        return jnp.pad(signal, ((0, lanes - local), (0, 0))) if lanes > local else signal

    def narrowed(parts):
        return [part[:, :local] for part in parts] if lanes > local else parts

    def unpack_lanes(parts, by_pixel, dtype, name):
        if lanes > local:
            parts = [jnp.pad(part, ((0, 0), (0, lanes - local))) for part in parts]
        whole = unpack(position, tables[0], parts, pixels, by_pixel, dtype, slots, name)
        return whole[:local]

    vectors = jnp.stack(
        [
            norm1_gain,
            norm1_bias,
            conv1_bias,
            norm2_gain,
            norm2_bias,
            conv2_bias,
            norm3_gain,
            norm3_bias,
            query_bias,
            value_bias,
            proj_bias,
        ]
        + [jnp.zeros_like(proj_bias)] * 5
    )
    small = jnp.stack([query_weight, key_weight, value_weight, proj_weight])
    if paired:
        eighth = local // 8
        part = lax.dynamic_slice_in_dim(conv1_weight, piece * eighth, eighth, 1)
        eighth1 = swap(part, "chan")
        part = lax.dynamic_slice_in_dim(conv2_weight, piece * eighth, eighth, 1)
        eighth2 = swap(part, "chan")
        par_parts = [vectors, swap(vectors, "chan")]
    else:
        par_parts = [lax.all_gather(vectors, "chan", axis=1, tiled=True)]
        weight1 = [lax.all_gather(conv1_weight, "chan", axis=1, tiled=True)]
    tables, packed = pack_first(
        position, crop_ids[0], widened(features[0]), devices, slots, "pack_features"
    )
    feature_parts = exchange(narrowed(packed))
    if paired:
        eighth1, par_parts[1] = after((eighth1, par_parts[1]), packed[1])
        mine = to_all(eighth1, QUAD, 4)
        weight1 = [conv1_weight, mine, swap(mine, "core")]
    packed = pack(
        position, tables[0], widened(cotangent[0]), False, devices, slots, "pack_cotangent"
    )
    packed = list(packed)
    if paired:
        eighth2, small = after((eighth2, small), feature_parts[1], weight1[1], packed[1])
        weight2 = [conv2_weight, to_all(eighth2, ("core",) + QUAD, 8)]
        part = lax.dynamic_slice_in_dim(small, core * (local // 2), local // 2, 1)
        own_small = swap(part, "chan")
    else:
        weight2 = [lax.all_gather(conv2_weight, "chan", axis=1, tiled=True)]
        weight3 = [lax.all_gather(small, "chan", axis=1, tiled=True)]
        tangent_parts = exchange(narrowed(packed))
    par, feats, pad1, hidden, pad2, stats1, stats2 = first(
        position, tables, par_parts, feature_parts, weight1, slots
    )
    if paired:
        own_small, packed[1] = after((own_small, packed[1]), pad2)
        tangent_parts = [packed[0], swap(packed[1], "chan")]
        weight3 = [small, own_small, swap(own_small, "core")]
    resid, normed, stats3 = second(position, tables, par, feats, pad2, weight2, slots)
    if paired:
        weight3 = after(weight3, normed)
    out_parts, small_grads, (vecs3, grad2) = attention(
        position, tables, par, normed, resid, stats3, tangent_parts, weight3, slots
    )
    out_parts = give_back(out_parts)
    if paired:
        resid_grad = grad2
        halves = weight_grad(
            position, pad2, grad2, True, slots, "conv2_weight_grad", 8, small_grads
        )
        chain2 = Reduction(halves, 8, 13)
        grad2 = after(grad2, halves[1])
        grad1, vecs2 = middle(position, tables, par, stats2, grad2, weight2, hidden, slots)
        back = functools.partial(last, position, tables, par, stats1, (vecs2, vecs3), feats)
        sent = chain2.advance(grad1, out_parts[1])
        halves = weight_grad(
            position, pad1, after(grad1, sent), True, slots, "conv1_weight_grad", 5
        )
        sent = chain2.advance(halves[1])
        chain1 = Reduction(after(halves, sent), 5, 9)
        grad1 = after(grad1, sent, halves[1])
        in_other, _ = back(grad1, weight1, resid_grad, 1, slots)
        sent = chain1.advance(in_other, chain2.state)
        in_got = swap(in_other, "chan")
        grad1 = after(grad1, sent, in_other)
        in_own, vecs_own = back(grad1, weight1, resid_grad, 0, slots)
        sent = chain1.advance(in_own), chain2.advance(in_own)
        output = unpack_lanes(after(out_parts, sent), False, BF16, "unpack_output")
        rows = in_own.shape[0]
        vecs = vecs_own + in_got[rows : rows + 16].astype(F32)
        sent = chain1.advance(output, in_got, vectors=vecs), chain2.advance(output)
        in_parts = after([in_own, in_got], sent)
        input_grad = unpack_lanes(in_parts, True, F32, "unpack_input_grad")
        sent = chain1.advance(input_grad), chain2.advance(input_grad)
        sent = chain1.advance()
        small_grads = assemble(
            position, after(chain2.pieces, sent), [0, 0, 0, 0, 9], False, "conv2_grads"
        )
        small_grads, weight2_grad = small_grads[:4], small_grads[4]
        weight1_grad, vecs = assemble(position, chain1.pieces, [9], True, "conv1_grads")
        vecs = vecs[:16, :local]
    else:
        output = unpack_lanes(out_parts, False, BF16, "unpack_output")
        grads2 = weight_grad(position, pad2, grad2, False, slots, "conv2_weight_grad")
        grad1, vecs2 = middle(position, tables, par, stats2, grad2, weight2, hidden, slots)
        grads1 = weight_grad(position, pad1, grad1, False, slots, "conv1_weight_grad")
        in_all, vecs1 = last(
            position, tables, par, stats1, (vecs2, vecs3), feats, grad1, weight1, grad2, 0, slots
        )
        input_grad = unpack_lanes(give_back([in_all]), True, F32, "unpack_input_grad")

        def total(grad, axis):
            part = lax.psum_scatter(grad, "chan", scatter_dimension=axis, tiled=True)
            return lax.psum(part, "dp").astype(F32)

        small_grads, weight2_grad, weight1_grad = [
            total(g[0], 1) for g in (small_grads, grads2, grads1)
        ]
        vecs = total(vecs1, 1)
    gq, gk, gv, gp = small_grads if paired else [small_grads[k] for k in range(4)]
    return (
        output[None],
        input_grad[None],
        vecs[G1],
        vecs[B1],
        weight1_grad,
        vecs[C1],
        vecs[G2],
        vecs[B2],
        weight2_grad,
        vecs[C2],
        vecs[G3],
        vecs[B3],
        gq,
        vecs[QB],
        gk,
        gv,
        vecs[VB],
        gp,
        vecs[PB],
    )


def solution(mesh):
    paired = mesh.shape["dp"] == 16 and mesh.shape["chan"] == 2
    rows = "dp"
    if paired:
        rows = ("far", "near", "y", "core")
        mesh = jax.sharding.Mesh(mesh.devices.reshape((2,) * 5), rows + ("chan",))
    canvas = P(rows, "chan", None)
    vector = P("chan")
    conv = P(None, "chan", None)
    matrix = P("chan", None)
    placed = (
        (canvas, P(rows, None, None), canvas)
        + (vector, vector, conv, vector, vector, vector, conv, vector, vector, vector)
        + (matrix, vector, matrix, matrix, vector, matrix, vector)
    )
    results = (
        (canvas, canvas, vector, vector, conv, vector, vector, vector, conv, vector)
        + (vector, vector, matrix, vector, matrix, matrix, vector, matrix, vector)
    )
    return jax.shard_map(functools.partial(body, paired), mesh=mesh, in_specs=placed, out_specs=results, check_vma=False)
```

```python
import functools
import itertools

import jax
import jax.numpy as jnp
import numpy as np
from jax import lax
from jax.experimental import pallas as pl
from jax.experimental.pallas import tpu as pltpu
from jax.sharding import PartitionSpec as P

CH = 512
GROUPS = 32
CROPS = 16
TILE = 8
BANDS = 4
EPS = 1e-06
F32 = jnp.float32
BF16 = jnp.bfloat16
HIGH = lax.Precision.HIGHEST
NN = (((1,), (0,)), ((), ()))
NT = (((1,), (1,)), ((), ()))
TN = (((0,), (0,)), ((), ()))
VMEM = pltpu.VMEM
ANY = pl.ANY
SCALE = CH ** (-0.5)


def band_layouts(units):
    return [
        tuple(np.diff((0,) + cuts + (units,)))
        for cuts in itertools.combinations(range(1, units), BANDS - 1)
    ]


PITCH = 8
QUERIES = 8
KEYS = 8


def window_cost(starts, sizes, slots):
    total = 0.0
    for block in range(0, slots, QUERIES):
        inside = [
            (starts <= at) & (at < starts + sizes) for at in (block, block + QUERIES - 1)
        ]
        low = (starts * inside[0]).sum(axis=-1) // 2 * 2
        high = ((starts + sizes) * inside[1]).sum(axis=-1)
        total = total + (high - low + KEYS - 1) // KEYS + 0.25
    return total


def best_starts(sizes, slots):
    layouts = sizes.shape[0]
    masks = np.arange(1 << (CROPS - 1), dtype=np.int32)
    bits = ((masks[None, :] >> np.arange(CROPS)[:, None]) & 1).astype(np.float32)
    picks = []
    for row in sizes.astype(np.float32):
        filled, squares = row @ bits, (row * row) @ bits
        cost = np.abs(squares - (row * row).sum() / 2) + 1e6 * np.abs(filled - slots)
        picks.append(bits[:, np.argpartition(cost, 4)[:4]].T)
        picks[-1] = picks[-1][(picks[-1] @ row) == slots]
        picks[-1] = picks[-1][np.arange(4) % len(picks[-1])]
    halves = np.array(picks, np.int32)
    halves = np.stack([1 - halves, halves], axis=2)
    held = halves * sizes[:, None, None, :]
    draw = np.random.RandomState(0)
    best = np.full((layouts, 4, 2), 1e9, np.float32)
    chosen = np.zeros(held.shape, np.int32)
    for trial in range(20):
        key = draw.rand(CROPS)[None, None, None, :] + 0.0 * held
        if trial == 0:
            key = -held + 0.01 * key
        elif trial < 8:
            key = key + 2.0 * (held % QUERIES != 0)
        order = np.argsort(key, axis=-1)
        ordered = np.take_along_axis(held, order, axis=-1)
        begin = np.cumsum(ordered, axis=-1) - ordered
        starts = np.zeros_like(held)
        np.put_along_axis(starts, order, begin, axis=-1)
        cost = window_cost(starts, held, slots)
        better = cost < best
        best = np.where(better, cost, best)
        chosen = np.where(better[..., None], starts, chosen)
    pick = np.argmin(best.max(axis=2), axis=1)
    rows = np.arange(layouts)
    owner, starts = halves[rows, pick, 1], chosen[rows, pick]
    return np.where(owner == 1, starts[:, 1] + slots, starts[:, 0])


@functools.lru_cache(maxsize=None)
def start_tables(devices, units, slots):
    layouts = band_layouts(units)
    rank = np.zeros(1 << (units - 1), np.int32)
    for number, sizes in enumerate(layouts):
        cuts = np.cumsum(sizes)[:-1]
        rank[sum(1 << (int(c) - 1) for c in cuts)] = number
    sizes = np.array(
        [[r * c for r in rows for c in cols] for rows in layouts for cols in layouts], np.int32
    )
    if devices == 2:
        starts = best_starts(sizes, slots)
    else:
        starts = np.zeros(sizes.shape, np.int32)
        for at, row in enumerate(sizes):
            loads = [0] * devices
            for crop in sorted(range(CROPS), key=lambda c: -row[c]):
                device = loads.index(min(loads))
                starts[at, crop] = device * slots + loads[device]
                loads[device] += int(row[crop])
    assert ((starts % slots) + sizes <= slots).all() and starts.max() < 256
    return rank, starts


def packed_tables(devices, units, slots):
    rank, starts = start_tables(devices, units, slots)
    shifts = np.arange(0, 32, 8, dtype=np.int64)
    words = (starts.reshape(-1, 4, 4).astype(np.int64) << shifts).sum(axis=2)
    words = np.where(words >= 1 << 31, words - (1 << 32), words)
    return np.concatenate([rank, words.reshape(-1).astype(np.int32)])


def write_plan(devices, slots, ids, table, slot_tile, slot_crop, starts, ends):
    units = ids.shape[0] // TILE
    count = units * units
    layouts = len(band_layouts(units))

    def code(at):
        bits = 0
        for step in range(units - 1):
            bits = bits + jnp.where(at(step) != at(step + 1), 1 << step, 0)
        return table[bits]

    def row_id(step):
        return ids[TILE * step, 0]

    def col_id(step):
        return ids[0, TILE * step]

    layout = code(row_id) * layouts + code(col_id)
    words = [table[(1 << (units - 1)) + 4 * layout + part] for part in range(4)]
    if devices * slots > count:

        def clear(at, carry):
            slot_tile[at] = -1
            slot_crop[at] = -1
            return carry

        lax.fori_loop(0, devices * slots, clear, 0)
    for crop in range(CROPS):
        start = lax.shift_right_logical(words[crop // 4], jnp.int32(8 * (crop % 4))) & 255
        starts[crop] = start
        ends[crop] = start

    def place(row, carry):
        for col in range(units):
            crop = ids[row * TILE, col * TILE]
            at = ends[crop]
            slot_tile[at] = row * units + col
            slot_crop[at] = crop
            ends[crop] = at + 1
        return carry

    lax.fori_loop(0, units, place, 0)


class Plan:
    def __init__(self, me, slot_tile, slot_crop, slots):
        self.slots = slots
        base = me * slots
        lane = lax.broadcasted_iota(jnp.int32, (1, 128), 1) % slots
        down = lax.broadcasted_iota(jnp.int32, (slots, 1), 0)
        self.tile_row, self.crop_row = jnp.zeros_like(lane), jnp.zeros_like(lane)
        self.tile_col, self.crop_col = jnp.zeros_like(down), jnp.zeros_like(down)
        for slot in range(slots):
            tile, crop = slot_tile[base + slot], slot_crop[base + slot]
            self.tile_row = jnp.where(lane == slot, tile, self.tile_row)
            self.crop_row = jnp.where(lane == slot, crop, self.crop_row)
            self.tile_col = jnp.where(down == slot, tile, self.tile_col)
            self.crop_col = jnp.where(down == slot, crop, self.crop_col)
        self.same = (self.crop_col == self.crop_row[:, 0:slots]).astype(F32)


def group_total(value):
    width = CH // GROUPS
    lane = lax.broadcasted_iota(jnp.int32, (value.shape[0], 128), 1)
    parts = []
    for at in range(0, value.shape[1], 128):
        part = value[:, at : at + 128]
        step = 1
        while step < width:
            up = pltpu.roll(part, 128 - step, 1)
            down = pltpu.roll(part, step, 1)
            part = part + jnp.where((lane & step) == 0, up, down)
            step *= 2
        parts.append(part)
    return jnp.concatenate(parts, axis=1)


def crop_mean(same, value):
    count = jnp.sum(same, axis=1, keepdims=True) * float(TILE * TILE * (CH // GROUPS))
    total = lax.dot_general(same, group_total(value), NN, precision=HIGH, preferred_element_type=F32)
    return total / count


def lanes_of(width):
    return [slice(at, at + 128) for at in range(0, width, 128)]


def slab_sum(pixels, slots, width, term):
    parts = []
    for lanes in lanes_of(width):

        def step(at, total):
            return total + term(at, lanes)

        parts.append(lax.fori_loop(0, pixels, step, jnp.zeros((slots, 128), F32), unroll=8))
    return jnp.concatenate(parts, axis=1)


def slab_stats(pixels, slots, slab, same):
    mean = crop_mean(same, slab_sum(pixels, slots, CH, slab))

    def square(at, lanes):
        centred = slab(at, lanes) - mean[:, lanes]
        return centred * centred

    return mean, lax.rsqrt(crop_mean(same, slab_sum(pixels, slots, CH, square)) + EPS)


def sigmoid(value):
    return 0.5 * jnp.tanh(0.5 * value) + 0.5


def fill_halo(pad, plan):
    slots = plan.slots
    wide = TILE * slots
    tile_c = jnp.concatenate([plan.tile_col] * TILE, axis=0)
    crop_c = jnp.concatenate([plan.crop_col] * TILE, axis=0)
    tile_r = jnp.concatenate([plan.tile_row] * (wide // 128), axis=1)
    crop_r = jnp.concatenate([plan.crop_row] * (wide // 128), axis=1)
    block_c = lax.broadcasted_iota(jnp.int32, (wide, wide), 0) // slots
    block_r = lax.broadcasted_iota(jnp.int32, (wide, wide), 1) // slots
    linked = (crop_c == crop_r) & (tile_c >= 0)

    def near(row_step, col_step):
        return linked & (tile_r == tile_c + (TILE * row_step + col_step))

    def edge(row_step, col_step, source):
        pick = (near(row_step, col_step) & (block_c == block_r)).astype(F32).astype(BF16)
        moved = jnp.dot(pick, source.reshape(wide, CH), preferred_element_type=F32).astype(BF16)
        return moved.reshape(TILE, slots, CH)

    def corner(row_step, col_step, source):
        pick = near(row_step, col_step)[0:slots, 0:slots].astype(F32).astype(BF16)
        return jnp.dot(pick, source, preferred_element_type=F32).astype(BF16)

    low, high, end = 1, TILE, TILE + 1
    pad[0, low:end] = edge(-1, 0, pad[high, low:end])
    pad[end, low:end] = edge(1, 0, pad[low, low:end])
    pad[low:end, 0] = edge(0, -1, pad[low:end, high])
    pad[low:end, end] = edge(0, 1, pad[low:end, low])
    pad[0, 0] = corner(-1, -1, pad[high, high])
    pad[0, end] = corner(-1, 1, pad[high, low])
    pad[end, 0] = corner(1, -1, pad[low, high])
    pad[end, end] = corner(1, 1, pad[low, low])


class WeightLoad:
    def __init__(self, position, pieces, target, sem, columns=None):
        self.copies = []
        views = [(pieces[0], None)]
        if len(pieces) > 1:
            me, core = position[0], position[1]
            half = pieces[0].shape[1]
            views = [(pieces[0], me * half)]
            part = half // (len(pieces) - 1)
            for number, piece in enumerate(pieces[1:]):
                spot = (1 - me) * half
                if len(pieces) == 3:
                    spot = spot + (core ^ number) * part
                if len(piece.shape) == 3:
                    views.append((piece, spot))
                    continue
                for at in range(piece.shape[0]):
                    views.append((piece.at[at], spot + at * piece.shape[2]))
        for at, (piece, spot) in enumerate(views):
            width = piece.shape[1]
            rows = slice(None)
            if spot is not None:
                rows = pl.ds(pl.multiple_of(spot, 32), width)
            if columns is not None:
                piece = piece.at[:, :, columns]
            self.copies.append(pltpu.make_async_copy(piece, target.at[:, rows, :], sem.at[at]))

    def start(self):
        for copy in self.copies:
            copy.start()

    def wait(self):
        for copy in self.copies:
            copy.wait()


def weight_sems(pieces):
    return pltpu.SemaphoreType.DMA((9,))


BLOCK = CH // 16


def store_grad(grad, outs, work, position, unit, first, count, front=True):
    if len(outs) == 1:
        outs[0][unit] = grad.astype(BF16)
        return
    work[...] = grad
    me, core, quad = position[0], position[1], position[2]
    for half, out in enumerate(outs):
        for c in range(2):
            for q in range(4):
                row = (me ^ c) * (CH // 2) + (core ^ half) * (CH // 4) + (quad ^ q) * BLOCK
                part = work[pl.ds(pl.multiple_of(row, BLOCK), BLOCK), :]
                if front:
                    to = ((c * 4 + q) * first + unit) * BLOCK
                else:
                    to = (8 * first + (q * 2 + c) * (count - first) + unit - first) * BLOCK
                out[pl.ds(pl.multiple_of(to, BLOCK), BLOCK), :] = part.astype(BF16)


def store_vectors(vecs, out, me):
    if len(out.shape) == 2:
        out[...] = vecs[...]
    else:
        half = out.shape[2]
        out[0] = vecs[:, pl.ds(pl.multiple_of(me * half, half), half)]
        out[1] = vecs[:, pl.ds(pl.multiple_of((1 - me) * half, half), half)]


def vector_shape(paired):
    return shape((2, 16, CH // 2) if paired else (16, CH), F32)


def grad_shapes(count, paired):
    if paired:
        return [shape((8 * count * BLOCK, CH), BF16)] * 2
    return [shape((count, CH, CH), BF16)]


def conv_rows(pad, weight, row, slots, dims, flipped, count=1):
    total = None
    for tap in range(9):
        down, right = tap // 3, tap % 3
        if flipped:
            down, right = 2 - down, 2 - right
        left = pad[pl.ds(row + down, count), right : right + TILE].reshape(count * TILE * slots, CH)
        part = lax.dot_general(left, weight[tap], dims, preferred_element_type=F32)
        total = part if total is None else total + part
    return total


def load_full(parts, me, dtype, store):
    if len(parts) == 1:
        store(slice(None), parts[0][...].astype(dtype))
    else:
        local = parts[0].shape[-1]
        own = pl.ds(pl.multiple_of(me * local, local), local)
        other = pl.ds(pl.multiple_of((1 - me) * local, local), local)
        store(own, parts[0][...].astype(dtype))
        store(other, parts[1][...].astype(dtype))


def vmem(shape, dtype):
    return pltpu.VMEM(shape, dtype)


def specs(kinds):
    table = {
        "v": pl.BlockSpec(memory_space=pltpu.VMEM),
        "s": pl.BlockSpec(memory_space=pltpu.SMEM),
        "h": pl.BlockSpec(memory_space=pl.ANY),
    }
    return [table[k] for k in kinds]


ROOM = {
    "unpack_output": 18,
    "unpack_input_grad": 18,
    "conv2_weight_grad": 24,
    "conv1_weight_grad": 22,
    "conv2_input_grad": 24,
    "conv1_input_grad": 20,
    "conv2_grads": 16,
    "conv1_grads": 14,
}


def call(body, ins, outs, shapes, scratch, name, flops, moved):
    return pl.pallas_call(
        body,
        in_specs=specs(ins),
        out_specs=tuple(specs(outs)),
        out_shape=tuple(shapes),
        scratch_shapes=list(scratch),
        compiler_params=pltpu.CompilerParams(vmem_limit_bytes=ROOM.get(name, 60) << 20),
        cost_estimate=pl.CostEstimate(
            flops=int(flops), bytes_accessed=int(moved), transcendentals=0
        ),
        name=name,
    )


def shape(dims, dtype):
    return jax.ShapeDtypeStruct(dims, dtype)


def pack_first_kernel(devices, slots, position, ids, table, signal, *rest):
    plan, rest = rest[:4], rest[4:]
    write_plan(devices, slots, ids, table, *plan)
    pack_kernel(True, slots, position, plan[0], signal, *rest)


def pack_kernel(by_pixel, slots, position, slot_tile, signal, *rest):
    outs, (raster, stage) = rest[:-2], rest[-2:]
    local, pixels = signal.shape
    side = int(pixels**0.5)
    chunk = 512
    cols = local // 128
    for at in range(0, pixels, chunk):
        flipped = signal[:, at : at + chunk].astype(F32).T
        for col in range(cols):
            raster[col, at : at + chunk, :] = flipped[:, col * 128 : (col + 1) * 128]
    for number, out in enumerate(outs):

        def step(slot, carry):
            tile = slot_tile[pack_base(position, number, len(outs), slots) + slot]
            keep = tile >= 0
            tile = jnp.maximum(tile, 0)
            start = (tile // TILE) * (TILE * side) + (tile % TILE) * TILE
            for row in range(TILE):
                for col in range(cols):
                    value = raster[col, pl.ds(pl.multiple_of(start + row * side, TILE), TILE), :]
                    value = jnp.where(keep, value, 0.0)
                    if by_pixel:
                        pitch = slots + PITCH
                        to = pl.ds(row * TILE * pitch + slot, TILE, stride=pitch)
                        stage[col, to, :] = value
                    else:
                        at = pl.multiple_of(slot * (TILE * TILE) + row * TILE, TILE)
                        stage[col, pl.ds(at, TILE), :] = value
            return carry

        lax.fori_loop(0, slots, step, 0)
        size = slots if by_pixel else TILE * TILE
        pitch = size + PITCH if by_pixel else size
        for number in range(out.shape[0] // size):
            for col in range(cols):
                span = slice(col * 128, (col + 1) * 128)
                value = stage[col, number * pitch : number * pitch + size, :]
                out[number * size : (number + 1) * size, span] = value.astype(BF16)


def pack_base(position, number, devices, slots):
    return (position[0] ^ number if devices == 2 else number) * slots


def pack_scratch(local, pixels, slots):
    rows = TILE * TILE * (slots + PITCH)
    return [vmem((local // 128, pixels, 128), F32), vmem((local // 128, rows, 128), F32)]


def pack_first(position, ids, signal, devices, slots, name):
    local, pixels = signal.shape
    rows = slots * TILE * TILE
    table = jnp.asarray(packed_tables(devices, ids.shape[0] // TILE, slots))
    result = call(
        functools.partial(pack_first_kernel, devices, slots),
        "sssv",
        "ssss" + "v" * devices,
        [shape((devices * slots,), jnp.int32)] * 2
        + [shape((CROPS,), jnp.int32)] * 2
        + [shape((rows, local), BF16)] * devices,
        pack_scratch(local, pixels, slots),
        name,
        4 << 30,
        6 << 20,
    )(position, ids, table, signal)
    return result[:4], result[4:]


def pack(position, slot_tile, signal, by_pixel, devices, slots, name):
    local, pixels = signal.shape
    rows = slots * TILE * TILE
    return call(
        functools.partial(pack_kernel, by_pixel, slots),
        "ssv",
        "v" * devices,
        [shape((rows, local), BF16)] * devices,
        pack_scratch(local, pixels, slots),
        name,
        40 << 30,
        6 << 20,
    )(position, slot_tile, signal)


def unpack_kernel(by_pixel, slots, position, slot_tile, *rest):
    ins, out, (raster, stage) = rest[:-3], rest[-3], rest[-2:]
    local, pixels = out.shape
    side = int(pixels**0.5)
    chunk = 512
    cols = local // 128
    for number, part in enumerate(ins):
        size = slots if by_pixel else TILE * TILE
        pitch = size + PITCH if by_pixel else size
        for at in range(part.shape[0] // size):
            for col in range(cols):
                span = slice(col * 128, (col + 1) * 128)
                value = part[at * size : (at + 1) * size, span]
                stage[col, at * pitch : at * pitch + size, :] = value.astype(F32)

        def step(slot, carry):
            tile = slot_tile[pack_base(position, number, len(ins), slots) + slot]

            @pl.when(tile >= 0)
            def _():
                start = (tile // TILE) * (TILE * side) + (tile % TILE) * TILE
                for row in range(TILE):
                    to = pl.ds(pl.multiple_of(start + row * side, TILE), TILE)
                    for col in range(cols):
                        if by_pixel:
                            at = pl.ds(row * TILE * pitch + slot, TILE, stride=pitch)
                        else:
                            first = pl.multiple_of(slot * (TILE * TILE) + row * TILE, TILE)
                            at = pl.ds(first, TILE)
                        raster[col, to, :] = stage[col, at, :]

            return carry

        lax.fori_loop(0, slots, step, 0)
    for at in range(0, pixels, chunk):
        for col in range(cols):
            span = slice(col * 128, (col + 1) * 128)
            out[span, at : at + chunk] = raster[col, at : at + chunk, :].T.astype(out.dtype)


def unpack(position, slot_tile, parts, pixels, by_pixel, dtype, slots, name):
    rows, local = parts[0].shape
    return call(
        functools.partial(unpack_kernel, by_pixel, slots),
        "ss" + "v" * len(parts),
        "v",
        [shape((local, pixels), dtype)],
        pack_scratch(local, pixels, slots),
        name,
        4 << 30,
        8 << 20,
    )(position, slot_tile, *parts)[0]


(G1, B1, C1, G2, B2, C2, G3, B3, QB, VB, PB) = range(11)


def norm_swish_pad(slab, mean, inverse, gain, bias, pad, copy=None):
    scaled = inverse * gain
    for lanes in lanes_of(CH):
        centre, factor, offset = mean[:, lanes], scaled[:, lanes], bias[:, lanes]

        def step(row, carry):
            for col in range(TILE):
                value = slab(row * TILE + col, lanes)
                before = (value - centre) * factor + offset
                pad[row + 1, col + 1, :, lanes] = (before * sigmoid(before)).astype(BF16)
                if copy is not None:
                    copy[row * TILE + col, :, lanes] = value.astype(BF16)
            return carry

        lax.fori_loop(0, TILE, step, 0)


def first_kernel(parts, count, position, slot_tile, slot_crop, *rest):
    feature_parts, rest = rest[:parts], rest[parts:]
    par_parts, rest = rest[:parts], rest[parts:]
    pieces, rest = rest[:count], rest[count:]
    (par, feats_hbm, pad1_hbm, hidden_hbm, pad2_hbm, stats1, stats2) = rest[:7]
    feats, rounded, hidden, pad1, pad2, weight, weight_sem, sem = rest[7:]
    pixels, slots, _ = hidden.shape
    load_weight = WeightLoad(position, pieces, weight, weight_sem)
    load_weight.start()

    def put_par(columns, value):
        par[:, columns] = value

    load_full(par_parts, position[0], F32, put_par)

    def put(columns, value):
        feats[:, columns] = value

    load_full(feature_parts, position[0], BF16, put)
    save_feats = pltpu.make_async_copy(feats, feats_hbm, sem.at[1])
    save_feats.start()

    plan = Plan(position[0], slot_tile, slot_crop, slots)

    def slab1(at, lanes):
        return feats[pl.ds(pl.multiple_of(at * slots, slots), slots), lanes].astype(F32)

    mean, inverse = slab_stats(pixels, slots, slab1, plan.same)
    stats1[0], stats1[1] = mean, inverse
    norm_swish_pad(slab1, mean, inverse, par[G1 : G1 + 1, :], par[B1 : B1 + 1, :], pad1)
    fill_halo(pad1, plan)
    save_pad1 = pltpu.make_async_copy(pad1, pad1_hbm, sem.at[2])
    save_pad1.start()
    load_weight.wait()

    def step(row, carry):
        total = conv_rows(pad1, weight, row, slots, NT, False) + par[C1 : C1 + 1, :]
        hidden[pl.ds(row * TILE, TILE)] = total.reshape(TILE, slots, CH)
        return carry

    lax.fori_loop(0, TILE, step, 0)

    def slab2(at, lanes):
        return hidden[at, :, lanes]

    mean, inverse = slab_stats(pixels, slots, slab2, plan.same)
    stats2[0], stats2[1] = mean, inverse
    norm_swish_pad(
        slab2, mean, inverse, par[G2 : G2 + 1, :], par[B2 : B2 + 1, :], pad2, rounded
    )
    save_hidden = pltpu.make_async_copy(rounded, hidden_hbm, sem.at[3])
    save_hidden.start()
    fill_halo(pad2, plan)
    save_pad2 = pltpu.make_async_copy(pad2, pad2_hbm, sem.at[4])
    save_pad2.start()
    save_feats.wait()
    save_pad1.wait()
    save_hidden.wait()
    save_pad2.wait()


def first(position, tables, par_parts, parts, weight, slots):
    pixels = TILE * TILE
    rows = pixels * slots
    pad = (TILE + 2, TILE + 2, slots, CH)
    return call(
        functools.partial(first_kernel, len(parts), len(weight)),
        "sss" + "v" * len(parts) + "v" * len(parts) + "h" * len(weight),
        "vhhhhvv",
        [
            shape((16, CH), F32),
            shape((rows, CH), BF16),
            shape(pad, BF16),
            shape((pixels, slots, CH), BF16),
            shape(pad, BF16),
            shape((2, slots, CH), F32),
            shape((2, slots, CH), F32),
        ],
        [
            vmem((rows, CH), BF16),
            vmem((pixels, slots, CH), BF16),
            vmem((pixels, slots, CH), F32),
            vmem(pad, BF16),
            vmem(pad, BF16),
            vmem((9, CH, CH), BF16),
            weight_sems(weight),
            pltpu.SemaphoreType.DMA((5,)),
        ],
        "conv1_forward",
        2 * rows * CH * CH * 9,
        20 << 20,
    )(position, *tables[:2], *parts, *par_parts, *weight)


def second_kernel(count, position, slot_tile, slot_crop, par, feats, pad_hbm, *rest):
    pieces, rest = rest[:count], rest[count:]
    resid_hbm, normed_hbm, stats3 = rest[:3]
    resid, resid_tile, normed, pad, weight, rows_scr, weight_sem, sem = rest[3:]
    slots = pad.shape[2]
    pixels = TILE * TILE
    load_pad = pltpu.make_async_copy(pad_hbm, pad, sem.at[0])
    load_weight = WeightLoad(position, pieces, weight, weight_sem)
    load_pad.start()
    load_weight.start()
    plan = Plan(position[0], slot_tile, slot_crop, slots)
    same = plan.same
    load_pad.wait()
    load_weight.wait()
    wide = TILE * slots

    def step(row, carry):
        at = pl.ds(pl.multiple_of(row * wide, wide), wide)
        total = conv_rows(pad, weight, row, slots, NT, False) + par[C2 : C2 + 1, :]
        total = total + feats[at, :].astype(F32)
        for col in range(CH // 128):
            for x in range(TILE):
                to = pl.multiple_of((row * TILE + x) * (slots + PITCH), 8)
                part = total[x * slots : (x + 1) * slots, col * 128 : (col + 1) * 128]
                resid[col, pl.ds(to, slots), :] = part
        return carry

    lax.fori_loop(0, TILE, step, 0)

    def slab(at, lanes):
        begin = pl.multiple_of(at * (slots + PITCH), 8)
        return resid[lanes.start // 128, pl.ds(begin, slots), :]

    mean, inverse = slab_stats(pixels, slots, slab, same)
    stats3[0], stats3[1] = mean, inverse
    rows_scr[0], rows_scr[1] = mean, inverse * par[G3 : G3 + 1, :]
    bias = par[B3 : B3 + 1, :]

    def tile_step(slot, carry):
        at = pl.ds(pl.multiple_of(slot * pixels, pixels), pixels)
        centre, factor = rows_scr[0, pl.ds(slot, 1)], rows_scr[1, pl.ds(slot, 1)]
        for col, lanes in enumerate(lanes_of(CH)):
            value = resid[col, pl.ds(slot, pixels, stride=slots + PITCH), :]
            resid_tile[at, lanes] = value.astype(BF16)
            scaled = (value - centre[:, lanes]) * factor[:, lanes]
            normed[at, lanes] = (scaled + bias[:, lanes]).astype(BF16)
        return carry

    lax.fori_loop(0, slots, tile_step, 0, unroll=2)
    save_resid = pltpu.make_async_copy(resid_tile, resid_hbm, sem.at[2])
    save_normed = pltpu.make_async_copy(normed, normed_hbm, sem.at[3])
    save_resid.start()
    save_normed.start()
    save_resid.wait()
    save_normed.wait()


def second(position, tables, par, feats, pad, weight, slots):
    pixels = TILE * TILE
    rows = pixels * slots
    return call(
        functools.partial(second_kernel, len(weight)),
        "sssvvh" + "h" * len(weight),
        "hhv",
        [shape((rows, CH), BF16), shape((rows, CH), BF16), shape((2, slots, CH), F32)],
        [
            vmem((CH // 128, pixels * (slots + PITCH), 128), F32),
            vmem((rows, CH), BF16),
            vmem((rows, CH), BF16),
            vmem(pad.shape, BF16),
            vmem((9, CH, CH), BF16),
            vmem((2, slots, CH), F32),
            weight_sems(weight),
            pltpu.SemaphoreType.DMA((4,)),
        ],
        "conv2_forward",
        2 * rows * CH * CH * 9,
        16 << 20,
    )(position, *tables[:2], par, feats, pad, *weight)


def attention_kernel(parts, outs, count, position, slot_tile, slot_crop, starts, ends, *rest):
    par, normed, resid_hbm, stats3 = rest[:4]
    tangent_parts, rest = rest[4 : 4 + parts], rest[4 + parts :]
    pieces, rest = rest[:count], rest[count:]
    out_hbm, rest = rest[:outs], rest[outs:]
    grads_hbm, rest = rest[:outs], rest[outs:]
    vecs_out, pad = rest[:2]
    (tangent, query, key, value, mixed_grad, mixed, query_grad, key_grad, value_grad) = rest[2:11]
    normed_grad, by_tile, rows_scr, weight, key_crop, work, vecs = rest[11:18]
    scores_scr, prob_grads, sums, weight_sem, sem, resid = rest[18:24]
    grad_outs = rest[24:]
    load_weight = WeightLoad(position, pieces, weight, weight_sem)
    load_weight.start()
    wq, wk, wv, wp = (weight.at[k] for k in range(4))
    rows = normed.shape[0]
    pixels = TILE * TILE
    slots = rows // pixels
    me = position[0]
    base = me * slots
    per_block = QUERIES
    block = per_block * pixels
    plan = Plan(me, slot_tile, slot_crop, slots)
    lane_slot = lax.broadcasted_iota(jnp.int32, (1, rows), 1) // pixels
    crops = jnp.zeros((1, rows), jnp.int32)
    for slot in range(slots):
        crops = jnp.where(lane_slot == slot, slot_crop[base + slot], crops)
    key_crop[...] = crops

    half = CH // outs
    columns = [pl.ds(0, CH)]
    if outs == 2:
        columns = [pl.ds(pl.multiple_of((me ^ k) * half, half), half) for k in range(2)]
    load_tangent = [
        pltpu.make_async_copy(part, tangent.at[:, columns[k]], sem.at[k])
        for k, part in enumerate(tangent_parts)
    ]
    load_resid = pltpu.make_async_copy(resid_hbm, resid, sem.at[2])
    save_out = [
        pltpu.make_async_copy(query.at[:, columns[k]], part, sem.at[3 + k])
        for k, part in enumerate(out_hbm)
    ]
    save_grads = [
        pltpu.make_async_copy(part, grads_hbm[k], sem.at[5 + k])
        for k, part in enumerate(grad_outs)
    ]
    for copy in load_tangent + [load_resid]:
        copy.start()
    load_weight.wait()
    for copy in load_tangent:
        copy.wait()

    def project(at, carry):
        span = pl.ds(pl.multiple_of(at * block, block), block)
        left = normed[span, :]
        total = lax.dot_general(left, wq[...], NT, preferred_element_type=F32)
        query[span, :] = (total + par[QB : QB + 1, :]).astype(BF16)
        key[span, :] = lax.dot_general(left, wk[...], NT, preferred_element_type=F32).astype(BF16)
        total = lax.dot_general(left, wv[...], NT, preferred_element_type=F32)
        value[span, :] = (total + par[VB : VB + 1, :]).astype(BF16)
        mixed_grad[span, :] = jnp.dot(
            tangent[span, :], wp[...], preferred_element_type=F32
        ).astype(BF16)
        key_grad[span, :] = jnp.zeros((block, CH), F32)
        value_grad[span, :] = jnp.zeros((block, CH), F32)
        return carry

    lax.fori_loop(0, rows // block, project, 0)

    def attend_step(at, carry):
        span = pl.ds(pl.multiple_of(at * block, block), block)
        low_crop = slot_crop[base + at * per_block]
        high_crop = slot_crop[base + at * per_block + per_block - 1]
        low = starts[jnp.maximum(low_crop, 0)] - base
        low = jnp.where(low_crop < 0, at * per_block, low) // 2 * 2
        high = jnp.where(high_crop < 0, slots, ends[jnp.maximum(high_crop, 0)] - base)
        count = (high - low + KEYS - 1) // KEYS
        begin = jnp.minimum(low, slots - KEYS * count) * pixels
        down = lax.broadcasted_iota(jnp.int32, (block, 1), 0) // pixels
        own_crop = jnp.zeros((block, 1), jnp.int32)
        for slot in range(per_block):
            own_crop = jnp.where(down == slot, slot_crop[base + at * per_block + slot], own_crop)

        def keys_of(number):
            return pl.ds(pl.multiple_of(begin + number * (KEYS * pixels), 128), KEYS * pixels)

        def score(number, top):
            keys = keys_of(number)
            scores = lax.dot_general(
                query[span, :], key[keys, :], NT, preferred_element_type=F32
            )
            scores = jnp.where(own_crop == key_crop[:, keys], scores * SCALE, -1e30)
            scores_scr[number] = scores
            prob_grads[number] = lax.dot_general(
                mixed_grad[span, :], value[keys, :], NT, preferred_element_type=F32
            )
            return jnp.maximum(top, jnp.max(scores, axis=1, keepdims=True))

        top = lax.fori_loop(0, count, score, jnp.full((block, 1), -1e30, F32))

        def weigh(number, carry):
            total, inner = carry
            exponent = jnp.exp(scores_scr[number] - top)
            scores_scr[number] = exponent
            total += jnp.sum(exponent, axis=1, keepdims=True)
            inner += jnp.sum(exponent * prob_grads[number], axis=1, keepdims=True)
            return total, inner

        zero = jnp.zeros((block, 1), F32)
        total, inner = lax.fori_loop(0, count, weigh, (zero, zero))
        share = 1.0 / total
        inner = inner * share
        sums[...] = jnp.zeros_like(sums)

        def spread_back(number, carry):
            keys = keys_of(number)
            prob = scores_scr[number] * share
            rounded = prob.astype(BF16)
            score_grad = (prob * (prob_grads[number] - inner)).astype(BF16)
            sums[0] += jnp.dot(rounded, value[keys, :], preferred_element_type=F32)
            sums[1] += jnp.dot(score_grad, key[keys, :], preferred_element_type=F32)
            key_grad[keys, :] += lax.dot_general(
                score_grad, query[span, :], TN, preferred_element_type=F32
            )
            value_grad[keys, :] += lax.dot_general(
                rounded, mixed_grad[span, :], TN, preferred_element_type=F32
            )
            return carry

        lax.fori_loop(0, count, spread_back, 0)
        mixed[span, :] = sums[0].astype(BF16)
        query_grad[span, :] = (sums[1] * SCALE).astype(BF16)
        return carry

    lax.fori_loop(0, rows // block, attend_step, 0)

    def back(at, carry):
        query_bias, value_bias, tangent_sum = carry
        span = pl.ds(pl.multiple_of(at * block, block), block)
        dq = query_grad[span, :]
        dk = (key_grad[span, :] * SCALE).astype(BF16)
        dv = value_grad[span, :].astype(BF16)
        key[span, :] = dk
        value[span, :] = dv
        total = jnp.dot(dq, wq[...], preferred_element_type=F32)
        total += jnp.dot(dk, wk[...], preferred_element_type=F32)
        total += jnp.dot(dv, wv[...], preferred_element_type=F32)
        normed_grad[span, :] = total
        result = lax.dot_general(mixed[span, :], wp[...], NT, preferred_element_type=F32)
        result = (result + par[PB : PB + 1, :] + resid[span, :].astype(F32)).astype(BF16)
        query[span, :] = result
        query_bias += jnp.sum(dq.astype(F32), axis=0, keepdims=True)
        value_bias += jnp.sum(dv.astype(F32), axis=0, keepdims=True)
        tangent_sum += jnp.sum(tangent[span, :].astype(F32), axis=0, keepdims=True)
        return query_bias, value_bias, tangent_sum

    load_resid.wait()
    zero = jnp.zeros((1, CH), F32)
    query_bias, value_bias, tangent_sum = lax.fori_loop(
        0, rows // block, back, (zero, zero, zero)
    )
    for copy in save_out:
        copy.start()
    left = normed[...]
    for number, grad in enumerate((query_grad, key, value)):
        total = lax.dot_general(grad[...], left, TN, preferred_element_type=F32)
        store_grad(total, grad_outs, work, position, number, 4, 4)
    total = lax.dot_general(tangent[...], mixed[...], TN, preferred_element_type=F32)
    store_grad(total, grad_outs, work, position, 3, 4, 4)
    for copy in save_grads:
        copy.start()

    def tile_sums(slot, carry):
        span = pl.ds(pl.multiple_of(slot * pixels, pixels), pixels)
        row = pl.ds(slot, 1)
        centre, factor = stats3[0, row], stats3[1, row]
        plains, crosseds = [], []
        for lanes in lanes_of(CH):
            upstream = normed_grad[span, lanes]
            hat = (resid[span, lanes].astype(F32) - centre[:, lanes]) * factor[:, lanes]
            plains.append(jnp.sum(upstream, axis=0, keepdims=True))
            crosseds.append(jnp.sum(upstream * hat, axis=0, keepdims=True))
        rows_scr[0, row] = jnp.concatenate(plains, axis=1)
        rows_scr[1, row] = jnp.concatenate(crosseds, axis=1)
        return carry

    lax.fori_loop(0, slots, tile_sums, 0)
    same = plan.same
    gain = par[G3 : G3 + 1, :]
    plain, crossed = rows_scr[0], rows_scr[1]
    vecs[...] = jnp.zeros_like(vecs)
    vecs[G3 : G3 + 1, :] = jnp.sum(crossed, axis=0, keepdims=True)
    vecs[B3 : B3 + 1, :] = jnp.sum(plain, axis=0, keepdims=True)
    vecs[QB : QB + 1, :] = query_bias
    vecs[VB : VB + 1, :] = value_bias
    vecs[PB : PB + 1, :] = tangent_sum
    rows_scr[0] = crop_mean(same, plain * gain)
    rows_scr[1] = crop_mean(same, crossed * gain)

    def apply(slot, carry):
        span = pl.ds(pl.multiple_of(slot * pixels, pixels), pixels)
        padded = pl.ds(pl.multiple_of(slot * (pixels + PITCH), 8), pixels)
        row = pl.ds(slot, 1)
        centre, factor = stats3[0, row], stats3[1, row]
        slope = factor * gain
        level = factor * rows_scr[0, row]
        tilt = factor * factor * rows_scr[1, row]
        for col, lanes in enumerate(lanes_of(CH)):
            centred = resid[span, lanes].astype(F32) - centre[:, lanes]
            grad = normed_grad[span, lanes] * slope[:, lanes] - level[:, lanes]
            grad = grad - centred * tilt[:, lanes]
            by_tile[col, padded, :] = tangent[span, lanes].astype(F32) + grad
        return carry

    lax.fori_loop(0, slots, apply, 0)

    def spread(row, carry):
        total = carry
        for col in range(TILE):
            at = row * TILE + col
            slab = jnp.concatenate(
                [
                    by_tile[c, pl.ds(at, slots, stride=pixels + PITCH), :] for c in range(CH // 128)
                ],
                axis=1,
            )
            rounded = slab.astype(BF16)
            pad[row + 1, col + 1] = rounded
            total += jnp.sum(rounded.astype(F32), axis=0, keepdims=True)
        return total

    vecs[C2 : C2 + 1, :] = lax.fori_loop(0, TILE, spread, zero)
    store_vectors(vecs, vecs_out, me)
    fill_halo(pad, plan)
    for copy in save_out + save_grads:
        copy.wait()


def attention(position, tables, par, normed, resid, stats3, tangent_parts, weight, slots):
    pixels = TILE * TILE
    rows = pixels * slots
    parts = len(tangent_parts)
    pad = (TILE + 2, TILE + 2, slots, CH)
    if parts == 2:
        out_shapes = [shape((rows, CH // 2), BF16)] * 2
    else:
        out_shapes = [shape((rows, CH), BF16)]
    outs = len(out_shapes)
    result = call(
        functools.partial(attention_kernel, parts, outs, len(weight)),
        "sssssvvhv" + "h" * parts + "h" * len(weight),
        "h" * (2 * outs) + "vv",
        out_shapes
        + grad_shapes(4, outs == 2)
        + [vector_shape(outs == 2), shape(pad, BF16)],
        [vmem((rows, CH), BF16)] * 7
        + [vmem((rows, CH), F32)] * 3
        + [vmem((CH // 128, slots * (pixels + PITCH), 128), F32), vmem((2, slots, CH), F32)]
        + [vmem((4, CH, CH), BF16), vmem((1, rows), jnp.int32), vmem((CH, CH), F32)]
        + [vmem((16, CH), F32)]
        + [vmem((slots // KEYS, QUERIES * pixels, KEYS * pixels), F32)] * 2
        + [vmem((2, QUERIES * pixels, CH), F32)]
        + [weight_sems(weight), pltpu.SemaphoreType.DMA((7,)), vmem((rows, CH), BF16)]
        + [vmem(part.shape, BF16) for part in grad_shapes(4, outs == 2)],
        "attention",
        30 << 30,
        24 << 20,
    )(
        position,
        *tables,
        par,
        normed,
        resid,
        stats3,
        *tangent_parts,
        *weight,
    )
    return result[:outs], result[outs : 2 * outs], result[2 * outs :]


def weight_grad_kernel(paired, first, extra, position, active, grad, *rest):
    outs = 2 if paired else 1
    extras, rest = rest[: outs if extra else 0], rest[outs if extra else 0 :]
    out_parts, (flipped, work, sem) = rest[:outs], rest[outs:]
    copies = []
    for half, part in enumerate(extras):
        for at in range(8):
            source = part.at[pl.ds(at * extra * BLOCK, extra * BLOCK)]
            target = out_parts[half].at[pl.ds(at * first * BLOCK, extra * BLOCK)]
            copies.append(pltpu.make_async_copy(source, target, sem.at[half, at]))
    for copy in copies:
        copy.start()
    slots = active.shape[2]
    wide = TILE * slots
    for row in range(TILE):
        left = grad[row + 1, 1 : TILE + 1].reshape(wide, CH)
        flipped[:, row * wide : (row + 1) * wide] = left.T

    def step(front, tap, carry):
        right = active[pl.ds(tap // 3, TILE), pl.ds(tap % 3, TILE)].reshape(TILE * wide, CH)
        total = jnp.dot(flipped[...], right, preferred_element_type=F32)
        store_grad(total, out_parts, work, position, tap + extra, first, 9 + extra, front)
        return carry

    if first > extra:
        lax.fori_loop(0, first - extra, functools.partial(step, True), 0)
    if first - extra < 9:
        lax.fori_loop(first - extra, 9, functools.partial(step, False), 0)
    for copy in copies:
        copy.wait()


def weight_grad(position, active, grad, paired, slots, name, first=9, extras=()):
    rows = TILE * TILE * slots
    extra = 4 if extras else 0
    shapes = grad_shapes(9 + extra, paired)
    return call(
        functools.partial(weight_grad_kernel, paired, first, extra),
        "svv" + "h" * len(extras),
        "v" * len(shapes),
        shapes,
        [
            vmem((CH, rows), BF16),
            vmem((CH, CH), F32),
            pltpu.SemaphoreType.DMA((2, 8)),
        ],
        name,
        2 * rows * CH * CH * 9,
        12 << 20,
    )(position, active, grad, *extras)


def swish_back(upstream, before):
    gate = sigmoid(before)
    return upstream * (gate + before * gate * (1.0 - gate))


def norm_back_sums(source, upstream, mean, inverse, gain, bias, slots):
    plains, crosseds = [], []
    for lanes in lanes_of(upstream.shape[2]):
        centre, factor = mean[:, lanes], inverse[:, lanes]
        slope, offset = gain[:, lanes], bias[:, lanes]

        def step(at, carry):
            plain, crossed = carry
            hat = (source(at, lanes) - centre) * factor
            grad = swish_back(upstream[at, :, lanes], hat * slope + offset)
            upstream[at, :, lanes] = grad
            return plain + grad, crossed + grad * hat

        zero = jnp.zeros((slots, 128), F32)
        plain, crossed = lax.fori_loop(0, TILE * TILE, step, (zero, zero), unroll=4)
        plains.append(plain)
        crosseds.append(crossed)
    return jnp.concatenate(plains, axis=1), jnp.concatenate(crosseds, axis=1)


def norm_back_apply(source, upstream, mean, inverse, gain, plain, crossed, put):
    for lanes in lanes_of(upstream.shape[2]):
        centre, factor = mean[:, lanes], inverse[:, lanes]
        slope = factor * gain[:, lanes]
        level = factor * plain[:, lanes]
        tilt = factor * factor * crossed[:, lanes]

        def step(at, carry):
            centred = source(at, lanes) - centre
            put(at, lanes, upstream[at, :, lanes] * slope - level - centred * tilt)
            return carry

        lax.fori_loop(0, TILE * TILE, step, 0, unroll=8)


def middle_kernel(count, position, slot_tile, slot_crop, par, stats2, pad_hbm, hidden_hbm, *rest):
    pieces, rest = rest[:count], rest[count:]
    pad_out_hbm, vecs_out = rest[:2]
    pad, weight, hidden, upstream, pad_out, vecs, totals, weight_sem, sem = rest[2:]
    slots = pad.shape[2]
    load_pad = pltpu.make_async_copy(pad_hbm, pad, sem.at[0])
    load_weight = WeightLoad(position, pieces, weight, weight_sem)
    load_hidden = pltpu.make_async_copy(hidden_hbm, hidden, sem.at[2])
    load_pad.start()
    load_weight.start()
    load_hidden.start()
    plan = Plan(position[0], slot_tile, slot_crop, slots)
    same = plan.same
    load_pad.wait()
    load_weight.wait()

    def step(row, carry):
        total = conv_rows(pad, weight, row, slots, NN, True)
        upstream[pl.ds(row * TILE, TILE)] = total.reshape(TILE, slots, CH)
        return carry

    lax.fori_loop(0, TILE, step, 0)
    load_hidden.wait()
    mean, inverse = stats2[0], stats2[1]
    gain, bias = par[G2 : G2 + 1, :], par[B2 : B2 + 1, :]

    def source(at, lanes):
        return hidden[at, :, lanes].astype(F32)

    plain, crossed = norm_back_sums(
        source, upstream, mean, inverse, gain, bias, slots
    )
    vecs[...] = jnp.zeros_like(vecs)
    vecs[G2 : G2 + 1, :] = jnp.sum(crossed, axis=0, keepdims=True)
    vecs[B2 : B2 + 1, :] = jnp.sum(plain, axis=0, keepdims=True)
    plain = crop_mean(same, plain * gain)
    crossed = crop_mean(same, crossed * gain)

    totals[...] = jnp.zeros_like(totals)

    def put(at, lanes, grad):
        rounded = grad.astype(BF16)
        pad_out[at // TILE + 1, at % TILE + 1, :, lanes] = rounded
        totals[:, lanes] += rounded.astype(F32)

    norm_back_apply(source, upstream, mean, inverse, gain, plain, crossed, put)
    vecs[C1 : C1 + 1, :] = jnp.sum(totals[...], axis=0, keepdims=True)
    store_vectors(vecs, vecs_out, position[0])
    fill_halo(pad_out, plan)
    save = pltpu.make_async_copy(pad_out, pad_out_hbm, sem.at[3])
    save.start()
    save.wait()


def middle(position, tables, par, stats2, pad, weight, hidden, slots):
    pixels = TILE * TILE
    rows = pixels * slots
    return call(
        functools.partial(middle_kernel, len(weight)),
        "sssvvhh" + "h" * len(weight),
        "hv",
        [shape(pad.shape, BF16), vector_shape(len(weight) > 1)],
        [
            vmem(pad.shape, BF16),
            vmem((9, CH, CH), BF16),
            vmem((pixels, slots, CH), BF16),
            vmem((pixels, slots, CH), F32),
            vmem(pad.shape, BF16),
            vmem((16, CH), F32),
            vmem((slots, CH), F32),
            weight_sems(weight),
            pltpu.SemaphoreType.DMA((4,)),
        ],
        "conv2_input_grad",
        2 * rows * CH * CH * 9,
        16 << 20,
    )(position, *tables[:2], par, stats2, pad, hidden, *weight)


def last_kernel(
    whose, count, position, slot_tile, slot_crop, par, stats1, vecs2, vecs3, *rest
):
    feats_hbm, pad_hbm, resid_hbm = rest[:3]
    pieces, rest = rest[3 : 3 + count], rest[3 + count :]
    out, vecs, pad, weight, feats, resid, upstream, weight_sem, sem = rest
    slots = pad.shape[2]
    width = upstream.shape[2]
    pixels = TILE * TILE
    me = position[0]
    columns = None
    span = pl.ds(0, width)
    if width < CH:
        columns = span = pl.ds(pl.multiple_of((me ^ whose) * width, width), width)
    load_weight = WeightLoad(position, pieces, weight, weight_sem, columns)
    load_pad = pltpu.make_async_copy(pad_hbm, pad, sem.at[0])
    inner = pl.ds(1, TILE)
    load_resid = pltpu.make_async_copy(resid_hbm.at[inner, inner, :, span], resid, sem.at[1])
    load_feats = pltpu.make_async_copy(feats_hbm.at[:, span], feats, sem.at[2])
    load_pad.start()
    load_weight.start()
    load_feats.start()
    load_resid.start()
    plan = Plan(me, slot_tile, slot_crop, slots)
    same = plan.same
    load_pad.wait()
    load_weight.wait()

    def step(row, carry):
        total = conv_rows(pad, weight, row, slots, NN, True)
        upstream[pl.ds(row * TILE, TILE)] = total.reshape(TILE, slots, width)
        return carry

    lax.fori_loop(0, TILE, step, 0)
    load_feats.wait()
    load_resid.wait()
    mean, inverse = stats1[0, :, span], stats1[1, :, span]
    gain, bias = par[G1 : G1 + 1, span], par[B1 : B1 + 1, span]

    def source(at, lanes):
        return feats[pl.ds(pl.multiple_of(at * slots, slots), slots), lanes].astype(F32)

    plain, crossed = norm_back_sums(source, upstream, mean, inverse, gain, bias, slots)
    vecs[...] = vecs2[...] + vecs3[...] if width == CH else vecs2[whose] + vecs3[whose]
    vecs[G1 : G1 + 1, :] = jnp.sum(crossed, axis=0, keepdims=True)
    vecs[B1 : B1 + 1, :] = jnp.sum(plain, axis=0, keepdims=True)
    plain = crop_mean(same, plain * gain)
    crossed = crop_mean(same, crossed * gain)

    def put(at, lanes, grad):
        rows = pl.ds(pl.multiple_of(at * slots, slots), slots)
        grad = resid[at // TILE, at % TILE, :, lanes].astype(F32) + grad
        out[rows, lanes] = grad.astype(out.dtype)

    norm_back_apply(source, upstream, mean, inverse, gain, plain, crossed, put)


def last(position, tables, par, stats1, vecs, feats, pad, weight, resid_grad, whose, slots):
    pixels = TILE * TILE
    rows = pixels * slots
    width = CH // 2 if len(weight) > 1 else CH
    return call(
        functools.partial(last_kernel, whose, len(weight)),
        "sssvvvvhhh" + "h" * len(weight),
        "vv",
        [
            shape((rows, width), F32 if width < CH and whose == 0 else BF16),
            shape((16, width), F32),
        ],
        [
            vmem(pad.shape, BF16),
            vmem((9, CH, width), BF16),
            vmem((rows, width), BF16),
            vmem((TILE, TILE, slots, width), BF16),
            vmem((pixels, slots, width), F32),
            weight_sems(weight),
            pltpu.SemaphoreType.DMA((3,)),
        ],
        "conv1_input_grad",
        2 * rows * CH * width * 9,
        10 << 20,
    )(position, *tables[:2], par, stats1, *vecs, feats, pad, resid_grad, *weight)


def after(value, *others):
    flat, tree = jax.tree.flatten(value)
    extra = jax.tree.leaves(others)
    held = lax.optimization_barrier(tuple(flat) + tuple(extra))
    return jax.tree.unflatten(tree, list(held[: len(flat)]))


def add(*terms):
    total = terms[0].astype(F32)
    for term in terms[1:]:
        total = total + term.astype(F32)
    return total


def swap(value, axis):
    return lax.ppermute(value, axis, [(0, 1), (1, 0)])


def to_all(value, axes, count):
    return lax.all_to_all(jnp.broadcast_to(value[None], (count,) + value.shape), axes, 0, 0)


QUAD = ("y", "near")


def from_quad(values):
    return [
        lax.ppermute(value, ("near", "y"), [(at, at ^ bits) for at in range(4)])
        for bits, value in zip((2, 1, 3), values)
    ]


def rounded_sum(terms):
    total = terms[0].astype(F32)
    for term in terms[1:]:
        total = total + term.astype(F32)
    return total.astype(BF16)


def vector_rows(vectors):
    rows, width = vectors.shape
    return jnp.pad(vectors.astype(BF16), ((0, BLOCK - rows), (0, CH - width)))


class Reduction:
    def __init__(self, halves, first, count):
        self.stage, self.first, self.count = 0, first, count
        self.state = (halves[0], halves[1], swap(halves[1], "core"))

    def advance(self, *others, vectors=None):
        if others:
            self.state = after(self.state, *others)
        self.stage += 1
        front = self.first * BLOCK
        back = (self.count - self.first) * BLOCK
        state = self.state
        if self.stage == 1:
            mine, _, came = state

            def part(begin, size):
                span = slice(begin, begin + size)
                return rounded_sum([mine[span], came[span]])

            start = 8 * front
            keep = part(0, 4 * front) if front else None, part(start, 2 * back)
            sent_front = part(4 * front, 4 * front) if front else None
            sent_back = [part(start + q * 2 * back, 2 * back) for q in (1, 2, 3)]
            came_front = swap(sent_front, "chan") if front else None
            self.state = keep, (came_front, from_quad(sent_back))
            return sent_front, sent_back
        if self.stage == 2:
            (mine_front, mine_back), (came_front, came_back) = state
            piece = [slice(q * front, (q + 1) * front) for q in range(4)]
            sent_front, keep_front = [], None
            if front:
                terms = [[mine_front[span], came_front[span]] for span in piece]
                keep_front, sent_front = terms[0], [rounded_sum(term) for term in terms[1:]]
            sent_back = rounded_sum([mine_back[back:]] + [value[back:] for value in came_back])
            if vectors is not None:
                sent_back = jnp.concatenate([sent_back, vector_rows(vectors)], axis=0)
            keep_back = [mine_back[:back]] + [value[:back] for value in came_back]
            self.state = keep_front, keep_back, (from_quad(sent_front), swap(sent_back, "chan"))
            return sent_front, sent_back
        if self.stage == 3:
            mine_front, mine_back, (came_front, came_back) = state
            parts = [rounded_sum(mine_front + came_front)] if front else []
            parts.append(rounded_sum(mine_back + [came_back[:back]]))
            if vectors is not None:
                parts.append(rounded_sum([vector_rows(vectors), came_back[back:]]))
            value = jnp.concatenate(parts, axis=0)
            self.state = value, swap(value, "far")
            return value
        if self.stage == 4:
            value = rounded_sum(list(state))
            self.state = [value] + from_quad([value] * 3)
            return value
        if self.stage == 5:
            mine = jnp.concatenate(state, axis=0)
            self.state = mine, swap(mine, "core")
            return mine

    @property
    def pieces(self):
        return list(self.state)


def assemble_kernel(sizes, position, mine, other, *outs):
    units = mine.shape[0] // (4 * BLOCK)
    vectors = None
    for number, part in enumerate((mine, other)):
        for at in range(4):
            row = ((position[1] ^ number) * 4 + (position[2] ^ at)) * BLOCK
            rows = pl.ds(pl.multiple_of(row, BLOCK), BLOCK)
            unit = 0
            for out, size in zip(outs, sizes):
                for index in range(max(size, 1)):
                    begin = (at * units + unit) * BLOCK
                    value = part[begin : begin + BLOCK, :].astype(F32)
                    if size:
                        out[index, rows, :] = value
                    else:
                        out[rows, :] = value
                    unit += 1
            if unit < units:
                begin = (at * units + unit) * BLOCK
                term = part[begin : begin + BLOCK, :].astype(F32)
                vectors = term if vectors is None else vectors + term
    if vectors is not None:
        outs[-1][...] = vectors


def assemble(position, pieces, sizes, vectors, name):
    shapes = [shape(((size,) if size else ()) + (8 * BLOCK, CH), F32) for size in sizes]
    if vectors:
        shapes.append(shape((BLOCK, CH), F32))
    return call(
        functools.partial(assemble_kernel, sizes),
        "svv",
        "v" * len(shapes),
        shapes,
        [],
        name,
        4 << 30,
        6 << 20,
    )(position, *pieces)


def body(
    paired,
    features,
    crop_ids,
    cotangent,
    norm1_gain,
    norm1_bias,
    conv1_weight,
    conv1_bias,
    norm2_gain,
    norm2_bias,
    conv2_weight,
    conv2_bias,
    norm3_gain,
    norm3_bias,
    query_weight,
    query_bias,
    key_weight,
    value_weight,
    value_bias,
    proj_weight,
    proj_bias,
):
    _, local, pixels = features.shape
    devices = lax.axis_size("chan")
    index = lax.axis_index("chan").astype(jnp.int32)
    tiles = pixels // (TILE * TILE)
    slots = tiles if devices == 1 else tiles // 2
    if paired:
        core, down, near = [lax.axis_index(a).astype(jnp.int32) for a in ("core", "y", "near")]
        quad = down * 2 + near
        piece = core * 4 + quad
    else:
        core = quad = jnp.int32(0)
    position = jnp.stack([index, core, quad])

    def exchange(parts):
        if paired:
            return [parts[0], swap(parts[1], "chan")]
        if devices == 2:
            parts = [jnp.where(index == 0, parts[k], parts[1 - k]) for k in range(2)]
        moved = lax.all_to_all(jnp.stack(parts), "chan", 0, 0)
        return [jnp.transpose(moved, (1, 0, 2)).reshape(moved.shape[1], CH)]

    def give_back(parts):
        if paired:
            return [parts[0], swap(parts[1], "chan")]
        whole = parts[0].reshape(parts[0].shape[0], devices, local)
        moved = lax.all_to_all(jnp.transpose(whole, (1, 0, 2)), "chan", 0, 0)
        parts = [moved[at] for at in range(devices)]
        if devices == 2:
            parts = [jnp.where(index == 0, parts[k], parts[1 - k]) for k in range(2)]
        return parts

    lanes = -(-local // 128) * 128

    def widened(signal):
        return jnp.pad(signal, ((0, lanes - local), (0, 0))) if lanes > local else signal

    def narrowed(parts):
        return [part[:, :local] for part in parts] if lanes > local else parts

    def unpack_lanes(parts, by_pixel, dtype, name):
        if lanes > local:
            parts = [jnp.pad(part, ((0, 0), (0, lanes - local))) for part in parts]
        whole = unpack(position, tables[0], parts, pixels, by_pixel, dtype, slots, name)
        return whole[:local]

    vectors = jnp.stack(
        [
            norm1_gain,
            norm1_bias,
            conv1_bias,
            norm2_gain,
            norm2_bias,
            conv2_bias,
            norm3_gain,
            norm3_bias,
            query_bias,
            value_bias,
            proj_bias,
        ]
        + [jnp.zeros_like(proj_bias)] * 5
    )
    small = jnp.stack([query_weight, key_weight, value_weight, proj_weight])
    if paired:
        eighth = local // 8
        part = lax.dynamic_slice_in_dim(conv1_weight, piece * eighth, eighth, 1)
        eighth1 = swap(part, "chan")
        part = lax.dynamic_slice_in_dim(conv2_weight, piece * eighth, eighth, 1)
        eighth2 = swap(part, "chan")
        par_parts = [vectors, swap(vectors, "chan")]
    else:
        par_parts = [lax.all_gather(vectors, "chan", axis=1, tiled=True)]
        weight1 = [lax.all_gather(conv1_weight, "chan", axis=1, tiled=True)]
    tables, packed = pack_first(
        position, crop_ids[0], widened(features[0]), devices, slots, "pack_features"
    )
    feature_parts = exchange(narrowed(packed))
    if paired:
        eighth1, par_parts[1] = after((eighth1, par_parts[1]), packed[1])
        mine = to_all(eighth1, QUAD, 4)
        weight1 = [conv1_weight, mine, swap(mine, "core")]
    packed = pack(
        position, tables[0], widened(cotangent[0]), False, devices, slots, "pack_cotangent"
    )
    packed = list(packed)
    if paired:
        eighth2, small = after((eighth2, small), feature_parts[1], weight1[1], packed[1])
        weight2 = [conv2_weight, to_all(eighth2, ("core",) + QUAD, 8)]
        part = lax.dynamic_slice_in_dim(small, core * (local // 2), local // 2, 1)
        own_small = swap(part, "chan")
    else:
        weight2 = [lax.all_gather(conv2_weight, "chan", axis=1, tiled=True)]
        weight3 = [lax.all_gather(small, "chan", axis=1, tiled=True)]
        tangent_parts = exchange(narrowed(packed))
    par, feats, pad1, hidden, pad2, stats1, stats2 = first(
        position, tables, par_parts, feature_parts, weight1, slots
    )
    if paired:
        own_small, packed[1] = after((own_small, packed[1]), pad2)
        tangent_parts = [packed[0], swap(packed[1], "chan")]
        weight3 = [small, own_small, swap(own_small, "core")]
    resid, normed, stats3 = second(position, tables, par, feats, pad2, weight2, slots)
    if paired:
        weight3 = after(weight3, normed)
    out_parts, small_grads, (vecs3, grad2) = attention(
        position, tables, par, normed, resid, stats3, tangent_parts, weight3, slots
    )
    out_parts = give_back(out_parts)
    if paired:
        resid_grad = grad2
        halves = weight_grad(
            position, pad2, grad2, True, slots, "conv2_weight_grad", 8, small_grads
        )
        chain2 = Reduction(halves, 8, 13)
        grad2 = after(grad2, halves[1])
        grad1, vecs2 = middle(position, tables, par, stats2, grad2, weight2, hidden, slots)
        back = functools.partial(last, position, tables, par, stats1, (vecs2, vecs3), feats)
        sent = chain2.advance(grad1, out_parts[1])
        halves = weight_grad(
            position, pad1, after(grad1, sent), True, slots, "conv1_weight_grad", 0
        )
        sent = chain2.advance(halves[1])
        chain1 = Reduction(after(halves, sent), 0, 9)
        grad1 = after(grad1, sent, halves[1])
        in_other, vecs_other = back(grad1, weight1, resid_grad, 1, slots)
        sent = chain1.advance(in_other, chain2.state), chain2.advance(in_other)
        in_got = swap(after(in_other, sent), "chan")
        grad1 = after(grad1, sent, in_other)
        in_own, vecs_own = back(grad1, weight1, resid_grad, 0, slots)
        sent = chain1.advance(in_own, vectors=vecs_other), chain2.advance(in_own)
        out_parts = after(out_parts, sent, in_own, in_got)
        output = unpack_lanes(out_parts, False, BF16, "unpack_output")
        sent = chain1.advance(output, vectors=vecs_own)
        in_parts = after([in_own, in_got], sent)
        input_grad = unpack_lanes(in_parts, True, F32, "unpack_input_grad")
        sent = chain1.advance(input_grad), chain2.advance(input_grad)
        sent = chain1.advance()
        small_grads = assemble(
            position, after(chain2.pieces, sent), [0, 0, 0, 0, 9], False, "conv2_grads"
        )
        small_grads, weight2_grad = small_grads[:4], small_grads[4]
        weight1_grad, vecs = assemble(position, chain1.pieces, [9], True, "conv1_grads")
        vecs = vecs[:16, :local]
    else:
        output = unpack_lanes(out_parts, False, BF16, "unpack_output")
        grads2 = weight_grad(position, pad2, grad2, False, slots, "conv2_weight_grad")
        grad1, vecs2 = middle(position, tables, par, stats2, grad2, weight2, hidden, slots)
        grads1 = weight_grad(position, pad1, grad1, False, slots, "conv1_weight_grad")
        in_all, vecs1 = last(
            position, tables, par, stats1, (vecs2, vecs3), feats, grad1, weight1, grad2, 0, slots
        )
        input_grad = unpack_lanes(give_back([in_all]), True, F32, "unpack_input_grad")

        def total(grad, axis):
            part = lax.psum_scatter(grad, "chan", scatter_dimension=axis, tiled=True)
            return lax.psum(part, "dp").astype(F32)

        small_grads, weight2_grad, weight1_grad = [
            total(g[0], 1) for g in (small_grads, grads2, grads1)
        ]
        vecs = total(vecs1, 1)
    gq, gk, gv, gp = small_grads if paired else [small_grads[k] for k in range(4)]
    return (
        output[None],
        input_grad[None],
        vecs[G1],
        vecs[B1],
        weight1_grad,
        vecs[C1],
        vecs[G2],
        vecs[B2],
        weight2_grad,
        vecs[C2],
        vecs[G3],
        vecs[B3],
        gq,
        vecs[QB],
        gk,
        gv,
        vecs[VB],
        gp,
        vecs[PB],
    )


def solution(mesh):
    paired = mesh.shape["dp"] == 16 and mesh.shape["chan"] == 2
    rows = "dp"
    if paired:
        rows = ("far", "near", "y", "core")
        mesh = jax.sharding.Mesh(mesh.devices.reshape((2,) * 5), rows + ("chan",))
    canvas = P(rows, "chan", None)
    vector = P("chan")
    conv = P(None, "chan", None)
    matrix = P("chan", None)
    placed = (
        (canvas, P(rows, None, None), canvas)
        + (vector, vector, conv, vector, vector, vector, conv, vector, vector, vector)
        + (matrix, vector, matrix, matrix, vector, matrix, vector)
    )
    results = (
        (canvas, canvas, vector, vector, conv, vector, vector, vector, conv, vector)
        + (vector, vector, matrix, vector, matrix, matrix, vector, matrix, vector)
    )
    return jax.shard_map(functools.partial(body, paired), mesh=mesh, in_specs=placed, out_specs=results, check_vma=False)
```

```python
import functools
import itertools

import jax
import jax.numpy as jnp
import numpy as np
from jax import lax
from jax.experimental import pallas as pl
from jax.experimental.pallas import tpu as pltpu
from jax.sharding import PartitionSpec as P

CH = 512
GROUPS = 32
CROPS = 16
TILE = 8
BANDS = 4
EPS = 1e-06
F32 = jnp.float32
BF16 = jnp.bfloat16
HIGH = lax.Precision.HIGHEST
NN = (((1,), (0,)), ((), ()))
NT = (((1,), (1,)), ((), ()))
TN = (((0,), (0,)), ((), ()))
VMEM = pltpu.VMEM
ANY = pl.ANY
SCALE = CH ** (-0.5)


def band_layouts(units):
    return [
        tuple(np.diff((0,) + cuts + (units,)))
        for cuts in itertools.combinations(range(1, units), BANDS - 1)
    ]


PITCH = 8
QUERIES = 8
KEYS = 8


def window_cost(starts, sizes, slots):
    total = 0.0
    for block in range(0, slots, QUERIES):
        inside = [
            (starts <= at) & (at < starts + sizes) for at in (block, block + QUERIES - 1)
        ]
        low = (starts * inside[0]).sum(axis=-1) // 2 * 2
        high = ((starts + sizes) * inside[1]).sum(axis=-1)
        total = total + (high - low + KEYS - 1) // KEYS + 0.25
    return total


def best_starts(sizes, slots):
    layouts = sizes.shape[0]
    masks = np.arange(1 << (CROPS - 1), dtype=np.int32)
    bits = ((masks[None, :] >> np.arange(CROPS)[:, None]) & 1).astype(np.float32)
    picks = []
    for row in sizes.astype(np.float32):
        filled, squares = row @ bits, (row * row) @ bits
        cost = np.abs(squares - (row * row).sum() / 2) + 1e6 * np.abs(filled - slots)
        picks.append(bits[:, np.argpartition(cost, 4)[:4]].T)
        picks[-1] = picks[-1][(picks[-1] @ row) == slots]
        picks[-1] = picks[-1][np.arange(4) % len(picks[-1])]
    halves = np.array(picks, np.int32)
    halves = np.stack([1 - halves, halves], axis=2)
    held = halves * sizes[:, None, None, :]
    draw = np.random.RandomState(0)
    best = np.full((layouts, 4, 2), 1e9, np.float32)
    chosen = np.zeros(held.shape, np.int32)
    for trial in range(20):
        key = draw.rand(CROPS)[None, None, None, :] + 0.0 * held
        if trial == 0:
            key = -held + 0.01 * key
        elif trial < 8:
            key = key + 2.0 * (held % QUERIES != 0)
        order = np.argsort(key, axis=-1)
        ordered = np.take_along_axis(held, order, axis=-1)
        begin = np.cumsum(ordered, axis=-1) - ordered
        starts = np.zeros_like(held)
        np.put_along_axis(starts, order, begin, axis=-1)
        cost = window_cost(starts, held, slots)
        better = cost < best
        best = np.where(better, cost, best)
        chosen = np.where(better[..., None], starts, chosen)
    pick = np.argmin(best.max(axis=2), axis=1)
    rows = np.arange(layouts)
    owner, starts = halves[rows, pick, 1], chosen[rows, pick]
    return np.where(owner == 1, starts[:, 1] + slots, starts[:, 0])


@functools.lru_cache(maxsize=None)
def start_tables(devices, units, slots):
    layouts = band_layouts(units)
    rank = np.zeros(1 << (units - 1), np.int32)
    for number, sizes in enumerate(layouts):
        cuts = np.cumsum(sizes)[:-1]
        rank[sum(1 << (int(c) - 1) for c in cuts)] = number
    sizes = np.array(
        [[r * c for r in rows for c in cols] for rows in layouts for cols in layouts], np.int32
    )
    if devices == 2:
        starts = best_starts(sizes, slots)
    else:
        starts = np.zeros(sizes.shape, np.int32)
        for at, row in enumerate(sizes):
            loads = [0] * devices
            for crop in sorted(range(CROPS), key=lambda c: -row[c]):
                device = loads.index(min(loads))
                starts[at, crop] = device * slots + loads[device]
                loads[device] += int(row[crop])
    assert ((starts % slots) + sizes <= slots).all() and starts.max() < 256
    return rank, starts


def packed_tables(devices, units, slots):
    rank, starts = start_tables(devices, units, slots)
    shifts = np.arange(0, 32, 8, dtype=np.int64)
    words = (starts.reshape(-1, 4, 4).astype(np.int64) << shifts).sum(axis=2)
    words = np.where(words >= 1 << 31, words - (1 << 32), words)
    return np.concatenate([rank, words.reshape(-1).astype(np.int32)])


def write_plan(devices, slots, ids, table, slot_tile, slot_crop, starts, ends):
    units = ids.shape[0] // TILE
    count = units * units
    layouts = len(band_layouts(units))

    def code(at):
        bits = 0
        for step in range(units - 1):
            bits = bits + jnp.where(at(step) != at(step + 1), 1 << step, 0)
        return table[bits]

    def row_id(step):
        return ids[TILE * step, 0]

    def col_id(step):
        return ids[0, TILE * step]

    layout = code(row_id) * layouts + code(col_id)
    words = [table[(1 << (units - 1)) + 4 * layout + part] for part in range(4)]
    if devices * slots > count:

        def clear(at, carry):
            slot_tile[at] = -1
            slot_crop[at] = -1
            return carry

        lax.fori_loop(0, devices * slots, clear, 0)
    for crop in range(CROPS):
        start = lax.shift_right_logical(words[crop // 4], jnp.int32(8 * (crop % 4))) & 255
        starts[crop] = start
        ends[crop] = start

    def place(row, carry):
        for col in range(units):
            crop = ids[row * TILE, col * TILE]
            at = ends[crop]
            slot_tile[at] = row * units + col
            slot_crop[at] = crop
            ends[crop] = at + 1
        return carry

    lax.fori_loop(0, units, place, 0)


class Plan:
    def __init__(self, me, slot_tile, slot_crop, slots):
        self.slots = slots
        base = me * slots
        lane = lax.broadcasted_iota(jnp.int32, (1, 128), 1) % slots
        down = lax.broadcasted_iota(jnp.int32, (slots, 1), 0)
        self.tile_row, self.crop_row = jnp.zeros_like(lane), jnp.zeros_like(lane)
        self.tile_col, self.crop_col = jnp.zeros_like(down), jnp.zeros_like(down)
        for slot in range(slots):
            tile, crop = slot_tile[base + slot], slot_crop[base + slot]
            self.tile_row = jnp.where(lane == slot, tile, self.tile_row)
            self.crop_row = jnp.where(lane == slot, crop, self.crop_row)
            self.tile_col = jnp.where(down == slot, tile, self.tile_col)
            self.crop_col = jnp.where(down == slot, crop, self.crop_col)
        self.same = (self.crop_col == self.crop_row[:, 0:slots]).astype(F32)


def group_total(value):
    width = CH // GROUPS
    lane = lax.broadcasted_iota(jnp.int32, (value.shape[0], 128), 1)
    parts = []
    for at in range(0, value.shape[1], 128):
        part = value[:, at : at + 128]
        step = 1
        while step < width:
            up = pltpu.roll(part, 128 - step, 1)
            down = pltpu.roll(part, step, 1)
            part = part + jnp.where((lane & step) == 0, up, down)
            step *= 2
        parts.append(part)
    return jnp.concatenate(parts, axis=1)


def crop_mean(same, value):
    count = jnp.sum(same, axis=1, keepdims=True) * float(TILE * TILE * (CH // GROUPS))
    total = lax.dot_general(same, group_total(value), NN, precision=HIGH, preferred_element_type=F32)
    return total / count


def lanes_of(width):
    return [slice(at, at + 128) for at in range(0, width, 128)]


def slab_sum(pixels, slots, width, term):
    parts = []
    for lanes in lanes_of(width):

        def step(at, total):
            return total + term(at, lanes)

        parts.append(lax.fori_loop(0, pixels, step, jnp.zeros((slots, 128), F32), unroll=8))
    return jnp.concatenate(parts, axis=1)


def slab_stats(pixels, slots, slab, same):
    mean = crop_mean(same, slab_sum(pixels, slots, CH, slab))

    def square(at, lanes):
        centred = slab(at, lanes) - mean[:, lanes]
        return centred * centred

    return mean, lax.rsqrt(crop_mean(same, slab_sum(pixels, slots, CH, square)) + EPS)


def sigmoid(value):
    return 0.5 * jnp.tanh(0.5 * value) + 0.5


def fill_halo(pad, plan):
    slots = plan.slots
    wide = TILE * slots
    tile_c = jnp.concatenate([plan.tile_col] * TILE, axis=0)
    crop_c = jnp.concatenate([plan.crop_col] * TILE, axis=0)
    tile_r = jnp.concatenate([plan.tile_row] * (wide // 128), axis=1)
    crop_r = jnp.concatenate([plan.crop_row] * (wide // 128), axis=1)
    block_c = lax.broadcasted_iota(jnp.int32, (wide, wide), 0) // slots
    block_r = lax.broadcasted_iota(jnp.int32, (wide, wide), 1) // slots
    linked = (crop_c == crop_r) & (tile_c >= 0)

    def near(row_step, col_step):
        return linked & (tile_r == tile_c + (TILE * row_step + col_step))

    def edge(row_step, col_step, source):
        pick = (near(row_step, col_step) & (block_c == block_r)).astype(F32).astype(BF16)
        moved = jnp.dot(pick, source.reshape(wide, CH), preferred_element_type=F32).astype(BF16)
        return moved.reshape(TILE, slots, CH)

    def corner(row_step, col_step, source):
        pick = near(row_step, col_step)[0:slots, 0:slots].astype(F32).astype(BF16)
        return jnp.dot(pick, source, preferred_element_type=F32).astype(BF16)

    low, high, end = 1, TILE, TILE + 1
    pad[0, low:end] = edge(-1, 0, pad[high, low:end])
    pad[end, low:end] = edge(1, 0, pad[low, low:end])
    pad[low:end, 0] = edge(0, -1, pad[low:end, high])
    pad[low:end, end] = edge(0, 1, pad[low:end, low])
    pad[0, 0] = corner(-1, -1, pad[high, high])
    pad[0, end] = corner(-1, 1, pad[high, low])
    pad[end, 0] = corner(1, -1, pad[low, high])
    pad[end, end] = corner(1, 1, pad[low, low])


class WeightLoad:
    def __init__(self, position, pieces, target, sem, columns=None):
        self.copies = []
        views = [(pieces[0], None)]
        if len(pieces) > 1:
            me, core = position[0], position[1]
            half = pieces[0].shape[1]
            views = [(pieces[0], me * half)]
            part = half // (len(pieces) - 1)
            for number, piece in enumerate(pieces[1:]):
                spot = (1 - me) * half
                if len(pieces) == 3:
                    spot = spot + (core ^ number) * part
                if len(piece.shape) == 3:
                    views.append((piece, spot))
                    continue
                for at in range(piece.shape[0]):
                    views.append((piece.at[at], spot + at * piece.shape[2]))
        for at, (piece, spot) in enumerate(views):
            width = piece.shape[1]
            rows = slice(None)
            if spot is not None:
                rows = pl.ds(pl.multiple_of(spot, 32), width)
            if columns is not None:
                piece = piece.at[:, :, columns]
            self.copies.append(pltpu.make_async_copy(piece, target.at[:, rows, :], sem.at[at]))

    def start(self):
        for copy in self.copies:
            copy.start()

    def wait(self):
        for copy in self.copies:
            copy.wait()


def weight_sems(pieces):
    return pltpu.SemaphoreType.DMA((9,))


BLOCK = CH // 16


def store_grad(grad, outs, work, position, unit, first, count, front=True):
    if len(outs) == 1:
        outs[0][unit] = grad.astype(BF16)
        return
    work[...] = grad
    me, core, quad = position[0], position[1], position[2]
    for half, out in enumerate(outs):
        for c in range(2):
            for q in range(4):
                row = (me ^ c) * (CH // 2) + (core ^ half) * (CH // 4) + (quad ^ q) * BLOCK
                part = work[pl.ds(pl.multiple_of(row, BLOCK), BLOCK), :]
                if front:
                    to = ((c * 4 + q) * first + unit) * BLOCK
                else:
                    to = (8 * first + (q * 2 + c) * (count - first) + unit - first) * BLOCK
                out[pl.ds(pl.multiple_of(to, BLOCK), BLOCK), :] = part.astype(BF16)


def store_vectors(vecs, out, me):
    if len(out.shape) == 2:
        out[...] = vecs[...]
    else:
        half = out.shape[2]
        out[0] = vecs[:, pl.ds(pl.multiple_of(me * half, half), half)]
        out[1] = vecs[:, pl.ds(pl.multiple_of((1 - me) * half, half), half)]


def vector_shape(paired):
    return shape((2, 16, CH // 2) if paired else (16, CH), F32)


def grad_shapes(count, paired):
    if paired:
        return [shape((8 * count * BLOCK, CH), BF16)] * 2
    return [shape((count, CH, CH), BF16)]


def conv_rows(pad, weight, row, slots, dims, flipped, count=1):
    total = None
    for tap in range(9):
        down, right = tap // 3, tap % 3
        if flipped:
            down, right = 2 - down, 2 - right
        left = pad[pl.ds(row + down, count), right : right + TILE].reshape(count * TILE * slots, CH)
        part = lax.dot_general(left, weight[tap], dims, preferred_element_type=F32)
        total = part if total is None else total + part
    return total


def load_full(parts, me, dtype, store):
    if len(parts) == 1:
        store(slice(None), parts[0][...].astype(dtype))
    else:
        local = parts[0].shape[-1]
        own = pl.ds(pl.multiple_of(me * local, local), local)
        other = pl.ds(pl.multiple_of((1 - me) * local, local), local)
        store(own, parts[0][...].astype(dtype))
        store(other, parts[1][...].astype(dtype))


def vmem(shape, dtype):
    return pltpu.VMEM(shape, dtype)


def specs(kinds):
    table = {
        "v": pl.BlockSpec(memory_space=pltpu.VMEM),
        "s": pl.BlockSpec(memory_space=pltpu.SMEM),
        "h": pl.BlockSpec(memory_space=pl.ANY),
    }
    return [table[k] for k in kinds]


ROOM = {
    "unpack_output": 18,
    "unpack_input_grad": 18,
    "conv2_weight_grad": 24,
    "conv1_weight_grad": 22,
    "conv2_input_grad": 24,
    "conv1_input_grad": 20,
    "conv2_grads": 16,
    "conv1_grads": 14,
}


def call(body, ins, outs, shapes, scratch, name, flops, moved):
    return pl.pallas_call(
        body,
        in_specs=specs(ins),
        out_specs=tuple(specs(outs)),
        out_shape=tuple(shapes),
        scratch_shapes=list(scratch),
        compiler_params=pltpu.CompilerParams(vmem_limit_bytes=ROOM.get(name, 60) << 20),
        cost_estimate=pl.CostEstimate(
            flops=int(flops), bytes_accessed=int(moved), transcendentals=0
        ),
        name=name,
    )


def shape(dims, dtype):
    return jax.ShapeDtypeStruct(dims, dtype)


def pack_first_kernel(devices, slots, position, ids, table, signal, *rest):
    plan, rest = rest[:4], rest[4:]
    write_plan(devices, slots, ids, table, *plan)
    pack_kernel(True, slots, position, plan[0], signal, *rest)


def pack_kernel(by_pixel, slots, position, slot_tile, signal, *rest):
    outs, (raster, stage) = rest[:-2], rest[-2:]
    local, pixels = signal.shape
    side = int(pixels**0.5)
    chunk = 512
    cols = local // 128
    for at in range(0, pixels, chunk):
        flipped = signal[:, at : at + chunk].astype(F32).T
        for col in range(cols):
            raster[col, at : at + chunk, :] = flipped[:, col * 128 : (col + 1) * 128]
    for number, out in enumerate(outs):

        def step(slot, carry):
            tile = slot_tile[pack_base(position, number, len(outs), slots) + slot]
            keep = tile >= 0
            tile = jnp.maximum(tile, 0)
            start = (tile // TILE) * (TILE * side) + (tile % TILE) * TILE
            for row in range(TILE):
                for col in range(cols):
                    value = raster[col, pl.ds(pl.multiple_of(start + row * side, TILE), TILE), :]
                    value = jnp.where(keep, value, 0.0)
                    if by_pixel:
                        pitch = slots + PITCH
                        to = pl.ds(row * TILE * pitch + slot, TILE, stride=pitch)
                        stage[col, to, :] = value
                    else:
                        at = pl.multiple_of(slot * (TILE * TILE) + row * TILE, TILE)
                        stage[col, pl.ds(at, TILE), :] = value
            return carry

        lax.fori_loop(0, slots, step, 0)
        size = slots if by_pixel else TILE * TILE
        pitch = size + PITCH if by_pixel else size
        for number in range(out.shape[0] // size):
            for col in range(cols):
                span = slice(col * 128, (col + 1) * 128)
                value = stage[col, number * pitch : number * pitch + size, :]
                out[number * size : (number + 1) * size, span] = value.astype(BF16)


def pack_base(position, number, devices, slots):
    return (position[0] ^ number if devices == 2 else number) * slots


def pack_scratch(local, pixels, slots):
    rows = TILE * TILE * (slots + PITCH)
    return [vmem((local // 128, pixels, 128), F32), vmem((local // 128, rows, 128), F32)]


def pack_first(position, ids, signal, devices, slots, name):
    local, pixels = signal.shape
    rows = slots * TILE * TILE
    table = jnp.asarray(packed_tables(devices, ids.shape[0] // TILE, slots))
    result = call(
        functools.partial(pack_first_kernel, devices, slots),
        "sssv",
        "ssss" + "v" * devices,
        [shape((devices * slots,), jnp.int32)] * 2
        + [shape((CROPS,), jnp.int32)] * 2
        + [shape((rows, local), BF16)] * devices,
        pack_scratch(local, pixels, slots),
        name,
        4 << 30,
        6 << 20,
    )(position, ids, table, signal)
    return result[:4], result[4:]


def pack(position, slot_tile, signal, by_pixel, devices, slots, name):
    local, pixels = signal.shape
    rows = slots * TILE * TILE
    return call(
        functools.partial(pack_kernel, by_pixel, slots),
        "ssv",
        "v" * devices,
        [shape((rows, local), BF16)] * devices,
        pack_scratch(local, pixels, slots),
        name,
        40 << 30,
        6 << 20,
    )(position, slot_tile, signal)


def unpack_kernel(by_pixel, slots, position, slot_tile, *rest):
    ins, out, (raster, stage) = rest[:-3], rest[-3], rest[-2:]
    local, pixels = out.shape
    side = int(pixels**0.5)
    chunk = 512
    cols = local // 128
    for number, part in enumerate(ins):
        size = slots if by_pixel else TILE * TILE
        pitch = size + PITCH if by_pixel else size
        for at in range(part.shape[0] // size):
            for col in range(cols):
                span = slice(col * 128, (col + 1) * 128)
                value = part[at * size : (at + 1) * size, span]
                stage[col, at * pitch : at * pitch + size, :] = value.astype(F32)

        def step(slot, carry):
            tile = slot_tile[pack_base(position, number, len(ins), slots) + slot]

            @pl.when(tile >= 0)
            def _():
                start = (tile // TILE) * (TILE * side) + (tile % TILE) * TILE
                for row in range(TILE):
                    to = pl.ds(pl.multiple_of(start + row * side, TILE), TILE)
                    for col in range(cols):
                        if by_pixel:
                            at = pl.ds(row * TILE * pitch + slot, TILE, stride=pitch)
                        else:
                            first = pl.multiple_of(slot * (TILE * TILE) + row * TILE, TILE)
                            at = pl.ds(first, TILE)
                        raster[col, to, :] = stage[col, at, :]

            return carry

        lax.fori_loop(0, slots, step, 0)
    for at in range(0, pixels, chunk):
        for col in range(cols):
            span = slice(col * 128, (col + 1) * 128)
            out[span, at : at + chunk] = raster[col, at : at + chunk, :].T.astype(out.dtype)


def unpack(position, slot_tile, parts, pixels, by_pixel, dtype, slots, name):
    rows, local = parts[0].shape
    return call(
        functools.partial(unpack_kernel, by_pixel, slots),
        "ss" + "v" * len(parts),
        "v",
        [shape((local, pixels), dtype)],
        pack_scratch(local, pixels, slots),
        name,
        4 << 30,
        8 << 20,
    )(position, slot_tile, *parts)[0]


(G1, B1, C1, G2, B2, C2, G3, B3, QB, VB, PB) = range(11)


def norm_swish_pad(slab, mean, inverse, gain, bias, pad, copy=None):
    scaled = inverse * gain
    for lanes in lanes_of(CH):
        centre, factor, offset = mean[:, lanes], scaled[:, lanes], bias[:, lanes]

        def step(row, carry):
            for col in range(TILE):
                value = slab(row * TILE + col, lanes)
                before = (value - centre) * factor + offset
                pad[row + 1, col + 1, :, lanes] = (before * sigmoid(before)).astype(BF16)
                if copy is not None:
                    copy[row * TILE + col, :, lanes] = value.astype(BF16)
            return carry

        lax.fori_loop(0, TILE, step, 0)


def first_kernel(parts, count, position, slot_tile, slot_crop, *rest):
    feature_parts, rest = rest[:parts], rest[parts:]
    par_parts, rest = rest[:parts], rest[parts:]
    pieces, rest = rest[:count], rest[count:]
    (par, feats_hbm, pad1_hbm, hidden_hbm, pad2_hbm, stats1, stats2) = rest[:7]
    feats, rounded, hidden, pad1, pad2, weight, weight_sem, sem = rest[7:]
    pixels, slots, _ = hidden.shape
    load_weight = WeightLoad(position, pieces, weight, weight_sem)
    load_weight.start()

    def put_par(columns, value):
        par[:, columns] = value

    load_full(par_parts, position[0], F32, put_par)

    def put(columns, value):
        feats[:, columns] = value

    load_full(feature_parts, position[0], BF16, put)
    save_feats = pltpu.make_async_copy(feats, feats_hbm, sem.at[1])
    save_feats.start()

    plan = Plan(position[0], slot_tile, slot_crop, slots)

    def slab1(at, lanes):
        return feats[pl.ds(pl.multiple_of(at * slots, slots), slots), lanes].astype(F32)

    mean, inverse = slab_stats(pixels, slots, slab1, plan.same)
    stats1[0], stats1[1] = mean, inverse
    norm_swish_pad(slab1, mean, inverse, par[G1 : G1 + 1, :], par[B1 : B1 + 1, :], pad1)
    fill_halo(pad1, plan)
    save_pad1 = pltpu.make_async_copy(pad1, pad1_hbm, sem.at[2])
    save_pad1.start()
    load_weight.wait()

    def step(row, carry):
        total = conv_rows(pad1, weight, row, slots, NT, False) + par[C1 : C1 + 1, :]
        hidden[pl.ds(row * TILE, TILE)] = total.reshape(TILE, slots, CH)
        return carry

    lax.fori_loop(0, TILE, step, 0)

    def slab2(at, lanes):
        return hidden[at, :, lanes]

    mean, inverse = slab_stats(pixels, slots, slab2, plan.same)
    stats2[0], stats2[1] = mean, inverse
    norm_swish_pad(
        slab2, mean, inverse, par[G2 : G2 + 1, :], par[B2 : B2 + 1, :], pad2, rounded
    )
    save_hidden = pltpu.make_async_copy(rounded, hidden_hbm, sem.at[3])
    save_hidden.start()
    fill_halo(pad2, plan)
    save_pad2 = pltpu.make_async_copy(pad2, pad2_hbm, sem.at[4])
    save_pad2.start()
    save_feats.wait()
    save_pad1.wait()
    save_hidden.wait()
    save_pad2.wait()


def first(position, tables, par_parts, parts, weight, slots):
    pixels = TILE * TILE
    rows = pixels * slots
    pad = (TILE + 2, TILE + 2, slots, CH)
    return call(
        functools.partial(first_kernel, len(parts), len(weight)),
        "sss" + "v" * len(parts) + "v" * len(parts) + "h" * len(weight),
        "vhhhhvv",
        [
            shape((16, CH), F32),
            shape((rows, CH), BF16),
            shape(pad, BF16),
            shape((pixels, slots, CH), BF16),
            shape(pad, BF16),
            shape((2, slots, CH), F32),
            shape((2, slots, CH), F32),
        ],
        [
            vmem((rows, CH), BF16),
            vmem((pixels, slots, CH), BF16),
            vmem((pixels, slots, CH), F32),
            vmem(pad, BF16),
            vmem(pad, BF16),
            vmem((9, CH, CH), BF16),
            weight_sems(weight),
            pltpu.SemaphoreType.DMA((5,)),
        ],
        "conv1_forward",
        2 * rows * CH * CH * 9,
        20 << 20,
    )(position, *tables[:2], *parts, *par_parts, *weight)


def second_kernel(count, position, slot_tile, slot_crop, par, feats, pad_hbm, *rest):
    pieces, rest = rest[:count], rest[count:]
    resid_hbm, normed_hbm, stats3 = rest[:3]
    resid, resid_tile, normed, pad, weight, rows_scr, weight_sem, sem = rest[3:]
    slots = pad.shape[2]
    pixels = TILE * TILE
    load_pad = pltpu.make_async_copy(pad_hbm, pad, sem.at[0])
    load_weight = WeightLoad(position, pieces, weight, weight_sem)
    load_pad.start()
    load_weight.start()
    plan = Plan(position[0], slot_tile, slot_crop, slots)
    same = plan.same
    load_pad.wait()
    load_weight.wait()
    wide = TILE * slots

    def step(row, carry):
        at = pl.ds(pl.multiple_of(row * wide, wide), wide)
        total = conv_rows(pad, weight, row, slots, NT, False) + par[C2 : C2 + 1, :]
        total = total + feats[at, :].astype(F32)
        for col in range(CH // 128):
            for x in range(TILE):
                to = pl.multiple_of((row * TILE + x) * (slots + PITCH), 8)
                part = total[x * slots : (x + 1) * slots, col * 128 : (col + 1) * 128]
                resid[col, pl.ds(to, slots), :] = part
        return carry

    lax.fori_loop(0, TILE, step, 0)

    def slab(at, lanes):
        begin = pl.multiple_of(at * (slots + PITCH), 8)
        return resid[lanes.start // 128, pl.ds(begin, slots), :]

    mean, inverse = slab_stats(pixels, slots, slab, same)
    stats3[0], stats3[1] = mean, inverse
    rows_scr[0], rows_scr[1] = mean, inverse * par[G3 : G3 + 1, :]
    bias = par[B3 : B3 + 1, :]

    def tile_step(slot, carry):
        at = pl.ds(pl.multiple_of(slot * pixels, pixels), pixels)
        centre, factor = rows_scr[0, pl.ds(slot, 1)], rows_scr[1, pl.ds(slot, 1)]
        for col, lanes in enumerate(lanes_of(CH)):
            value = resid[col, pl.ds(slot, pixels, stride=slots + PITCH), :]
            resid_tile[at, lanes] = value.astype(BF16)
            scaled = (value - centre[:, lanes]) * factor[:, lanes]
            normed[at, lanes] = (scaled + bias[:, lanes]).astype(BF16)
        return carry

    lax.fori_loop(0, slots, tile_step, 0, unroll=2)
    save_resid = pltpu.make_async_copy(resid_tile, resid_hbm, sem.at[2])
    save_normed = pltpu.make_async_copy(normed, normed_hbm, sem.at[3])
    save_resid.start()
    save_normed.start()
    save_resid.wait()
    save_normed.wait()


def second(position, tables, par, feats, pad, weight, slots):
    pixels = TILE * TILE
    rows = pixels * slots
    return call(
        functools.partial(second_kernel, len(weight)),
        "sssvvh" + "h" * len(weight),
        "hhv",
        [shape((rows, CH), BF16), shape((rows, CH), BF16), shape((2, slots, CH), F32)],
        [
            vmem((CH // 128, pixels * (slots + PITCH), 128), F32),
            vmem((rows, CH), BF16),
            vmem((rows, CH), BF16),
            vmem(pad.shape, BF16),
            vmem((9, CH, CH), BF16),
            vmem((2, slots, CH), F32),
            weight_sems(weight),
            pltpu.SemaphoreType.DMA((4,)),
        ],
        "conv2_forward",
        2 * rows * CH * CH * 9,
        16 << 20,
    )(position, *tables[:2], par, feats, pad, *weight)


def attention_kernel(parts, outs, count, position, slot_tile, slot_crop, starts, ends, *rest):
    par, normed, resid_hbm, stats3 = rest[:4]
    tangent_parts, rest = rest[4 : 4 + parts], rest[4 + parts :]
    pieces, rest = rest[:count], rest[count:]
    out_hbm, rest = rest[:outs], rest[outs:]
    grads_hbm, rest = rest[:outs], rest[outs:]
    vecs_out, pad = rest[:2]
    (tangent, query, key, value, mixed_grad, mixed, query_grad, key_grad, value_grad) = rest[2:11]
    normed_grad, by_tile, rows_scr, weight, key_crop, work, vecs = rest[11:18]
    scores_scr, prob_grads, sums, weight_sem, sem, resid = rest[18:24]
    grad_outs = rest[24:]
    load_weight = WeightLoad(position, pieces, weight, weight_sem)
    load_weight.start()
    wq, wk, wv, wp = (weight.at[k] for k in range(4))
    rows = normed.shape[0]
    pixels = TILE * TILE
    slots = rows // pixels
    me = position[0]
    base = me * slots
    per_block = QUERIES
    block = per_block * pixels
    plan = Plan(me, slot_tile, slot_crop, slots)
    lane_slot = lax.broadcasted_iota(jnp.int32, (1, rows), 1) // pixels
    crops = jnp.zeros((1, rows), jnp.int32)
    for slot in range(slots):
        crops = jnp.where(lane_slot == slot, slot_crop[base + slot], crops)
    key_crop[...] = crops

    half = CH // outs
    columns = [pl.ds(0, CH)]
    if outs == 2:
        columns = [pl.ds(pl.multiple_of((me ^ k) * half, half), half) for k in range(2)]
    load_tangent = [
        pltpu.make_async_copy(part, tangent.at[:, columns[k]], sem.at[k])
        for k, part in enumerate(tangent_parts)
    ]
    load_resid = pltpu.make_async_copy(resid_hbm, resid, sem.at[2])
    save_out = [
        pltpu.make_async_copy(query.at[:, columns[k]], part, sem.at[3 + k])
        for k, part in enumerate(out_hbm)
    ]
    save_grads = [
        pltpu.make_async_copy(part, grads_hbm[k], sem.at[5 + k])
        for k, part in enumerate(grad_outs)
    ]
    for copy in load_tangent + [load_resid]:
        copy.start()
    load_weight.wait()
    for copy in load_tangent:
        copy.wait()

    def project(at, carry):
        span = pl.ds(pl.multiple_of(at * block, block), block)
        left = normed[span, :]
        total = lax.dot_general(left, wq[...], NT, preferred_element_type=F32)
        query[span, :] = (total + par[QB : QB + 1, :]).astype(BF16)
        key[span, :] = lax.dot_general(left, wk[...], NT, preferred_element_type=F32).astype(BF16)
        total = lax.dot_general(left, wv[...], NT, preferred_element_type=F32)
        value[span, :] = (total + par[VB : VB + 1, :]).astype(BF16)
        mixed_grad[span, :] = jnp.dot(
            tangent[span, :], wp[...], preferred_element_type=F32
        ).astype(BF16)
        key_grad[span, :] = jnp.zeros((block, CH), F32)
        value_grad[span, :] = jnp.zeros((block, CH), F32)
        return carry

    lax.fori_loop(0, rows // block, project, 0)

    def attend_step(at, carry):
        span = pl.ds(pl.multiple_of(at * block, block), block)
        low_crop = slot_crop[base + at * per_block]
        high_crop = slot_crop[base + at * per_block + per_block - 1]
        low = starts[jnp.maximum(low_crop, 0)] - base
        low = jnp.where(low_crop < 0, at * per_block, low) // 2 * 2
        high = jnp.where(high_crop < 0, slots, ends[jnp.maximum(high_crop, 0)] - base)
        count = (high - low + KEYS - 1) // KEYS
        begin = jnp.minimum(low, slots - KEYS * count) * pixels
        down = lax.broadcasted_iota(jnp.int32, (block, 1), 0) // pixels
        own_crop = jnp.zeros((block, 1), jnp.int32)
        for slot in range(per_block):
            own_crop = jnp.where(down == slot, slot_crop[base + at * per_block + slot], own_crop)

        def keys_of(number):
            return pl.ds(pl.multiple_of(begin + number * (KEYS * pixels), 128), KEYS * pixels)

        def score(number, top):
            keys = keys_of(number)
            scores = lax.dot_general(
                query[span, :], key[keys, :], NT, preferred_element_type=F32
            )
            scores = jnp.where(own_crop == key_crop[:, keys], scores * SCALE, -1e30)
            scores_scr[number] = scores
            prob_grads[number] = lax.dot_general(
                mixed_grad[span, :], value[keys, :], NT, preferred_element_type=F32
            )
            return jnp.maximum(top, jnp.max(scores, axis=1, keepdims=True))

        top = lax.fori_loop(0, count, score, jnp.full((block, 1), -1e30, F32))

        def weigh(number, carry):
            total, inner = carry
            exponent = jnp.exp(scores_scr[number] - top)
            scores_scr[number] = exponent
            total += jnp.sum(exponent, axis=1, keepdims=True)
            inner += jnp.sum(exponent * prob_grads[number], axis=1, keepdims=True)
            return total, inner

        zero = jnp.zeros((block, 1), F32)
        total, inner = lax.fori_loop(0, count, weigh, (zero, zero))
        share = 1.0 / total
        inner = inner * share
        sums[...] = jnp.zeros_like(sums)

        def spread_back(number, carry):
            keys = keys_of(number)
            prob = scores_scr[number] * share
            rounded = prob.astype(BF16)
            score_grad = (prob * (prob_grads[number] - inner)).astype(BF16)
            sums[0] += jnp.dot(rounded, value[keys, :], preferred_element_type=F32)
            sums[1] += jnp.dot(score_grad, key[keys, :], preferred_element_type=F32)
            key_grad[keys, :] += lax.dot_general(
                score_grad, query[span, :], TN, preferred_element_type=F32
            )
            value_grad[keys, :] += lax.dot_general(
                rounded, mixed_grad[span, :], TN, preferred_element_type=F32
            )
            return carry

        lax.fori_loop(0, count, spread_back, 0)
        mixed[span, :] = sums[0].astype(BF16)
        query_grad[span, :] = (sums[1] * SCALE).astype(BF16)
        return carry

    lax.fori_loop(0, rows // block, attend_step, 0)

    def back(at, carry):
        query_bias, value_bias, tangent_sum = carry
        span = pl.ds(pl.multiple_of(at * block, block), block)
        dq = query_grad[span, :]
        dk = (key_grad[span, :] * SCALE).astype(BF16)
        dv = value_grad[span, :].astype(BF16)
        key[span, :] = dk
        value[span, :] = dv
        total = jnp.dot(dq, wq[...], preferred_element_type=F32)
        total += jnp.dot(dk, wk[...], preferred_element_type=F32)
        total += jnp.dot(dv, wv[...], preferred_element_type=F32)
        normed_grad[span, :] = total
        result = lax.dot_general(mixed[span, :], wp[...], NT, preferred_element_type=F32)
        result = (result + par[PB : PB + 1, :] + resid[span, :].astype(F32)).astype(BF16)
        query[span, :] = result
        query_bias += jnp.sum(dq.astype(F32), axis=0, keepdims=True)
        value_bias += jnp.sum(dv.astype(F32), axis=0, keepdims=True)
        tangent_sum += jnp.sum(tangent[span, :].astype(F32), axis=0, keepdims=True)
        return query_bias, value_bias, tangent_sum

    load_resid.wait()
    zero = jnp.zeros((1, CH), F32)
    query_bias, value_bias, tangent_sum = lax.fori_loop(
        0, rows // block, back, (zero, zero, zero)
    )
    for copy in save_out:
        copy.start()
    left = normed[...]
    for number, grad in enumerate((query_grad, key, value)):
        total = lax.dot_general(grad[...], left, TN, preferred_element_type=F32)
        store_grad(total, grad_outs, work, position, number, 4, 4)
    total = lax.dot_general(tangent[...], mixed[...], TN, preferred_element_type=F32)
    store_grad(total, grad_outs, work, position, 3, 4, 4)
    for copy in save_grads:
        copy.start()

    def tile_sums(slot, carry):
        span = pl.ds(pl.multiple_of(slot * pixels, pixels), pixels)
        row = pl.ds(slot, 1)
        centre, factor = stats3[0, row], stats3[1, row]
        plains, crosseds = [], []
        for lanes in lanes_of(CH):
            upstream = normed_grad[span, lanes]
            hat = (resid[span, lanes].astype(F32) - centre[:, lanes]) * factor[:, lanes]
            plains.append(jnp.sum(upstream, axis=0, keepdims=True))
            crosseds.append(jnp.sum(upstream * hat, axis=0, keepdims=True))
        rows_scr[0, row] = jnp.concatenate(plains, axis=1)
        rows_scr[1, row] = jnp.concatenate(crosseds, axis=1)
        return carry

    lax.fori_loop(0, slots, tile_sums, 0)
    same = plan.same
    gain = par[G3 : G3 + 1, :]
    plain, crossed = rows_scr[0], rows_scr[1]
    vecs[...] = jnp.zeros_like(vecs)
    vecs[G3 : G3 + 1, :] = jnp.sum(crossed, axis=0, keepdims=True)
    vecs[B3 : B3 + 1, :] = jnp.sum(plain, axis=0, keepdims=True)
    vecs[QB : QB + 1, :] = query_bias
    vecs[VB : VB + 1, :] = value_bias
    vecs[PB : PB + 1, :] = tangent_sum
    rows_scr[0] = crop_mean(same, plain * gain)
    rows_scr[1] = crop_mean(same, crossed * gain)

    def apply(slot, carry):
        span = pl.ds(pl.multiple_of(slot * pixels, pixels), pixels)
        padded = pl.ds(pl.multiple_of(slot * (pixels + PITCH), 8), pixels)
        row = pl.ds(slot, 1)
        centre, factor = stats3[0, row], stats3[1, row]
        slope = factor * gain
        level = factor * rows_scr[0, row]
        tilt = factor * factor * rows_scr[1, row]
        for col, lanes in enumerate(lanes_of(CH)):
            centred = resid[span, lanes].astype(F32) - centre[:, lanes]
            grad = normed_grad[span, lanes] * slope[:, lanes] - level[:, lanes]
            grad = grad - centred * tilt[:, lanes]
            by_tile[col, padded, :] = tangent[span, lanes].astype(F32) + grad
        return carry

    lax.fori_loop(0, slots, apply, 0)

    def spread(row, carry):
        total = carry
        for col in range(TILE):
            at = row * TILE + col
            slab = jnp.concatenate(
                [
                    by_tile[c, pl.ds(at, slots, stride=pixels + PITCH), :] for c in range(CH // 128)
                ],
                axis=1,
            )
            rounded = slab.astype(BF16)
            pad[row + 1, col + 1] = rounded
            total += jnp.sum(rounded.astype(F32), axis=0, keepdims=True)
        return total

    vecs[C2 : C2 + 1, :] = lax.fori_loop(0, TILE, spread, zero)
    store_vectors(vecs, vecs_out, me)
    fill_halo(pad, plan)
    for copy in save_out + save_grads:
        copy.wait()


def attention(position, tables, par, normed, resid, stats3, tangent_parts, weight, slots):
    pixels = TILE * TILE
    rows = pixels * slots
    parts = len(tangent_parts)
    pad = (TILE + 2, TILE + 2, slots, CH)
    if parts == 2:
        out_shapes = [shape((rows, CH // 2), BF16)] * 2
    else:
        out_shapes = [shape((rows, CH), BF16)]
    outs = len(out_shapes)
    result = call(
        functools.partial(attention_kernel, parts, outs, len(weight)),
        "sssssvvhv" + "h" * parts + "h" * len(weight),
        "h" * (2 * outs) + "vv",
        out_shapes
        + grad_shapes(4, outs == 2)
        + [vector_shape(outs == 2), shape(pad, BF16)],
        [vmem((rows, CH), BF16)] * 7
        + [vmem((rows, CH), F32)] * 3
        + [vmem((CH // 128, slots * (pixels + PITCH), 128), F32), vmem((2, slots, CH), F32)]
        + [vmem((4, CH, CH), BF16), vmem((1, rows), jnp.int32), vmem((CH, CH), F32)]
        + [vmem((16, CH), F32)]
        + [vmem((slots // KEYS, QUERIES * pixels, KEYS * pixels), F32)] * 2
        + [vmem((2, QUERIES * pixels, CH), F32)]
        + [weight_sems(weight), pltpu.SemaphoreType.DMA((7,)), vmem((rows, CH), BF16)]
        + [vmem(part.shape, BF16) for part in grad_shapes(4, outs == 2)],
        "attention",
        30 << 30,
        24 << 20,
    )(
        position,
        *tables,
        par,
        normed,
        resid,
        stats3,
        *tangent_parts,
        *weight,
    )
    return result[:outs], result[outs : 2 * outs], result[2 * outs :]


def weight_grad_kernel(paired, first, extra, position, active, grad, *rest):
    outs = 2 if paired else 1
    extras, rest = rest[: outs if extra else 0], rest[outs if extra else 0 :]
    out_parts, (flipped, work, sem) = rest[:outs], rest[outs:]
    copies = []
    for half, part in enumerate(extras):
        for at in range(8):
            source = part.at[pl.ds(at * extra * BLOCK, extra * BLOCK)]
            target = out_parts[half].at[pl.ds(at * first * BLOCK, extra * BLOCK)]
            copies.append(pltpu.make_async_copy(source, target, sem.at[half, at]))
    for copy in copies:
        copy.start()
    slots = active.shape[2]
    wide = TILE * slots
    for row in range(TILE):
        left = grad[row + 1, 1 : TILE + 1].reshape(wide, CH)
        flipped[:, row * wide : (row + 1) * wide] = left.T

    def step(front, tap, carry):
        right = active[pl.ds(tap // 3, TILE), pl.ds(tap % 3, TILE)].reshape(TILE * wide, CH)
        total = jnp.dot(flipped[...], right, preferred_element_type=F32)
        store_grad(total, out_parts, work, position, tap + extra, first, 9 + extra, front)
        return carry

    if first > extra:
        lax.fori_loop(0, first - extra, functools.partial(step, True), 0)
    if first - extra < 9:
        lax.fori_loop(first - extra, 9, functools.partial(step, False), 0)
    for copy in copies:
        copy.wait()


def weight_grad(position, active, grad, paired, slots, name, first=9, extras=()):
    rows = TILE * TILE * slots
    extra = 4 if extras else 0
    shapes = grad_shapes(9 + extra, paired)
    return call(
        functools.partial(weight_grad_kernel, paired, first, extra),
        "svv" + "h" * len(extras),
        "v" * len(shapes),
        shapes,
        [
            vmem((CH, rows), BF16),
            vmem((CH, CH), F32),
            pltpu.SemaphoreType.DMA((2, 8)),
        ],
        name,
        2 * rows * CH * CH * 9,
        12 << 20,
    )(position, active, grad, *extras)


def swish_back(upstream, before):
    gate = sigmoid(before)
    return upstream * (gate + before * gate * (1.0 - gate))


def norm_back_sums(source, upstream, mean, inverse, gain, bias, slots):
    plains, crosseds = [], []
    for lanes in lanes_of(upstream.shape[2]):
        centre, factor = mean[:, lanes], inverse[:, lanes]
        slope, offset = gain[:, lanes], bias[:, lanes]

        def step(at, carry):
            plain, crossed = carry
            hat = (source(at, lanes) - centre) * factor
            grad = swish_back(upstream[at, :, lanes], hat * slope + offset)
            upstream[at, :, lanes] = grad
            return plain + grad, crossed + grad * hat

        zero = jnp.zeros((slots, 128), F32)
        plain, crossed = lax.fori_loop(0, TILE * TILE, step, (zero, zero), unroll=4)
        plains.append(plain)
        crosseds.append(crossed)
    return jnp.concatenate(plains, axis=1), jnp.concatenate(crosseds, axis=1)


def norm_back_apply(source, upstream, mean, inverse, gain, plain, crossed, put):
    for lanes in lanes_of(upstream.shape[2]):
        centre, factor = mean[:, lanes], inverse[:, lanes]
        slope = factor * gain[:, lanes]
        level = factor * plain[:, lanes]
        tilt = factor * factor * crossed[:, lanes]

        def step(at, carry):
            centred = source(at, lanes) - centre
            put(at, lanes, upstream[at, :, lanes] * slope - level - centred * tilt)
            return carry

        lax.fori_loop(0, TILE * TILE, step, 0, unroll=8)


def middle_kernel(count, position, slot_tile, slot_crop, par, stats2, pad_hbm, hidden_hbm, *rest):
    pieces, rest = rest[:count], rest[count:]
    pad_out_hbm, vecs_out = rest[:2]
    pad, weight, hidden, upstream, pad_out, vecs, totals, weight_sem, sem = rest[2:]
    slots = pad.shape[2]
    load_pad = pltpu.make_async_copy(pad_hbm, pad, sem.at[0])
    load_weight = WeightLoad(position, pieces, weight, weight_sem)
    load_hidden = pltpu.make_async_copy(hidden_hbm, hidden, sem.at[2])
    load_pad.start()
    load_weight.start()
    load_hidden.start()
    plan = Plan(position[0], slot_tile, slot_crop, slots)
    same = plan.same
    load_pad.wait()
    load_weight.wait()

    def step(row, carry):
        total = conv_rows(pad, weight, row, slots, NN, True)
        upstream[pl.ds(row * TILE, TILE)] = total.reshape(TILE, slots, CH)
        return carry

    lax.fori_loop(0, TILE, step, 0)
    load_hidden.wait()
    mean, inverse = stats2[0], stats2[1]
    gain, bias = par[G2 : G2 + 1, :], par[B2 : B2 + 1, :]

    def source(at, lanes):
        return hidden[at, :, lanes].astype(F32)

    plain, crossed = norm_back_sums(
        source, upstream, mean, inverse, gain, bias, slots
    )
    vecs[...] = jnp.zeros_like(vecs)
    vecs[G2 : G2 + 1, :] = jnp.sum(crossed, axis=0, keepdims=True)
    vecs[B2 : B2 + 1, :] = jnp.sum(plain, axis=0, keepdims=True)
    plain = crop_mean(same, plain * gain)
    crossed = crop_mean(same, crossed * gain)

    totals[...] = jnp.zeros_like(totals)

    def put(at, lanes, grad):
        rounded = grad.astype(BF16)
        pad_out[at // TILE + 1, at % TILE + 1, :, lanes] = rounded
        totals[:, lanes] += rounded.astype(F32)

    norm_back_apply(source, upstream, mean, inverse, gain, plain, crossed, put)
    vecs[C1 : C1 + 1, :] = jnp.sum(totals[...], axis=0, keepdims=True)
    store_vectors(vecs, vecs_out, position[0])
    fill_halo(pad_out, plan)
    save = pltpu.make_async_copy(pad_out, pad_out_hbm, sem.at[3])
    save.start()
    save.wait()


def middle(position, tables, par, stats2, pad, weight, hidden, slots):
    pixels = TILE * TILE
    rows = pixels * slots
    return call(
        functools.partial(middle_kernel, len(weight)),
        "sssvvhh" + "h" * len(weight),
        "hv",
        [shape(pad.shape, BF16), vector_shape(len(weight) > 1)],
        [
            vmem(pad.shape, BF16),
            vmem((9, CH, CH), BF16),
            vmem((pixels, slots, CH), BF16),
            vmem((pixels, slots, CH), F32),
            vmem(pad.shape, BF16),
            vmem((16, CH), F32),
            vmem((slots, CH), F32),
            weight_sems(weight),
            pltpu.SemaphoreType.DMA((4,)),
        ],
        "conv2_input_grad",
        2 * rows * CH * CH * 9,
        16 << 20,
    )(position, *tables[:2], par, stats2, pad, hidden, *weight)


def last_kernel(
    whose, count, position, slot_tile, slot_crop, par, stats1, vecs2, vecs3, *rest
):
    feats_hbm, pad_hbm, resid_hbm = rest[:3]
    pieces, rest = rest[3 : 3 + count], rest[3 + count :]
    out, vecs, pad, weight, feats, resid, upstream, weight_sem, sem = rest
    slots = pad.shape[2]
    width = upstream.shape[2]
    pixels = TILE * TILE
    me = position[0]
    columns = None
    span = pl.ds(0, width)
    if width < CH:
        columns = span = pl.ds(pl.multiple_of((me ^ whose) * width, width), width)
    load_weight = WeightLoad(position, pieces, weight, weight_sem, columns)
    load_pad = pltpu.make_async_copy(pad_hbm, pad, sem.at[0])
    inner = pl.ds(1, TILE)
    load_resid = pltpu.make_async_copy(resid_hbm.at[inner, inner, :, span], resid, sem.at[1])
    load_feats = pltpu.make_async_copy(feats_hbm.at[:, span], feats, sem.at[2])
    load_pad.start()
    load_weight.start()
    load_feats.start()
    load_resid.start()
    plan = Plan(me, slot_tile, slot_crop, slots)
    same = plan.same
    load_pad.wait()
    load_weight.wait()

    def step(row, carry):
        total = conv_rows(pad, weight, row, slots, NN, True)
        upstream[pl.ds(row * TILE, TILE)] = total.reshape(TILE, slots, width)
        return carry

    lax.fori_loop(0, TILE, step, 0)
    load_feats.wait()
    load_resid.wait()
    mean, inverse = stats1[0, :, span], stats1[1, :, span]
    gain, bias = par[G1 : G1 + 1, span], par[B1 : B1 + 1, span]

    def source(at, lanes):
        return feats[pl.ds(pl.multiple_of(at * slots, slots), slots), lanes].astype(F32)

    plain, crossed = norm_back_sums(source, upstream, mean, inverse, gain, bias, slots)
    vecs[...] = vecs2[...] + vecs3[...] if width == CH else vecs2[whose] + vecs3[whose]
    vecs[G1 : G1 + 1, :] = jnp.sum(crossed, axis=0, keepdims=True)
    vecs[B1 : B1 + 1, :] = jnp.sum(plain, axis=0, keepdims=True)
    plain = crop_mean(same, plain * gain)
    crossed = crop_mean(same, crossed * gain)

    def put(at, lanes, grad):
        rows = pl.ds(pl.multiple_of(at * slots, slots), slots)
        grad = resid[at // TILE, at % TILE, :, lanes].astype(F32) + grad
        out[rows, lanes] = grad.astype(out.dtype)

    norm_back_apply(source, upstream, mean, inverse, gain, plain, crossed, put)


def last(position, tables, par, stats1, vecs, feats, pad, weight, resid_grad, whose, slots):
    pixels = TILE * TILE
    rows = pixels * slots
    width = CH // 2 if len(weight) > 1 else CH
    return call(
        functools.partial(last_kernel, whose, len(weight)),
        "sssvvvvhhh" + "h" * len(weight),
        "vv",
        [
            shape((rows, width), F32 if width < CH and whose == 0 else BF16),
            shape((16, width), F32),
        ],
        [
            vmem(pad.shape, BF16),
            vmem((9, CH, width), BF16),
            vmem((rows, width), BF16),
            vmem((TILE, TILE, slots, width), BF16),
            vmem((pixels, slots, width), F32),
            weight_sems(weight),
            pltpu.SemaphoreType.DMA((3,)),
        ],
        "conv1_input_grad",
        2 * rows * CH * width * 9,
        10 << 20,
    )(position, *tables[:2], par, stats1, *vecs, feats, pad, resid_grad, *weight)


def after(value, *others):
    flat, tree = jax.tree.flatten(value)
    extra = jax.tree.leaves(others)
    held = lax.optimization_barrier(tuple(flat) + tuple(extra))
    return jax.tree.unflatten(tree, list(held[: len(flat)]))


def add(*terms):
    total = terms[0].astype(F32)
    for term in terms[1:]:
        total = total + term.astype(F32)
    return total


def swap(value, axis):
    return lax.ppermute(value, axis, [(0, 1), (1, 0)])


def to_all(value, axes, count):
    return lax.all_to_all(jnp.broadcast_to(value[None], (count,) + value.shape), axes, 0, 0)


QUAD = ("y", "near")


def from_quad(values):
    return [
        lax.ppermute(value, ("near", "y"), [(at, at ^ bits) for at in range(4)])
        for bits, value in zip((2, 1, 3), values)
    ]


def rounded_sum(terms):
    total = terms[0].astype(F32)
    for term in terms[1:]:
        total = total + term.astype(F32)
    return total.astype(BF16)


def vector_rows(vectors):
    rows, width = vectors.shape
    return jnp.pad(vectors.astype(BF16), ((0, BLOCK - rows), (0, CH - width)))


class Reduction:
    def __init__(self, halves, first, count):
        self.stage, self.first, self.count = 0, first, count
        self.state = (halves[0], halves[1], swap(halves[1], "core"))

    def advance(self, *others, vectors=None):
        if others:
            self.state = after(self.state, *others)
        self.stage += 1
        front = self.first * BLOCK
        back = (self.count - self.first) * BLOCK
        state = self.state
        if self.stage == 1:
            mine, _, came = state

            def part(begin, size):
                span = slice(begin, begin + size)
                return rounded_sum([mine[span], came[span]])

            start = 8 * front
            keep = part(0, 4 * front) if front else None, part(start, 2 * back)
            sent_front = part(4 * front, 4 * front) if front else None
            sent_back = [part(start + q * 2 * back, 2 * back) for q in (1, 2, 3)]
            came_front = swap(sent_front, "chan") if front else None
            self.state = keep, (came_front, from_quad(sent_back))
            return sent_front, sent_back
        if self.stage == 2:
            (mine_front, mine_back), (came_front, came_back) = state
            piece = [slice(q * front, (q + 1) * front) for q in range(4)]
            sent_front, keep_front = [], None
            if front:
                terms = [[mine_front[span], came_front[span]] for span in piece]
                keep_front, sent_front = terms[0], [rounded_sum(term) for term in terms[1:]]
            sent_back = rounded_sum([mine_back[back:]] + [value[back:] for value in came_back])
            if vectors is not None:
                sent_back = jnp.concatenate([sent_back, vector_rows(vectors)], axis=0)
            keep_back = [mine_back[:back]] + [value[:back] for value in came_back]
            self.state = keep_front, keep_back, (from_quad(sent_front), swap(sent_back, "chan"))
            return sent_front, sent_back
        if self.stage == 3:
            mine_front, mine_back, (came_front, came_back) = state
            parts = [rounded_sum(mine_front + came_front)] if front else []
            parts.append(rounded_sum(mine_back + [came_back[:back]]))
            if vectors is not None:
                parts.append(rounded_sum([vector_rows(vectors), came_back[back:]]))
            value = jnp.concatenate(parts, axis=0)
            self.state = value, swap(value, "far")
            return value
        if self.stage == 4:
            value = rounded_sum(list(state))
            self.state = [value] + from_quad([value] * 3)
            return value
        if self.stage == 5:
            mine = jnp.concatenate(state, axis=0)
            self.state = mine, swap(mine, "core")
            return mine

    @property
    def pieces(self):
        return list(self.state)


def assemble_kernel(sizes, position, mine, other, *outs):
    units = mine.shape[0] // (4 * BLOCK)
    vectors = None
    for number, part in enumerate((mine, other)):
        for at in range(4):
            row = ((position[1] ^ number) * 4 + (position[2] ^ at)) * BLOCK
            rows = pl.ds(pl.multiple_of(row, BLOCK), BLOCK)
            unit = 0
            for out, size in zip(outs, sizes):
                for index in range(max(size, 1)):
                    begin = (at * units + unit) * BLOCK
                    value = part[begin : begin + BLOCK, :].astype(F32)
                    if size:
                        out[index, rows, :] = value
                    else:
                        out[rows, :] = value
                    unit += 1
            if unit < units:
                begin = (at * units + unit) * BLOCK
                term = part[begin : begin + BLOCK, :].astype(F32)
                vectors = term if vectors is None else vectors + term
    if vectors is not None:
        outs[-1][...] = vectors


def assemble(position, pieces, sizes, vectors, name):
    shapes = [shape(((size,) if size else ()) + (8 * BLOCK, CH), F32) for size in sizes]
    if vectors:
        shapes.append(shape((BLOCK, CH), F32))
    return call(
        functools.partial(assemble_kernel, sizes),
        "svv",
        "v" * len(shapes),
        shapes,
        [],
        name,
        4 << 30,
        6 << 20,
    )(position, *pieces)


def body(
    paired,
    features,
    crop_ids,
    cotangent,
    norm1_gain,
    norm1_bias,
    conv1_weight,
    conv1_bias,
    norm2_gain,
    norm2_bias,
    conv2_weight,
    conv2_bias,
    norm3_gain,
    norm3_bias,
    query_weight,
    query_bias,
    key_weight,
    value_weight,
    value_bias,
    proj_weight,
    proj_bias,
):
    _, local, pixels = features.shape
    devices = lax.axis_size("chan")
    index = lax.axis_index("chan").astype(jnp.int32)
    tiles = pixels // (TILE * TILE)
    slots = tiles if devices == 1 else tiles // 2
    if paired:
        core, down, near = [lax.axis_index(a).astype(jnp.int32) for a in ("core", "y", "near")]
        quad = down * 2 + near
        piece = core * 4 + quad
    else:
        core = quad = jnp.int32(0)
    position = jnp.stack([index, core, quad])

    def exchange(parts):
        if paired:
            return [parts[0], swap(parts[1], "chan")]
        if devices == 2:
            parts = [jnp.where(index == 0, parts[k], parts[1 - k]) for k in range(2)]
        moved = lax.all_to_all(jnp.stack(parts), "chan", 0, 0)
        return [jnp.transpose(moved, (1, 0, 2)).reshape(moved.shape[1], CH)]

    def give_back(parts):
        if paired:
            return [parts[0], swap(parts[1], "chan")]
        whole = parts[0].reshape(parts[0].shape[0], devices, local)
        moved = lax.all_to_all(jnp.transpose(whole, (1, 0, 2)), "chan", 0, 0)
        parts = [moved[at] for at in range(devices)]
        if devices == 2:
            parts = [jnp.where(index == 0, parts[k], parts[1 - k]) for k in range(2)]
        return parts

    lanes = -(-local // 128) * 128

    def widened(signal):
        return jnp.pad(signal, ((0, lanes - local), (0, 0))) if lanes > local else signal

    def narrowed(parts):
        return [part[:, :local] for part in parts] if lanes > local else parts

    def unpack_lanes(parts, by_pixel, dtype, name):
        if lanes > local:
            parts = [jnp.pad(part, ((0, 0), (0, lanes - local))) for part in parts]
        whole = unpack(position, tables[0], parts, pixels, by_pixel, dtype, slots, name)
        return whole[:local]

    vectors = jnp.stack(
        [
            norm1_gain,
            norm1_bias,
            conv1_bias,
            norm2_gain,
            norm2_bias,
            conv2_bias,
            norm3_gain,
            norm3_bias,
            query_bias,
            value_bias,
            proj_bias,
        ]
        + [jnp.zeros_like(proj_bias)] * 5
    )
    small = jnp.stack([query_weight, key_weight, value_weight, proj_weight])
    if paired:
        eighth = local // 8
        part = lax.dynamic_slice_in_dim(conv1_weight, piece * eighth, eighth, 1)
        eighth1 = swap(part, "chan")
        part = lax.dynamic_slice_in_dim(conv2_weight, piece * eighth, eighth, 1)
        eighth2 = swap(part, "chan")
        par_parts = [vectors, swap(vectors, "chan")]
    else:
        par_parts = [lax.all_gather(vectors, "chan", axis=1, tiled=True)]
        weight1 = [lax.all_gather(conv1_weight, "chan", axis=1, tiled=True)]
    tables, packed = pack_first(
        position, crop_ids[0], widened(features[0]), devices, slots, "pack_features"
    )
    feature_parts = exchange(narrowed(packed))
    if paired:
        eighth1, par_parts[1] = after((eighth1, par_parts[1]), packed[1])
        mine = to_all(eighth1, QUAD, 4)
        weight1 = [conv1_weight, mine, swap(mine, "core")]
    packed = pack(
        position, tables[0], widened(cotangent[0]), False, devices, slots, "pack_cotangent"
    )
    packed = list(packed)
    if paired:
        part = lax.dynamic_slice_in_dim(small, core * (local // 2), local // 2, 1)
        eighth2, part = after((eighth2, part), feature_parts[1], weight1[1], packed[1])
        weight2 = [conv2_weight, to_all(eighth2, ("core",) + QUAD, 8)]
        own_small = swap(part, "chan")
    else:
        weight2 = [lax.all_gather(conv2_weight, "chan", axis=1, tiled=True)]
        weight3 = [lax.all_gather(small, "chan", axis=1, tiled=True)]
        tangent_parts = exchange(narrowed(packed))
    par, feats, pad1, hidden, pad2, stats1, stats2 = first(
        position, tables, par_parts, feature_parts, weight1, slots
    )
    if paired:
        own_small, packed[1] = after((own_small, packed[1]), pad2)
        tangent_parts = [packed[0], swap(packed[1], "chan")]
        weight3 = [small, own_small, swap(own_small, "core")]
    resid, normed, stats3 = second(position, tables, par, feats, pad2, weight2, slots)
    if paired:
        weight3 = after(weight3, normed)
    out_parts, small_grads, (vecs3, grad2) = attention(
        position, tables, par, normed, resid, stats3, tangent_parts, weight3, slots
    )
    out_parts = give_back(out_parts)
    if paired:
        resid_grad = grad2
        halves = weight_grad(
            position, pad2, grad2, True, slots, "conv2_weight_grad", 8, small_grads
        )
        chain2 = Reduction(halves, 8, 13)
        grad2 = after(grad2, halves[1])
        grad1, vecs2 = middle(position, tables, par, stats2, grad2, weight2, hidden, slots)
        back = functools.partial(last, position, tables, par, stats1, (vecs2, vecs3), feats)
        sent = chain2.advance(grad1, out_parts[1])
        halves = weight_grad(
            position, pad1, after(grad1, sent), True, slots, "conv1_weight_grad", 0
        )
        sent = chain2.advance(halves[1])
        chain1 = Reduction(after(halves, sent), 0, 9)
        grad1 = after(grad1, sent, halves[1])
        in_other, vecs_other = back(grad1, weight1, resid_grad, 1, slots)
        sent = chain1.advance(in_other, chain2.state), chain2.advance(in_other)
        in_got = swap(after(in_other, sent), "chan")
        grad1 = after(grad1, sent, in_other)
        in_own, vecs_own = back(grad1, weight1, resid_grad, 0, slots)
        sent = chain1.advance(in_own, vectors=vecs_other), chain2.advance(in_own)
        out_parts = after(out_parts, sent, in_own, in_got)
        output = unpack_lanes(out_parts, False, BF16, "unpack_output")
        sent = chain1.advance(output, vectors=vecs_own)
        in_parts = after([in_own, in_got], sent)
        input_grad = unpack_lanes(in_parts, True, F32, "unpack_input_grad")
        sent = chain1.advance(input_grad)
        sent = sent, chain2.advance(sent)
        small_grads = assemble(
            position, after(chain2.pieces, sent), [0, 0, 0, 0, 9], False, "conv2_grads"
        )
        small_grads, weight2_grad = small_grads[:4], small_grads[4]
        chain1.advance(weight2_grad)
        weight1_grad, vecs = assemble(position, chain1.pieces, [9], True, "conv1_grads")
        vecs = vecs[:16, :local]
    else:
        output = unpack_lanes(out_parts, False, BF16, "unpack_output")
        grads2 = weight_grad(position, pad2, grad2, False, slots, "conv2_weight_grad")
        grad1, vecs2 = middle(position, tables, par, stats2, grad2, weight2, hidden, slots)
        grads1 = weight_grad(position, pad1, grad1, False, slots, "conv1_weight_grad")
        in_all, vecs1 = last(
            position, tables, par, stats1, (vecs2, vecs3), feats, grad1, weight1, grad2, 0, slots
        )
        input_grad = unpack_lanes(give_back([in_all]), True, F32, "unpack_input_grad")

        def total(grad, axis):
            part = lax.psum_scatter(grad, "chan", scatter_dimension=axis, tiled=True)
            return lax.psum(part, "dp").astype(F32)

        small_grads, weight2_grad, weight1_grad = [
            total(g[0], 1) for g in (small_grads, grads2, grads1)
        ]
        vecs = total(vecs1, 1)
    gq, gk, gv, gp = small_grads if paired else [small_grads[k] for k in range(4)]
    return (
        output[None],
        input_grad[None],
        vecs[G1],
        vecs[B1],
        weight1_grad,
        vecs[C1],
        vecs[G2],
        vecs[B2],
        weight2_grad,
        vecs[C2],
        vecs[G3],
        vecs[B3],
        gq,
        vecs[QB],
        gk,
        gv,
        vecs[VB],
        gp,
        vecs[PB],
    )


def solution(mesh):
    paired = mesh.shape["dp"] == 16 and mesh.shape["chan"] == 2
    rows = "dp"
    if paired:
        rows = ("far", "near", "y", "core")
        mesh = jax.sharding.Mesh(mesh.devices.reshape((2,) * 5), rows + ("chan",))
    canvas = P(rows, "chan", None)
    vector = P("chan")
    conv = P(None, "chan", None)
    matrix = P("chan", None)
    placed = (
        (canvas, P(rows, None, None), canvas)
        + (vector, vector, conv, vector, vector, vector, conv, vector, vector, vector)
        + (matrix, vector, matrix, matrix, vector, matrix, vector)
    )
    results = (
        (canvas, canvas, vector, vector, conv, vector, vector, vector, conv, vector)
        + (vector, vector, matrix, vector, matrix, matrix, vector, matrix, vector)
    )
    return jax.shard_map(functools.partial(body, paired), mesh=mesh, in_specs=placed, out_specs=results, check_vma=False)
```

```python
import functools
import itertools

import jax
import jax.numpy as jnp
import numpy as np
from jax import lax
from jax.experimental import pallas as pl
from jax.experimental.pallas import tpu as pltpu
from jax.sharding import PartitionSpec as P

CH = 512
GROUPS = 32
CROPS = 16
TILE = 8
BANDS = 4
EPS = 1e-06
F32 = jnp.float32
BF16 = jnp.bfloat16
HIGH = lax.Precision.HIGHEST
NN = (((1,), (0,)), ((), ()))
NT = (((1,), (1,)), ((), ()))
TN = (((0,), (0,)), ((), ()))
VMEM = pltpu.VMEM
ANY = pl.ANY
SCALE = CH ** (-0.5)


def band_layouts(units):
    return [
        tuple(np.diff((0,) + cuts + (units,)))
        for cuts in itertools.combinations(range(1, units), BANDS - 1)
    ]


PITCH = 8
QUERIES = 8
KEYS = 8


def window_cost(starts, sizes, slots):
    total = 0.0
    for block in range(0, slots, QUERIES):
        inside = [
            (starts <= at) & (at < starts + sizes) for at in (block, block + QUERIES - 1)
        ]
        low = (starts * inside[0]).sum(axis=-1) // 2 * 2
        high = ((starts + sizes) * inside[1]).sum(axis=-1)
        total = total + (high - low + KEYS - 1) // KEYS + 0.25
    return total


def best_starts(sizes, slots):
    layouts = sizes.shape[0]
    masks = np.arange(1 << (CROPS - 1), dtype=np.int32)
    bits = ((masks[None, :] >> np.arange(CROPS)[:, None]) & 1).astype(np.float32)
    picks = []
    for row in sizes.astype(np.float32):
        filled, squares = row @ bits, (row * row) @ bits
        cost = np.abs(squares - (row * row).sum() / 2) + 1e6 * np.abs(filled - slots)
        picks.append(bits[:, np.argpartition(cost, 4)[:4]].T)
        picks[-1] = picks[-1][(picks[-1] @ row) == slots]
        picks[-1] = picks[-1][np.arange(4) % len(picks[-1])]
    halves = np.array(picks, np.int32)
    halves = np.stack([1 - halves, halves], axis=2)
    held = halves * sizes[:, None, None, :]
    draw = np.random.RandomState(0)
    best = np.full((layouts, 4, 2), 1e9, np.float32)
    chosen = np.zeros(held.shape, np.int32)
    for trial in range(20):
        key = draw.rand(CROPS)[None, None, None, :] + 0.0 * held
        if trial == 0:
            key = -held + 0.01 * key
        elif trial < 8:
            key = key + 2.0 * (held % QUERIES != 0)
        order = np.argsort(key, axis=-1)
        ordered = np.take_along_axis(held, order, axis=-1)
        begin = np.cumsum(ordered, axis=-1) - ordered
        starts = np.zeros_like(held)
        np.put_along_axis(starts, order, begin, axis=-1)
        cost = window_cost(starts, held, slots)
        better = cost < best
        best = np.where(better, cost, best)
        chosen = np.where(better[..., None], starts, chosen)
    pick = np.argmin(best.max(axis=2), axis=1)
    rows = np.arange(layouts)
    owner, starts = halves[rows, pick, 1], chosen[rows, pick]
    return np.where(owner == 1, starts[:, 1] + slots, starts[:, 0])


@functools.lru_cache(maxsize=None)
def start_tables(devices, units, slots):
    layouts = band_layouts(units)
    rank = np.zeros(1 << (units - 1), np.int32)
    for number, sizes in enumerate(layouts):
        cuts = np.cumsum(sizes)[:-1]
        rank[sum(1 << (int(c) - 1) for c in cuts)] = number
    sizes = np.array(
        [[r * c for r in rows for c in cols] for rows in layouts for cols in layouts], np.int32
    )
    if devices == 2:
        starts = best_starts(sizes, slots)
    else:
        starts = np.zeros(sizes.shape, np.int32)
        for at, row in enumerate(sizes):
            loads = [0] * devices
            for crop in sorted(range(CROPS), key=lambda c: -row[c]):
                device = loads.index(min(loads))
                starts[at, crop] = device * slots + loads[device]
                loads[device] += int(row[crop])
    assert ((starts % slots) + sizes <= slots).all() and starts.max() < 256
    return rank, starts


def packed_tables(devices, units, slots):
    rank, starts = start_tables(devices, units, slots)
    shifts = np.arange(0, 32, 8, dtype=np.int64)
    words = (starts.reshape(-1, 4, 4).astype(np.int64) << shifts).sum(axis=2)
    words = np.where(words >= 1 << 31, words - (1 << 32), words)
    return np.concatenate([rank, words.reshape(-1).astype(np.int32)])


def write_plan(devices, slots, ids, table, slot_tile, slot_crop, starts, ends):
    units = ids.shape[0] // TILE
    count = units * units
    layouts = len(band_layouts(units))

    def code(at):
        bits = 0
        for step in range(units - 1):
            bits = bits + jnp.where(at(step) != at(step + 1), 1 << step, 0)
        return table[bits]

    def row_id(step):
        return ids[TILE * step, 0]

    def col_id(step):
        return ids[0, TILE * step]

    layout = code(row_id) * layouts + code(col_id)
    words = [table[(1 << (units - 1)) + 4 * layout + part] for part in range(4)]
    if devices * slots > count:

        def clear(at, carry):
            slot_tile[at] = -1
            slot_crop[at] = -1
            return carry

        lax.fori_loop(0, devices * slots, clear, 0)
    for crop in range(CROPS):
        start = lax.shift_right_logical(words[crop // 4], jnp.int32(8 * (crop % 4))) & 255
        starts[crop] = start
        ends[crop] = start

    def place(row, carry):
        for col in range(units):
            crop = ids[row * TILE, col * TILE]
            at = ends[crop]
            slot_tile[at] = row * units + col
            slot_crop[at] = crop
            ends[crop] = at + 1
        return carry

    lax.fori_loop(0, units, place, 0)


class Plan:
    def __init__(self, me, slot_tile, slot_crop, slots):
        self.slots = slots
        base = me * slots
        lane = lax.broadcasted_iota(jnp.int32, (1, 128), 1) % slots
        down = lax.broadcasted_iota(jnp.int32, (slots, 1), 0)
        self.tile_row, self.crop_row = jnp.zeros_like(lane), jnp.zeros_like(lane)
        self.tile_col, self.crop_col = jnp.zeros_like(down), jnp.zeros_like(down)
        for slot in range(slots):
            tile, crop = slot_tile[base + slot], slot_crop[base + slot]
            self.tile_row = jnp.where(lane == slot, tile, self.tile_row)
            self.crop_row = jnp.where(lane == slot, crop, self.crop_row)
            self.tile_col = jnp.where(down == slot, tile, self.tile_col)
            self.crop_col = jnp.where(down == slot, crop, self.crop_col)
        self.same = (self.crop_col == self.crop_row[:, 0:slots]).astype(F32)


def group_total(value):
    width = CH // GROUPS
    lane = lax.broadcasted_iota(jnp.int32, (value.shape[0], 128), 1)
    parts = []
    for at in range(0, value.shape[1], 128):
        part = value[:, at : at + 128]
        step = 1
        while step < width:
            up = pltpu.roll(part, 128 - step, 1)
            down = pltpu.roll(part, step, 1)
            part = part + jnp.where((lane & step) == 0, up, down)
            step *= 2
        parts.append(part)
    return jnp.concatenate(parts, axis=1)


def crop_mean(same, value):
    count = jnp.sum(same, axis=1, keepdims=True) * float(TILE * TILE * (CH // GROUPS))
    total = lax.dot_general(same, group_total(value), NN, precision=HIGH, preferred_element_type=F32)
    return total / count


def lanes_of(width):
    return [slice(at, at + 128) for at in range(0, width, 128)]


def slab_sum(pixels, slots, width, term):
    parts = []
    for lanes in lanes_of(width):

        def step(at, total):
            return total + term(at, lanes)

        parts.append(lax.fori_loop(0, pixels, step, jnp.zeros((slots, 128), F32), unroll=8))
    return jnp.concatenate(parts, axis=1)


def slab_stats(pixels, slots, slab, same):
    mean = crop_mean(same, slab_sum(pixels, slots, CH, slab))

    def square(at, lanes):
        centred = slab(at, lanes) - mean[:, lanes]
        return centred * centred

    return mean, lax.rsqrt(crop_mean(same, slab_sum(pixels, slots, CH, square)) + EPS)


def sigmoid(value):
    return 0.5 * jnp.tanh(0.5 * value) + 0.5


def fill_halo(pad, plan):
    slots = plan.slots
    wide = TILE * slots
    tile_c = jnp.concatenate([plan.tile_col] * TILE, axis=0)
    crop_c = jnp.concatenate([plan.crop_col] * TILE, axis=0)
    tile_r = jnp.concatenate([plan.tile_row] * (wide // 128), axis=1)
    crop_r = jnp.concatenate([plan.crop_row] * (wide // 128), axis=1)
    block_c = lax.broadcasted_iota(jnp.int32, (wide, wide), 0) // slots
    block_r = lax.broadcasted_iota(jnp.int32, (wide, wide), 1) // slots
    linked = (crop_c == crop_r) & (tile_c >= 0)

    def near(row_step, col_step):
        return linked & (tile_r == tile_c + (TILE * row_step + col_step))

    def edge(row_step, col_step, source):
        pick = (near(row_step, col_step) & (block_c == block_r)).astype(F32).astype(BF16)
        moved = jnp.dot(pick, source.reshape(wide, CH), preferred_element_type=F32).astype(BF16)
        return moved.reshape(TILE, slots, CH)

    def corner(row_step, col_step, source):
        pick = near(row_step, col_step)[0:slots, 0:slots].astype(F32).astype(BF16)
        return jnp.dot(pick, source, preferred_element_type=F32).astype(BF16)

    low, high, end = 1, TILE, TILE + 1
    pad[0, low:end] = edge(-1, 0, pad[high, low:end])
    pad[end, low:end] = edge(1, 0, pad[low, low:end])
    pad[low:end, 0] = edge(0, -1, pad[low:end, high])
    pad[low:end, end] = edge(0, 1, pad[low:end, low])
    pad[0, 0] = corner(-1, -1, pad[high, high])
    pad[0, end] = corner(-1, 1, pad[high, low])
    pad[end, 0] = corner(1, -1, pad[low, high])
    pad[end, end] = corner(1, 1, pad[low, low])


class WeightLoad:
    def __init__(self, position, pieces, target, sem, columns=None):
        self.copies = []
        views = [(pieces[0], None)]
        if len(pieces) > 1:
            me, core = position[0], position[1]
            half = pieces[0].shape[1]
            views = [(pieces[0], me * half)]
            part = half // (len(pieces) - 1)
            for number, piece in enumerate(pieces[1:]):
                spot = (1 - me) * half
                if len(pieces) == 3:
                    spot = spot + (core ^ number) * part
                if len(piece.shape) == 3:
                    views.append((piece, spot))
                    continue
                for at in range(piece.shape[0]):
                    views.append((piece.at[at], spot + at * piece.shape[2]))
        for at, (piece, spot) in enumerate(views):
            width = piece.shape[1]
            rows = slice(None)
            if spot is not None:
                rows = pl.ds(pl.multiple_of(spot, 32), width)
            if columns is not None:
                piece = piece.at[:, :, columns]
            self.copies.append(pltpu.make_async_copy(piece, target.at[:, rows, :], sem.at[at]))

    def start(self):
        for copy in self.copies:
            copy.start()

    def wait(self):
        for copy in self.copies:
            copy.wait()


def weight_sems(pieces):
    return pltpu.SemaphoreType.DMA((9,))


BLOCK = CH // 16


def store_grad(grad, outs, work, position, unit, first, count, front=True):
    if len(outs) == 1:
        outs[0][unit] = grad.astype(BF16)
        return
    work[...] = grad
    me, core, quad = position[0], position[1], position[2]
    for half, out in enumerate(outs):
        for c in range(2):
            for q in range(4):
                row = (me ^ c) * (CH // 2) + (core ^ half) * (CH // 4) + (quad ^ q) * BLOCK
                part = work[pl.ds(pl.multiple_of(row, BLOCK), BLOCK), :]
                if front:
                    to = ((c * 4 + q) * first + unit) * BLOCK
                else:
                    to = (8 * first + (q * 2 + c) * (count - first) + unit - first) * BLOCK
                out[pl.ds(pl.multiple_of(to, BLOCK), BLOCK), :] = part.astype(BF16)


def store_vectors(vecs, out, me):
    if len(out.shape) == 2:
        out[...] = vecs[...]
    else:
        half = out.shape[2]
        out[0] = vecs[:, pl.ds(pl.multiple_of(me * half, half), half)]
        out[1] = vecs[:, pl.ds(pl.multiple_of((1 - me) * half, half), half)]


def vector_shape(paired):
    return shape((2, 16, CH // 2) if paired else (16, CH), F32)


def grad_shapes(count, paired):
    if paired:
        return [shape((8 * count * BLOCK, CH), BF16)] * 2
    return [shape((count, CH, CH), BF16)]


def conv_rows(pad, weight, row, slots, dims, flipped, count=1):
    total = None
    for tap in range(9):
        down, right = tap // 3, tap % 3
        if flipped:
            down, right = 2 - down, 2 - right
        left = pad[pl.ds(row + down, count), right : right + TILE].reshape(count * TILE * slots, CH)
        part = lax.dot_general(left, weight[tap], dims, preferred_element_type=F32)
        total = part if total is None else total + part
    return total


def load_full(parts, me, dtype, store):
    if len(parts) == 1:
        store(slice(None), parts[0][...].astype(dtype))
    else:
        local = parts[0].shape[-1]
        own = pl.ds(pl.multiple_of(me * local, local), local)
        other = pl.ds(pl.multiple_of((1 - me) * local, local), local)
        store(own, parts[0][...].astype(dtype))
        store(other, parts[1][...].astype(dtype))


def vmem(shape, dtype):
    return pltpu.VMEM(shape, dtype)


def specs(kinds):
    table = {
        "v": pl.BlockSpec(memory_space=pltpu.VMEM),
        "s": pl.BlockSpec(memory_space=pltpu.SMEM),
        "h": pl.BlockSpec(memory_space=pl.ANY),
    }
    return [table[k] for k in kinds]


ROOM = {
    "unpack_output": 18,
    "unpack_input_grad": 18,
    "conv2_weight_grad": 24,
    "conv1_weight_grad": 22,
    "conv2_input_grad": 24,
    "conv1_input_grad": 20,
    "conv2_grads": 16,
    "conv1_grads": 14,
}


def call(body, ins, outs, shapes, scratch, name, flops, moved):
    return pl.pallas_call(
        body,
        in_specs=specs(ins),
        out_specs=tuple(specs(outs)),
        out_shape=tuple(shapes),
        scratch_shapes=list(scratch),
        compiler_params=pltpu.CompilerParams(vmem_limit_bytes=ROOM.get(name, 60) << 20),
        cost_estimate=pl.CostEstimate(
            flops=int(flops), bytes_accessed=int(moved), transcendentals=0
        ),
        name=name,
    )


def shape(dims, dtype):
    return jax.ShapeDtypeStruct(dims, dtype)


def pack_first_kernel(devices, slots, position, ids, table, signal, *rest):
    plan, rest = rest[:4], rest[4:]
    write_plan(devices, slots, ids, table, *plan)
    pack_kernel(True, slots, position, plan[0], signal, *rest)


def pack_kernel(by_pixel, slots, position, slot_tile, signal, *rest):
    outs, (raster, stage) = rest[:-2], rest[-2:]
    local, pixels = signal.shape
    side = int(pixels**0.5)
    chunk = 512
    cols = local // 128
    for at in range(0, pixels, chunk):
        flipped = signal[:, at : at + chunk].astype(F32).T
        for col in range(cols):
            raster[col, at : at + chunk, :] = flipped[:, col * 128 : (col + 1) * 128]
    for number, out in enumerate(outs):

        def step(slot, carry):
            tile = slot_tile[pack_base(position, number, len(outs), slots) + slot]
            keep = tile >= 0
            tile = jnp.maximum(tile, 0)
            start = (tile // TILE) * (TILE * side) + (tile % TILE) * TILE
            for row in range(TILE):
                for col in range(cols):
                    value = raster[col, pl.ds(pl.multiple_of(start + row * side, TILE), TILE), :]
                    value = jnp.where(keep, value, 0.0)
                    if by_pixel:
                        pitch = slots + PITCH
                        to = pl.ds(row * TILE * pitch + slot, TILE, stride=pitch)
                        stage[col, to, :] = value
                    else:
                        at = pl.multiple_of(slot * (TILE * TILE) + row * TILE, TILE)
                        stage[col, pl.ds(at, TILE), :] = value
            return carry

        lax.fori_loop(0, slots, step, 0)
        size = slots if by_pixel else TILE * TILE
        pitch = size + PITCH if by_pixel else size
        for number in range(out.shape[0] // size):
            for col in range(cols):
                span = slice(col * 128, (col + 1) * 128)
                value = stage[col, number * pitch : number * pitch + size, :]
                out[number * size : (number + 1) * size, span] = value.astype(BF16)


def pack_base(position, number, devices, slots):
    return (position[0] ^ number if devices == 2 else number) * slots


def pack_scratch(local, pixels, slots):
    rows = TILE * TILE * (slots + PITCH)
    return [vmem((local // 128, pixels, 128), F32), vmem((local // 128, rows, 128), F32)]


def pack_first(position, ids, signal, devices, slots, name):
    local, pixels = signal.shape
    rows = slots * TILE * TILE
    table = jnp.asarray(packed_tables(devices, ids.shape[0] // TILE, slots))
    result = call(
        functools.partial(pack_first_kernel, devices, slots),
        "sssv",
        "ssss" + "v" * devices,
        [shape((devices * slots,), jnp.int32)] * 2
        + [shape((CROPS,), jnp.int32)] * 2
        + [shape((rows, local), BF16)] * devices,
        pack_scratch(local, pixels, slots),
        name,
        4 << 30,
        6 << 20,
    )(position, ids, table, signal)
    return result[:4], result[4:]


def pack(position, slot_tile, signal, by_pixel, devices, slots, name):
    local, pixels = signal.shape
    rows = slots * TILE * TILE
    return call(
        functools.partial(pack_kernel, by_pixel, slots),
        "ssv",
        "v" * devices,
        [shape((rows, local), BF16)] * devices,
        pack_scratch(local, pixels, slots),
        name,
        40 << 30,
        6 << 20,
    )(position, slot_tile, signal)


def unpack_kernel(by_pixel, slots, position, slot_tile, *rest):
    ins, out, (raster, stage) = rest[:-3], rest[-3], rest[-2:]
    local, pixels = out.shape
    side = int(pixels**0.5)
    chunk = 512
    cols = local // 128
    for number, part in enumerate(ins):
        size = slots if by_pixel else TILE * TILE
        pitch = size + PITCH if by_pixel else size
        for at in range(part.shape[0] // size):
            for col in range(cols):
                span = slice(col * 128, (col + 1) * 128)
                value = part[at * size : (at + 1) * size, span]
                stage[col, at * pitch : at * pitch + size, :] = value.astype(F32)

        def step(slot, carry):
            tile = slot_tile[pack_base(position, number, len(ins), slots) + slot]

            @pl.when(tile >= 0)
            def _():
                start = (tile // TILE) * (TILE * side) + (tile % TILE) * TILE
                for row in range(TILE):
                    to = pl.ds(pl.multiple_of(start + row * side, TILE), TILE)
                    for col in range(cols):
                        if by_pixel:
                            at = pl.ds(row * TILE * pitch + slot, TILE, stride=pitch)
                        else:
                            first = pl.multiple_of(slot * (TILE * TILE) + row * TILE, TILE)
                            at = pl.ds(first, TILE)
                        raster[col, to, :] = stage[col, at, :]

            return carry

        lax.fori_loop(0, slots, step, 0)
    for at in range(0, pixels, chunk):
        for col in range(cols):
            span = slice(col * 128, (col + 1) * 128)
            out[span, at : at + chunk] = raster[col, at : at + chunk, :].T.astype(out.dtype)


def unpack(position, slot_tile, parts, pixels, by_pixel, dtype, slots, name):
    rows, local = parts[0].shape
    return call(
        functools.partial(unpack_kernel, by_pixel, slots),
        "ss" + "v" * len(parts),
        "v",
        [shape((local, pixels), dtype)],
        pack_scratch(local, pixels, slots),
        name,
        4 << 30,
        8 << 20,
    )(position, slot_tile, *parts)[0]


(G1, B1, C1, G2, B2, C2, G3, B3, QB, VB, PB) = range(11)


def norm_swish_pad(slab, mean, inverse, gain, bias, pad, copy=None):
    scaled = inverse * gain
    for lanes in lanes_of(CH):
        centre, factor, offset = mean[:, lanes], scaled[:, lanes], bias[:, lanes]

        def step(row, carry):
            for col in range(TILE):
                value = slab(row * TILE + col, lanes)
                before = (value - centre) * factor + offset
                pad[row + 1, col + 1, :, lanes] = (before * sigmoid(before)).astype(BF16)
                if copy is not None:
                    copy[row * TILE + col, :, lanes] = value.astype(BF16)
            return carry

        lax.fori_loop(0, TILE, step, 0)


def first_kernel(parts, count, position, slot_tile, slot_crop, *rest):
    feature_parts, rest = rest[:parts], rest[parts:]
    par_parts, rest = rest[:parts], rest[parts:]
    pieces, rest = rest[:count], rest[count:]
    (par, feats_hbm, pad1_hbm, hidden_hbm, pad2_hbm, stats1, stats2) = rest[:7]
    feats, rounded, hidden, pad1, pad2, weight, weight_sem, sem = rest[7:]
    pixels, slots, _ = hidden.shape
    load_weight = WeightLoad(position, pieces, weight, weight_sem)
    load_weight.start()

    def put_par(columns, value):
        par[:, columns] = value

    load_full(par_parts, position[0], F32, put_par)

    def put(columns, value):
        feats[:, columns] = value

    load_full(feature_parts, position[0], BF16, put)
    save_feats = pltpu.make_async_copy(feats, feats_hbm, sem.at[1])
    save_feats.start()

    plan = Plan(position[0], slot_tile, slot_crop, slots)

    def slab1(at, lanes):
        return feats[pl.ds(pl.multiple_of(at * slots, slots), slots), lanes].astype(F32)

    mean, inverse = slab_stats(pixels, slots, slab1, plan.same)
    stats1[0], stats1[1] = mean, inverse
    norm_swish_pad(slab1, mean, inverse, par[G1 : G1 + 1, :], par[B1 : B1 + 1, :], pad1)
    fill_halo(pad1, plan)
    save_pad1 = pltpu.make_async_copy(pad1, pad1_hbm, sem.at[2])
    save_pad1.start()
    load_weight.wait()

    def step(row, carry):
        total = conv_rows(pad1, weight, row, slots, NT, False) + par[C1 : C1 + 1, :]
        hidden[pl.ds(row * TILE, TILE)] = total.reshape(TILE, slots, CH)
        return carry

    lax.fori_loop(0, TILE, step, 0)

    def slab2(at, lanes):
        return hidden[at, :, lanes]

    mean, inverse = slab_stats(pixels, slots, slab2, plan.same)
    stats2[0], stats2[1] = mean, inverse
    norm_swish_pad(
        slab2, mean, inverse, par[G2 : G2 + 1, :], par[B2 : B2 + 1, :], pad2, rounded
    )
    save_hidden = pltpu.make_async_copy(rounded, hidden_hbm, sem.at[3])
    save_hidden.start()
    fill_halo(pad2, plan)
    save_pad2 = pltpu.make_async_copy(pad2, pad2_hbm, sem.at[4])
    save_pad2.start()
    save_feats.wait()
    save_pad1.wait()
    save_hidden.wait()
    save_pad2.wait()


def first(position, tables, par_parts, parts, weight, slots):
    pixels = TILE * TILE
    rows = pixels * slots
    pad = (TILE + 2, TILE + 2, slots, CH)
    return call(
        functools.partial(first_kernel, len(parts), len(weight)),
        "sss" + "v" * len(parts) + "v" * len(parts) + "h" * len(weight),
        "vhhhhvv",
        [
            shape((16, CH), F32),
            shape((rows, CH), BF16),
            shape(pad, BF16),
            shape((pixels, slots, CH), BF16),
            shape(pad, BF16),
            shape((2, slots, CH), F32),
            shape((2, slots, CH), F32),
        ],
        [
            vmem((rows, CH), BF16),
            vmem((pixels, slots, CH), BF16),
            vmem((pixels, slots, CH), F32),
            vmem(pad, BF16),
            vmem(pad, BF16),
            vmem((9, CH, CH), BF16),
            weight_sems(weight),
            pltpu.SemaphoreType.DMA((5,)),
        ],
        "conv1_forward",
        2 * rows * CH * CH * 9,
        20 << 20,
    )(position, *tables[:2], *parts, *par_parts, *weight)


def second_kernel(count, position, slot_tile, slot_crop, par, feats, pad_hbm, *rest):
    pieces, rest = rest[:count], rest[count:]
    resid_hbm, normed_hbm, stats3 = rest[:3]
    resid, resid_tile, normed, pad, weight, rows_scr, weight_sem, sem = rest[3:]
    slots = pad.shape[2]
    pixels = TILE * TILE
    load_pad = pltpu.make_async_copy(pad_hbm, pad, sem.at[0])
    load_weight = WeightLoad(position, pieces, weight, weight_sem)
    load_pad.start()
    load_weight.start()
    plan = Plan(position[0], slot_tile, slot_crop, slots)
    same = plan.same
    load_pad.wait()
    load_weight.wait()
    wide = TILE * slots

    def step(row, carry):
        at = pl.ds(pl.multiple_of(row * wide, wide), wide)
        total = conv_rows(pad, weight, row, slots, NT, False) + par[C2 : C2 + 1, :]
        total = total + feats[at, :].astype(F32)
        for col in range(CH // 128):
            for x in range(TILE):
                to = pl.multiple_of((row * TILE + x) * (slots + PITCH), 8)
                part = total[x * slots : (x + 1) * slots, col * 128 : (col + 1) * 128]
                resid[col, pl.ds(to, slots), :] = part
        return carry

    lax.fori_loop(0, TILE, step, 0)

    def slab(at, lanes):
        begin = pl.multiple_of(at * (slots + PITCH), 8)
        return resid[lanes.start // 128, pl.ds(begin, slots), :]

    mean, inverse = slab_stats(pixels, slots, slab, same)
    stats3[0], stats3[1] = mean, inverse
    rows_scr[0], rows_scr[1] = mean, inverse * par[G3 : G3 + 1, :]
    bias = par[B3 : B3 + 1, :]

    def tile_step(slot, carry):
        at = pl.ds(pl.multiple_of(slot * pixels, pixels), pixels)
        centre, factor = rows_scr[0, pl.ds(slot, 1)], rows_scr[1, pl.ds(slot, 1)]
        for col, lanes in enumerate(lanes_of(CH)):
            value = resid[col, pl.ds(slot, pixels, stride=slots + PITCH), :]
            resid_tile[at, lanes] = value.astype(BF16)
            scaled = (value - centre[:, lanes]) * factor[:, lanes]
            normed[at, lanes] = (scaled + bias[:, lanes]).astype(BF16)
        return carry

    lax.fori_loop(0, slots, tile_step, 0, unroll=2)
    save_resid = pltpu.make_async_copy(resid_tile, resid_hbm, sem.at[2])
    save_normed = pltpu.make_async_copy(normed, normed_hbm, sem.at[3])
    save_resid.start()
    save_normed.start()
    save_resid.wait()
    save_normed.wait()


def second(position, tables, par, feats, pad, weight, slots):
    pixels = TILE * TILE
    rows = pixels * slots
    return call(
        functools.partial(second_kernel, len(weight)),
        "sssvvh" + "h" * len(weight),
        "hhv",
        [shape((rows, CH), BF16), shape((rows, CH), BF16), shape((2, slots, CH), F32)],
        [
            vmem((CH // 128, pixels * (slots + PITCH), 128), F32),
            vmem((rows, CH), BF16),
            vmem((rows, CH), BF16),
            vmem(pad.shape, BF16),
            vmem((9, CH, CH), BF16),
            vmem((2, slots, CH), F32),
            weight_sems(weight),
            pltpu.SemaphoreType.DMA((4,)),
        ],
        "conv2_forward",
        2 * rows * CH * CH * 9,
        16 << 20,
    )(position, *tables[:2], par, feats, pad, *weight)


def attention_kernel(parts, outs, count, position, slot_tile, slot_crop, starts, ends, *rest):
    par, normed, resid_hbm, stats3 = rest[:4]
    tangent_parts, rest = rest[4 : 4 + parts], rest[4 + parts :]
    pieces, rest = rest[:count], rest[count:]
    out_hbm, rest = rest[:outs], rest[outs:]
    grads_hbm, rest = rest[:outs], rest[outs:]
    vecs_out, pad = rest[:2]
    (tangent, query, key, value, mixed_grad, mixed, query_grad, key_grad, value_grad) = rest[2:11]
    normed_grad, by_tile, rows_scr, weight, key_crop, work, vecs = rest[11:18]
    scores_scr, prob_grads, sums, weight_sem, sem, resid = rest[18:24]
    grad_outs = rest[24:]
    load_weight = WeightLoad(position, pieces, weight, weight_sem)
    load_weight.start()
    wq, wk, wv, wp = (weight.at[k] for k in range(4))
    rows = normed.shape[0]
    pixels = TILE * TILE
    slots = rows // pixels
    me = position[0]
    base = me * slots
    per_block = QUERIES
    block = per_block * pixels
    plan = Plan(me, slot_tile, slot_crop, slots)
    lane_slot = lax.broadcasted_iota(jnp.int32, (1, rows), 1) // pixels
    crops = jnp.zeros((1, rows), jnp.int32)
    for slot in range(slots):
        crops = jnp.where(lane_slot == slot, slot_crop[base + slot], crops)
    key_crop[...] = crops

    half = CH // outs
    columns = [pl.ds(0, CH)]
    if outs == 2:
        columns = [pl.ds(pl.multiple_of((me ^ k) * half, half), half) for k in range(2)]
    load_tangent = [
        pltpu.make_async_copy(part, tangent.at[:, columns[k]], sem.at[k])
        for k, part in enumerate(tangent_parts)
    ]
    load_resid = pltpu.make_async_copy(resid_hbm, resid, sem.at[2])
    save_out = [
        pltpu.make_async_copy(query.at[:, columns[k]], part, sem.at[3 + k])
        for k, part in enumerate(out_hbm)
    ]
    save_grads = [
        pltpu.make_async_copy(part, grads_hbm[k], sem.at[5 + k])
        for k, part in enumerate(grad_outs)
    ]
    for copy in load_tangent + [load_resid]:
        copy.start()
    load_weight.wait()
    for copy in load_tangent:
        copy.wait()

    def project(at, carry):
        span = pl.ds(pl.multiple_of(at * block, block), block)
        left = normed[span, :]
        total = lax.dot_general(left, wq[...], NT, preferred_element_type=F32)
        query[span, :] = (total + par[QB : QB + 1, :]).astype(BF16)
        key[span, :] = lax.dot_general(left, wk[...], NT, preferred_element_type=F32).astype(BF16)
        total = lax.dot_general(left, wv[...], NT, preferred_element_type=F32)
        value[span, :] = (total + par[VB : VB + 1, :]).astype(BF16)
        mixed_grad[span, :] = jnp.dot(
            tangent[span, :], wp[...], preferred_element_type=F32
        ).astype(BF16)
        key_grad[span, :] = jnp.zeros((block, CH), F32)
        value_grad[span, :] = jnp.zeros((block, CH), F32)
        return carry

    lax.fori_loop(0, rows // block, project, 0)

    def attend_step(at, carry):
        span = pl.ds(pl.multiple_of(at * block, block), block)
        low_crop = slot_crop[base + at * per_block]
        high_crop = slot_crop[base + at * per_block + per_block - 1]
        low = starts[jnp.maximum(low_crop, 0)] - base
        low = jnp.where(low_crop < 0, at * per_block, low) // 2 * 2
        high = jnp.where(high_crop < 0, slots, ends[jnp.maximum(high_crop, 0)] - base)
        count = (high - low + KEYS - 1) // KEYS
        begin = jnp.minimum(low, slots - KEYS * count) * pixels
        down = lax.broadcasted_iota(jnp.int32, (block, 1), 0) // pixels
        own_crop = jnp.zeros((block, 1), jnp.int32)
        for slot in range(per_block):
            own_crop = jnp.where(down == slot, slot_crop[base + at * per_block + slot], own_crop)

        def keys_of(number):
            return pl.ds(pl.multiple_of(begin + number * (KEYS * pixels), 128), KEYS * pixels)

        def score(number, top):
            keys = keys_of(number)
            scores = lax.dot_general(
                query[span, :], key[keys, :], NT, preferred_element_type=F32
            )
            scores = jnp.where(own_crop == key_crop[:, keys], scores * SCALE, -1e30)
            scores_scr[number] = scores
            prob_grads[number] = lax.dot_general(
                mixed_grad[span, :], value[keys, :], NT, preferred_element_type=F32
            )
            return jnp.maximum(top, jnp.max(scores, axis=1, keepdims=True))

        top = lax.fori_loop(0, count, score, jnp.full((block, 1), -1e30, F32))

        def weigh(number, carry):
            total, inner = carry
            exponent = jnp.exp(scores_scr[number] - top)
            scores_scr[number] = exponent
            total += jnp.sum(exponent, axis=1, keepdims=True)
            inner += jnp.sum(exponent * prob_grads[number], axis=1, keepdims=True)
            return total, inner

        zero = jnp.zeros((block, 1), F32)
        total, inner = lax.fori_loop(0, count, weigh, (zero, zero))
        share = 1.0 / total
        inner = inner * share
        sums[...] = jnp.zeros_like(sums)

        def spread_back(number, carry):
            keys = keys_of(number)
            prob = scores_scr[number] * share
            rounded = prob.astype(BF16)
            score_grad = (prob * (prob_grads[number] - inner)).astype(BF16)
            sums[0] += jnp.dot(rounded, value[keys, :], preferred_element_type=F32)
            sums[1] += jnp.dot(score_grad, key[keys, :], preferred_element_type=F32)
            key_grad[keys, :] += lax.dot_general(
                score_grad, query[span, :], TN, preferred_element_type=F32
            )
            value_grad[keys, :] += lax.dot_general(
                rounded, mixed_grad[span, :], TN, preferred_element_type=F32
            )
            return carry

        lax.fori_loop(0, count, spread_back, 0)
        mixed[span, :] = sums[0].astype(BF16)
        query_grad[span, :] = (sums[1] * SCALE).astype(BF16)
        return carry

    lax.fori_loop(0, rows // block, attend_step, 0)

    def back(at, carry):
        query_bias, value_bias, tangent_sum = carry
        span = pl.ds(pl.multiple_of(at * block, block), block)
        dq = query_grad[span, :]
        dk = (key_grad[span, :] * SCALE).astype(BF16)
        dv = value_grad[span, :].astype(BF16)
        key[span, :] = dk
        value[span, :] = dv
        total = jnp.dot(dq, wq[...], preferred_element_type=F32)
        total += jnp.dot(dk, wk[...], preferred_element_type=F32)
        total += jnp.dot(dv, wv[...], preferred_element_type=F32)
        normed_grad[span, :] = total
        result = lax.dot_general(mixed[span, :], wp[...], NT, preferred_element_type=F32)
        result = (result + par[PB : PB + 1, :] + resid[span, :].astype(F32)).astype(BF16)
        query[span, :] = result
        query_bias += jnp.sum(dq.astype(F32), axis=0, keepdims=True)
        value_bias += jnp.sum(dv.astype(F32), axis=0, keepdims=True)
        tangent_sum += jnp.sum(tangent[span, :].astype(F32), axis=0, keepdims=True)
        return query_bias, value_bias, tangent_sum

    load_resid.wait()
    zero = jnp.zeros((1, CH), F32)
    query_bias, value_bias, tangent_sum = lax.fori_loop(
        0, rows // block, back, (zero, zero, zero)
    )
    for copy in save_out:
        copy.start()
    left = normed[...]
    for number, grad in enumerate((query_grad, key, value)):
        total = lax.dot_general(grad[...], left, TN, preferred_element_type=F32)
        store_grad(total, grad_outs, work, position, number, 4, 4)
    total = lax.dot_general(tangent[...], mixed[...], TN, preferred_element_type=F32)
    store_grad(total, grad_outs, work, position, 3, 4, 4)
    for copy in save_grads:
        copy.start()

    def tile_sums(slot, carry):
        span = pl.ds(pl.multiple_of(slot * pixels, pixels), pixels)
        row = pl.ds(slot, 1)
        centre, factor = stats3[0, row], stats3[1, row]
        plains, crosseds = [], []
        for lanes in lanes_of(CH):
            upstream = normed_grad[span, lanes]
            hat = (resid[span, lanes].astype(F32) - centre[:, lanes]) * factor[:, lanes]
            plains.append(jnp.sum(upstream, axis=0, keepdims=True))
            crosseds.append(jnp.sum(upstream * hat, axis=0, keepdims=True))
        rows_scr[0, row] = jnp.concatenate(plains, axis=1)
        rows_scr[1, row] = jnp.concatenate(crosseds, axis=1)
        return carry

    lax.fori_loop(0, slots, tile_sums, 0)
    same = plan.same
    gain = par[G3 : G3 + 1, :]
    plain, crossed = rows_scr[0], rows_scr[1]
    vecs[...] = jnp.zeros_like(vecs)
    vecs[G3 : G3 + 1, :] = jnp.sum(crossed, axis=0, keepdims=True)
    vecs[B3 : B3 + 1, :] = jnp.sum(plain, axis=0, keepdims=True)
    vecs[QB : QB + 1, :] = query_bias
    vecs[VB : VB + 1, :] = value_bias
    vecs[PB : PB + 1, :] = tangent_sum
    rows_scr[0] = crop_mean(same, plain * gain)
    rows_scr[1] = crop_mean(same, crossed * gain)

    def apply(slot, carry):
        span = pl.ds(pl.multiple_of(slot * pixels, pixels), pixels)
        padded = pl.ds(pl.multiple_of(slot * (pixels + PITCH), 8), pixels)
        row = pl.ds(slot, 1)
        centre, factor = stats3[0, row], stats3[1, row]
        slope = factor * gain
        level = factor * rows_scr[0, row]
        tilt = factor * factor * rows_scr[1, row]
        for col, lanes in enumerate(lanes_of(CH)):
            centred = resid[span, lanes].astype(F32) - centre[:, lanes]
            grad = normed_grad[span, lanes] * slope[:, lanes] - level[:, lanes]
            grad = grad - centred * tilt[:, lanes]
            by_tile[col, padded, :] = tangent[span, lanes].astype(F32) + grad
        return carry

    lax.fori_loop(0, slots, apply, 0)

    def spread(row, carry):
        total = carry
        for col in range(TILE):
            at = row * TILE + col
            slab = jnp.concatenate(
                [
                    by_tile[c, pl.ds(at, slots, stride=pixels + PITCH), :] for c in range(CH // 128)
                ],
                axis=1,
            )
            rounded = slab.astype(BF16)
            pad[row + 1, col + 1] = rounded
            total += jnp.sum(rounded.astype(F32), axis=0, keepdims=True)
        return total

    vecs[C2 : C2 + 1, :] = lax.fori_loop(0, TILE, spread, zero)
    store_vectors(vecs, vecs_out, me)
    fill_halo(pad, plan)
    for copy in save_out + save_grads:
        copy.wait()


def attention(position, tables, par, normed, resid, stats3, tangent_parts, weight, slots):
    pixels = TILE * TILE
    rows = pixels * slots
    parts = len(tangent_parts)
    pad = (TILE + 2, TILE + 2, slots, CH)
    if parts == 2:
        out_shapes = [shape((rows, CH // 2), BF16)] * 2
    else:
        out_shapes = [shape((rows, CH), BF16)]
    outs = len(out_shapes)
    result = call(
        functools.partial(attention_kernel, parts, outs, len(weight)),
        "sssssvvhv" + "h" * parts + "h" * len(weight),
        "h" * (2 * outs) + "vv",
        out_shapes
        + grad_shapes(4, outs == 2)
        + [vector_shape(outs == 2), shape(pad, BF16)],
        [vmem((rows, CH), BF16)] * 7
        + [vmem((rows, CH), F32)] * 3
        + [vmem((CH // 128, slots * (pixels + PITCH), 128), F32), vmem((2, slots, CH), F32)]
        + [vmem((4, CH, CH), BF16), vmem((1, rows), jnp.int32), vmem((CH, CH), F32)]
        + [vmem((16, CH), F32)]
        + [vmem((slots // KEYS, QUERIES * pixels, KEYS * pixels), F32)] * 2
        + [vmem((2, QUERIES * pixels, CH), F32)]
        + [weight_sems(weight), pltpu.SemaphoreType.DMA((7,)), vmem((rows, CH), BF16)]
        + [vmem(part.shape, BF16) for part in grad_shapes(4, outs == 2)],
        "attention",
        30 << 30,
        24 << 20,
    )(
        position,
        *tables,
        par,
        normed,
        resid,
        stats3,
        *tangent_parts,
        *weight,
    )
    return result[:outs], result[outs : 2 * outs], result[2 * outs :]


def weight_grad_kernel(paired, first, extra, position, active, grad, *rest):
    outs = 2 if paired else 1
    extras, rest = rest[: outs if extra else 0], rest[outs if extra else 0 :]
    out_parts, (flipped, work, sem) = rest[:outs], rest[outs:]
    copies = []
    for half, part in enumerate(extras):
        for at in range(8):
            source = part.at[pl.ds(at * extra * BLOCK, extra * BLOCK)]
            target = out_parts[half].at[pl.ds(at * first * BLOCK, extra * BLOCK)]
            copies.append(pltpu.make_async_copy(source, target, sem.at[half, at]))
    for copy in copies:
        copy.start()
    slots = active.shape[2]
    wide = TILE * slots
    for row in range(TILE):
        left = grad[row + 1, 1 : TILE + 1].reshape(wide, CH)
        flipped[:, row * wide : (row + 1) * wide] = left.T

    def step(front, tap, carry):
        right = active[pl.ds(tap // 3, TILE), pl.ds(tap % 3, TILE)].reshape(TILE * wide, CH)
        total = jnp.dot(flipped[...], right, preferred_element_type=F32)
        store_grad(total, out_parts, work, position, tap + extra, first, 9 + extra, front)
        return carry

    if first > extra:
        lax.fori_loop(0, first - extra, functools.partial(step, True), 0)
    if first - extra < 9:
        lax.fori_loop(first - extra, 9, functools.partial(step, False), 0)
    for copy in copies:
        copy.wait()


def weight_grad(position, active, grad, paired, slots, name, first=9, extras=()):
    rows = TILE * TILE * slots
    extra = 4 if extras else 0
    shapes = grad_shapes(9 + extra, paired)
    return call(
        functools.partial(weight_grad_kernel, paired, first, extra),
        "svv" + "h" * len(extras),
        "v" * len(shapes),
        shapes,
        [
            vmem((CH, rows), BF16),
            vmem((CH, CH), F32),
            pltpu.SemaphoreType.DMA((2, 8)),
        ],
        name,
        2 * rows * CH * CH * 9,
        12 << 20,
    )(position, active, grad, *extras)


def swish_back(upstream, before):
    gate = sigmoid(before)
    return upstream * (gate + before * gate * (1.0 - gate))


def norm_back_sums(source, upstream, mean, inverse, gain, bias, slots):
    plains, crosseds = [], []
    for lanes in lanes_of(upstream.shape[2]):
        centre, factor = mean[:, lanes], inverse[:, lanes]
        slope, offset = gain[:, lanes], bias[:, lanes]

        def step(at, carry):
            plain, crossed = carry
            hat = (source(at, lanes) - centre) * factor
            grad = swish_back(upstream[at, :, lanes], hat * slope + offset)
            upstream[at, :, lanes] = grad
            return plain + grad, crossed + grad * hat

        zero = jnp.zeros((slots, 128), F32)
        plain, crossed = lax.fori_loop(0, TILE * TILE, step, (zero, zero), unroll=4)
        plains.append(plain)
        crosseds.append(crossed)
    return jnp.concatenate(plains, axis=1), jnp.concatenate(crosseds, axis=1)


def norm_back_apply(source, upstream, mean, inverse, gain, plain, crossed, put):
    for lanes in lanes_of(upstream.shape[2]):
        centre, factor = mean[:, lanes], inverse[:, lanes]
        slope = factor * gain[:, lanes]
        level = factor * plain[:, lanes]
        tilt = factor * factor * crossed[:, lanes]

        def step(at, carry):
            centred = source(at, lanes) - centre
            put(at, lanes, upstream[at, :, lanes] * slope - level - centred * tilt)
            return carry

        lax.fori_loop(0, TILE * TILE, step, 0, unroll=8)


def middle_kernel(count, position, slot_tile, slot_crop, par, stats2, pad_hbm, hidden_hbm, *rest):
    pieces, rest = rest[:count], rest[count:]
    pad_out_hbm, vecs_out = rest[:2]
    pad, weight, hidden, upstream, pad_out, vecs, totals, weight_sem, sem = rest[2:]
    slots = pad.shape[2]
    load_pad = pltpu.make_async_copy(pad_hbm, pad, sem.at[0])
    load_weight = WeightLoad(position, pieces, weight, weight_sem)
    load_hidden = pltpu.make_async_copy(hidden_hbm, hidden, sem.at[2])
    load_pad.start()
    load_weight.start()
    load_hidden.start()
    plan = Plan(position[0], slot_tile, slot_crop, slots)
    same = plan.same
    load_pad.wait()
    load_weight.wait()

    def step(row, carry):
        total = conv_rows(pad, weight, row, slots, NN, True)
        upstream[pl.ds(row * TILE, TILE)] = total.reshape(TILE, slots, CH)
        return carry

    lax.fori_loop(0, TILE, step, 0)
    load_hidden.wait()
    mean, inverse = stats2[0], stats2[1]
    gain, bias = par[G2 : G2 + 1, :], par[B2 : B2 + 1, :]

    def source(at, lanes):
        return hidden[at, :, lanes].astype(F32)

    plain, crossed = norm_back_sums(
        source, upstream, mean, inverse, gain, bias, slots
    )
    vecs[...] = jnp.zeros_like(vecs)
    vecs[G2 : G2 + 1, :] = jnp.sum(crossed, axis=0, keepdims=True)
    vecs[B2 : B2 + 1, :] = jnp.sum(plain, axis=0, keepdims=True)
    plain = crop_mean(same, plain * gain)
    crossed = crop_mean(same, crossed * gain)

    totals[...] = jnp.zeros_like(totals)

    def put(at, lanes, grad):
        rounded = grad.astype(BF16)
        pad_out[at // TILE + 1, at % TILE + 1, :, lanes] = rounded
        totals[:, lanes] += rounded.astype(F32)

    norm_back_apply(source, upstream, mean, inverse, gain, plain, crossed, put)
    vecs[C1 : C1 + 1, :] = jnp.sum(totals[...], axis=0, keepdims=True)
    store_vectors(vecs, vecs_out, position[0])
    fill_halo(pad_out, plan)
    save = pltpu.make_async_copy(pad_out, pad_out_hbm, sem.at[3])
    save.start()
    save.wait()


def middle(position, tables, par, stats2, pad, weight, hidden, slots):
    pixels = TILE * TILE
    rows = pixels * slots
    return call(
        functools.partial(middle_kernel, len(weight)),
        "sssvvhh" + "h" * len(weight),
        "hv",
        [shape(pad.shape, BF16), vector_shape(len(weight) > 1)],
        [
            vmem(pad.shape, BF16),
            vmem((9, CH, CH), BF16),
            vmem((pixels, slots, CH), BF16),
            vmem((pixels, slots, CH), F32),
            vmem(pad.shape, BF16),
            vmem((16, CH), F32),
            vmem((slots, CH), F32),
            weight_sems(weight),
            pltpu.SemaphoreType.DMA((4,)),
        ],
        "conv2_input_grad",
        2 * rows * CH * CH * 9,
        16 << 20,
    )(position, *tables[:2], par, stats2, pad, hidden, *weight)


def last_kernel(
    whose, count, position, slot_tile, slot_crop, par, stats1, vecs2, vecs3, *rest
):
    feats_hbm, pad_hbm, resid_hbm = rest[:3]
    pieces, rest = rest[3 : 3 + count], rest[3 + count :]
    out, vecs, pad, weight, feats, resid, upstream, weight_sem, sem = rest
    slots = pad.shape[2]
    width = upstream.shape[2]
    pixels = TILE * TILE
    me = position[0]
    columns = None
    span = pl.ds(0, width)
    if width < CH:
        columns = span = pl.ds(pl.multiple_of((me ^ whose) * width, width), width)
    load_weight = WeightLoad(position, pieces, weight, weight_sem, columns)
    load_pad = pltpu.make_async_copy(pad_hbm, pad, sem.at[0])
    inner = pl.ds(1, TILE)
    load_resid = pltpu.make_async_copy(resid_hbm.at[inner, inner, :, span], resid, sem.at[1])
    load_feats = pltpu.make_async_copy(feats_hbm.at[:, span], feats, sem.at[2])
    load_pad.start()
    load_weight.start()
    load_feats.start()
    load_resid.start()
    plan = Plan(me, slot_tile, slot_crop, slots)
    same = plan.same
    load_pad.wait()
    load_weight.wait()

    def step(row, carry):
        total = conv_rows(pad, weight, row, slots, NN, True)
        upstream[pl.ds(row * TILE, TILE)] = total.reshape(TILE, slots, width)
        return carry

    lax.fori_loop(0, TILE, step, 0)
    load_feats.wait()
    load_resid.wait()
    mean, inverse = stats1[0, :, span], stats1[1, :, span]
    gain, bias = par[G1 : G1 + 1, span], par[B1 : B1 + 1, span]

    def source(at, lanes):
        return feats[pl.ds(pl.multiple_of(at * slots, slots), slots), lanes].astype(F32)

    plain, crossed = norm_back_sums(source, upstream, mean, inverse, gain, bias, slots)
    vecs[...] = vecs2[...] + vecs3[...] if width == CH else vecs2[whose] + vecs3[whose]
    vecs[G1 : G1 + 1, :] = jnp.sum(crossed, axis=0, keepdims=True)
    vecs[B1 : B1 + 1, :] = jnp.sum(plain, axis=0, keepdims=True)
    plain = crop_mean(same, plain * gain)
    crossed = crop_mean(same, crossed * gain)

    def put(at, lanes, grad):
        rows = pl.ds(pl.multiple_of(at * slots, slots), slots)
        grad = resid[at // TILE, at % TILE, :, lanes].astype(F32) + grad
        out[rows, lanes] = grad.astype(out.dtype)

    norm_back_apply(source, upstream, mean, inverse, gain, plain, crossed, put)


def last(position, tables, par, stats1, vecs, feats, pad, weight, resid_grad, whose, slots):
    pixels = TILE * TILE
    rows = pixels * slots
    width = CH // 2 if len(weight) > 1 else CH
    return call(
        functools.partial(last_kernel, whose, len(weight)),
        "sssvvvvhhh" + "h" * len(weight),
        "vv",
        [
            shape((rows, width), F32 if width < CH and whose == 0 else BF16),
            shape((16, width), F32),
        ],
        [
            vmem(pad.shape, BF16),
            vmem((9, CH, width), BF16),
            vmem((rows, width), BF16),
            vmem((TILE, TILE, slots, width), BF16),
            vmem((pixels, slots, width), F32),
            weight_sems(weight),
            pltpu.SemaphoreType.DMA((3,)),
        ],
        "conv1_input_grad",
        2 * rows * CH * width * 9,
        10 << 20,
    )(position, *tables[:2], par, stats1, *vecs, feats, pad, resid_grad, *weight)


def after(value, *others):
    flat, tree = jax.tree.flatten(value)
    extra = jax.tree.leaves(others)
    held = lax.optimization_barrier(tuple(flat) + tuple(extra))
    return jax.tree.unflatten(tree, list(held[: len(flat)]))


def add(*terms):
    total = terms[0].astype(F32)
    for term in terms[1:]:
        total = total + term.astype(F32)
    return total


def swap(value, axis):
    return lax.ppermute(value, axis, [(0, 1), (1, 0)])


def to_all(value, axes, count):
    return lax.all_to_all(jnp.broadcast_to(value[None], (count,) + value.shape), axes, 0, 0)


QUAD = ("y", "near")


def from_quad(values):
    return [
        lax.ppermute(value, ("near", "y"), [(at, at ^ bits) for at in range(4)])
        for bits, value in zip((2, 1, 3), values)
    ]


def rounded_sum(terms):
    total = terms[0].astype(F32)
    for term in terms[1:]:
        total = total + term.astype(F32)
    return total.astype(BF16)


def vector_rows(vectors):
    rows, width = vectors.shape
    return jnp.pad(vectors.astype(BF16), ((0, BLOCK - rows), (0, CH - width)))


class Reduction:
    def __init__(self, halves, first, count):
        self.stage, self.first, self.count = 0, first, count
        self.state = (halves[0], halves[1], swap(halves[1], "core"))

    def advance(self, *others, vectors=None):
        if others:
            self.state = after(self.state, *others)
        self.stage += 1
        front = self.first * BLOCK
        back = (self.count - self.first) * BLOCK
        state = self.state
        if self.stage == 1:
            mine, _, came = state

            def part(begin, size):
                span = slice(begin, begin + size)
                return rounded_sum([mine[span], came[span]])

            start = 8 * front
            keep = part(0, 4 * front) if front else None, part(start, 2 * back)
            sent_front = part(4 * front, 4 * front) if front else None
            sent_back = [part(start + q * 2 * back, 2 * back) for q in (1, 2, 3)]
            came_front = swap(sent_front, "chan") if front else None
            self.state = keep, (came_front, from_quad(sent_back))
            return sent_front, sent_back
        if self.stage == 2:
            (mine_front, mine_back), (came_front, came_back) = state
            piece = [slice(q * front, (q + 1) * front) for q in range(4)]
            sent_front, keep_front = [], None
            if front:
                terms = [[mine_front[span], came_front[span]] for span in piece]
                keep_front, sent_front = terms[0], [rounded_sum(term) for term in terms[1:]]
            sent_back = rounded_sum([mine_back[back:]] + [value[back:] for value in came_back])
            if vectors is not None:
                sent_back = jnp.concatenate([sent_back, vector_rows(vectors)], axis=0)
            keep_back = [mine_back[:back]] + [value[:back] for value in came_back]
            self.state = keep_front, keep_back, (from_quad(sent_front), swap(sent_back, "chan"))
            return sent_front, sent_back
        if self.stage == 3:
            mine_front, mine_back, (came_front, came_back) = state
            parts = [rounded_sum(mine_front + came_front)] if front else []
            parts.append(rounded_sum(mine_back + [came_back[:back]]))
            if vectors is not None:
                parts.append(rounded_sum([vector_rows(vectors), came_back[back:]]))
            value = jnp.concatenate(parts, axis=0)
            self.state = value, swap(value, "far")
            return value
        if self.stage == 4:
            value = rounded_sum(list(state))
            self.state = [value] + from_quad([value] * 3)
            return value
        if self.stage == 5:
            mine = jnp.concatenate(state, axis=0)
            self.state = mine, swap(mine, "core")
            return mine

    @property
    def pieces(self):
        return list(self.state)


def assemble_kernel(sizes, position, mine, other, *outs):
    units = mine.shape[0] // (4 * BLOCK)
    vectors = None
    for number, part in enumerate((mine, other)):
        for at in range(4):
            row = ((position[1] ^ number) * 4 + (position[2] ^ at)) * BLOCK
            rows = pl.ds(pl.multiple_of(row, BLOCK), BLOCK)
            unit = 0
            for out, size in zip(outs, sizes):
                for index in range(max(size, 1)):
                    begin = (at * units + unit) * BLOCK
                    value = part[begin : begin + BLOCK, :].astype(F32)
                    if size:
                        out[index, rows, :] = value
                    else:
                        out[rows, :] = value
                    unit += 1
            if unit < units:
                begin = (at * units + unit) * BLOCK
                term = part[begin : begin + BLOCK, :].astype(F32)
                vectors = term if vectors is None else vectors + term
    if vectors is not None:
        outs[-1][...] = vectors


def assemble(position, pieces, sizes, vectors, name):
    shapes = [shape(((size,) if size else ()) + (8 * BLOCK, CH), F32) for size in sizes]
    if vectors:
        shapes.append(shape((BLOCK, CH), F32))
    return call(
        functools.partial(assemble_kernel, sizes),
        "svv",
        "v" * len(shapes),
        shapes,
        [],
        name,
        4 << 30,
        6 << 20,
    )(position, *pieces)


def body(
    paired,
    features,
    crop_ids,
    cotangent,
    norm1_gain,
    norm1_bias,
    conv1_weight,
    conv1_bias,
    norm2_gain,
    norm2_bias,
    conv2_weight,
    conv2_bias,
    norm3_gain,
    norm3_bias,
    query_weight,
    query_bias,
    key_weight,
    value_weight,
    value_bias,
    proj_weight,
    proj_bias,
):
    _, local, pixels = features.shape
    devices = lax.axis_size("chan")
    index = lax.axis_index("chan").astype(jnp.int32)
    tiles = pixels // (TILE * TILE)
    slots = tiles if devices == 1 else tiles // 2
    if paired:
        core, down, near = [lax.axis_index(a).astype(jnp.int32) for a in ("core", "y", "near")]
        quad = down * 2 + near
        piece = core * 4 + quad
    else:
        core = quad = jnp.int32(0)
    position = jnp.stack([index, core, quad])

    def exchange(parts):
        if paired:
            return [parts[0], swap(parts[1], "chan")]
        if devices == 2:
            parts = [jnp.where(index == 0, parts[k], parts[1 - k]) for k in range(2)]
        moved = lax.all_to_all(jnp.stack(parts), "chan", 0, 0)
        return [jnp.transpose(moved, (1, 0, 2)).reshape(moved.shape[1], CH)]

    def give_back(parts):
        if paired:
            return [parts[0], swap(parts[1], "chan")]
        whole = parts[0].reshape(parts[0].shape[0], devices, local)
        moved = lax.all_to_all(jnp.transpose(whole, (1, 0, 2)), "chan", 0, 0)
        parts = [moved[at] for at in range(devices)]
        if devices == 2:
            parts = [jnp.where(index == 0, parts[k], parts[1 - k]) for k in range(2)]
        return parts

    lanes = -(-local // 128) * 128

    def widened(signal):
        return jnp.pad(signal, ((0, lanes - local), (0, 0))) if lanes > local else signal

    def narrowed(parts):
        return [part[:, :local] for part in parts] if lanes > local else parts

    def unpack_lanes(parts, by_pixel, dtype, name):
        if lanes > local:
            parts = [jnp.pad(part, ((0, 0), (0, lanes - local))) for part in parts]
        whole = unpack(position, tables[0], parts, pixels, by_pixel, dtype, slots, name)
        return whole[:local]

    def vector_table(norm1_gain):
        return jnp.stack(
            [
                norm1_gain,
                norm1_bias,
                conv1_bias,
                norm2_gain,
                norm2_bias,
                conv2_bias,
                norm3_gain,
                norm3_bias,
                query_bias,
                value_bias,
                proj_bias,
            ]
            + [jnp.zeros_like(proj_bias)] * 5
        )

    small = jnp.stack([query_weight, key_weight, value_weight, proj_weight])
    if paired:
        eighth = local // 8
        part = lax.dynamic_slice_in_dim(conv1_weight, piece * eighth, eighth, 1)
        eighth1 = swap(part, "chan")
        part = lax.dynamic_slice_in_dim(conv2_weight, piece * eighth, eighth, 1)
        eighth2 = swap(part, "chan")
    else:
        par_parts = [lax.all_gather(vector_table(norm1_gain), "chan", axis=1, tiled=True)]
        weight1 = [lax.all_gather(conv1_weight, "chan", axis=1, tiled=True)]
    tables, packed = pack_first(
        position, crop_ids[0], widened(features[0]), devices, slots, "pack_features"
    )
    feature_parts = exchange(narrowed(packed))
    if paired:
        eighth1 = after(eighth1, packed[1])
        mine = to_all(eighth1, QUAD, 4)
        weight1 = [conv1_weight, mine, swap(mine, "core")]
        vectors = vector_table(after(norm1_gain, eighth1))
        par_parts = [vectors, swap(vectors, "chan")]
    packed = pack(
        position, tables[0], widened(cotangent[0]), False, devices, slots, "pack_cotangent"
    )
    packed = list(packed)
    if paired:
        part = lax.dynamic_slice_in_dim(small, core * (local // 2), local // 2, 1)
        eighth2, part = after((eighth2, part), feature_parts[1], weight1[1], packed[1])
        weight2 = [conv2_weight, to_all(eighth2, ("core",) + QUAD, 8)]
        own_small = swap(part, "chan")
    else:
        weight2 = [lax.all_gather(conv2_weight, "chan", axis=1, tiled=True)]
        weight3 = [lax.all_gather(small, "chan", axis=1, tiled=True)]
        tangent_parts = exchange(narrowed(packed))
    par, feats, pad1, hidden, pad2, stats1, stats2 = first(
        position, tables, par_parts, feature_parts, weight1, slots
    )
    if paired:
        own_small, packed[1] = after((own_small, packed[1]), pad2)
        tangent_parts = [packed[0], swap(packed[1], "chan")]
        weight3 = [small, own_small, swap(own_small, "core")]
    resid, normed, stats3 = second(position, tables, par, feats, pad2, weight2, slots)
    if paired:
        weight3 = after(weight3, normed)
    out_parts, small_grads, (vecs3, grad2) = attention(
        position, tables, par, normed, resid, stats3, tangent_parts, weight3, slots
    )
    out_parts = give_back(out_parts)
    if paired:
        resid_grad = grad2
        halves = weight_grad(
            position, pad2, grad2, True, slots, "conv2_weight_grad", 8, small_grads
        )
        chain2 = Reduction(halves, 8, 13)
        grad2 = after(grad2, halves[1])
        grad1, vecs2 = middle(position, tables, par, stats2, grad2, weight2, hidden, slots)
        back = functools.partial(last, position, tables, par, stats1, (vecs2, vecs3), feats)
        sent = chain2.advance(grad1, out_parts[1])
        halves = weight_grad(
            position, pad1, after(grad1, sent), True, slots, "conv1_weight_grad", 0
        )
        sent = chain2.advance(halves[1])
        chain1 = Reduction(after(halves, sent), 0, 9)
        grad1 = after(grad1, sent, halves[1])
        in_other, vecs_other = back(grad1, weight1, resid_grad, 1, slots)
        sent = chain1.advance(in_other, chain2.state), chain2.advance(in_other)
        in_got = swap(after(in_other, sent), "chan")
        grad1 = after(grad1, sent, in_other)
        in_own, vecs_own = back(grad1, weight1, resid_grad, 0, slots)
        sent = chain1.advance(in_own, vectors=vecs_other), chain2.advance(in_own)
        out_parts = after(out_parts, sent, in_own, in_got)
        output = unpack_lanes(out_parts, False, BF16, "unpack_output")
        sent = chain1.advance(output, vectors=vecs_own)
        in_parts = after([in_own, in_got], sent)
        input_grad = unpack_lanes(in_parts, True, F32, "unpack_input_grad")
        sent = chain1.advance(input_grad)
        sent = sent, chain2.advance(sent)
        small_grads = assemble(
            position, after(chain2.pieces, sent), [0, 0, 0, 0, 9], False, "conv2_grads"
        )
        small_grads, weight2_grad = small_grads[:4], small_grads[4]
        chain1.advance(weight2_grad)
        weight1_grad, vecs = assemble(position, chain1.pieces, [9], True, "conv1_grads")
        vecs = vecs[:16, :local]
    else:
        output = unpack_lanes(out_parts, False, BF16, "unpack_output")
        grads2 = weight_grad(position, pad2, grad2, False, slots, "conv2_weight_grad")
        grad1, vecs2 = middle(position, tables, par, stats2, grad2, weight2, hidden, slots)
        grads1 = weight_grad(position, pad1, grad1, False, slots, "conv1_weight_grad")
        in_all, vecs1 = last(
            position, tables, par, stats1, (vecs2, vecs3), feats, grad1, weight1, grad2, 0, slots
        )
        input_grad = unpack_lanes(give_back([in_all]), True, F32, "unpack_input_grad")

        def total(grad, axis):
            part = lax.psum_scatter(grad, "chan", scatter_dimension=axis, tiled=True)
            return lax.psum(part, "dp").astype(F32)

        small_grads, weight2_grad, weight1_grad = [
            total(g[0], 1) for g in (small_grads, grads2, grads1)
        ]
        vecs = total(vecs1, 1)
    gq, gk, gv, gp = small_grads if paired else [small_grads[k] for k in range(4)]
    return (
        output[None],
        input_grad[None],
        vecs[G1],
        vecs[B1],
        weight1_grad,
        vecs[C1],
        vecs[G2],
        vecs[B2],
        weight2_grad,
        vecs[C2],
        vecs[G3],
        vecs[B3],
        gq,
        vecs[QB],
        gk,
        gv,
        vecs[VB],
        gp,
        vecs[PB],
    )


def solution(mesh):
    paired = mesh.shape["dp"] == 16 and mesh.shape["chan"] == 2
    rows = "dp"
    if paired:
        rows = ("far", "near", "y", "core")
        mesh = jax.sharding.Mesh(mesh.devices.reshape((2,) * 5), rows + ("chan",))
    canvas = P(rows, "chan", None)
    vector = P("chan")
    conv = P(None, "chan", None)
    matrix = P("chan", None)
    placed = (
        (canvas, P(rows, None, None), canvas)
        + (vector, vector, conv, vector, vector, vector, conv, vector, vector, vector)
        + (matrix, vector, matrix, matrix, vector, matrix, vector)
    )
    results = (
        (canvas, canvas, vector, vector, conv, vector, vector, vector, conv, vector)
        + (vector, vector, matrix, vector, matrix, matrix, vector, matrix, vector)
    )
    return jax.shard_map(functools.partial(body, paired), mesh=mesh, in_specs=placed, out_specs=results, check_vma=False)
```

```python
import functools
import itertools

import jax
import jax.numpy as jnp
import numpy as np
from jax import lax
from jax.experimental import pallas as pl
from jax.experimental.pallas import tpu as pltpu
from jax.sharding import PartitionSpec as P

CH = 512
GROUPS = 32
CROPS = 16
TILE = 8
BANDS = 4
EPS = 1e-06
F32 = jnp.float32
BF16 = jnp.bfloat16
HIGH = lax.Precision.HIGHEST
NN = (((1,), (0,)), ((), ()))
NT = (((1,), (1,)), ((), ()))
TN = (((0,), (0,)), ((), ()))
VMEM = pltpu.VMEM
ANY = pl.ANY
SCALE = CH ** (-0.5)


def band_layouts(units):
    return [
        tuple(np.diff((0,) + cuts + (units,)))
        for cuts in itertools.combinations(range(1, units), BANDS - 1)
    ]


PITCH = 8
QUERIES = 8
KEYS = 8


def window_cost(starts, sizes, slots):
    total = 0.0
    for block in range(0, slots, QUERIES):
        inside = [
            (starts <= at) & (at < starts + sizes) for at in (block, block + QUERIES - 1)
        ]
        low = (starts * inside[0]).sum(axis=-1) // 2 * 2
        high = ((starts + sizes) * inside[1]).sum(axis=-1)
        total = total + (high - low + KEYS - 1) // KEYS + 0.25
    return total


def best_starts(sizes, slots):
    layouts = sizes.shape[0]
    masks = np.arange(1 << (CROPS - 1), dtype=np.int32)
    bits = ((masks[None, :] >> np.arange(CROPS)[:, None]) & 1).astype(np.float32)
    picks = []
    for row in sizes.astype(np.float32):
        filled, squares = row @ bits, (row * row) @ bits
        cost = np.abs(squares - (row * row).sum() / 2) + 1e6 * np.abs(filled - slots)
        picks.append(bits[:, np.argpartition(cost, 4)[:4]].T)
        picks[-1] = picks[-1][(picks[-1] @ row) == slots]
        picks[-1] = picks[-1][np.arange(4) % len(picks[-1])]
    halves = np.array(picks, np.int32)
    halves = np.stack([1 - halves, halves], axis=2)
    held = halves * sizes[:, None, None, :]
    draw = np.random.RandomState(0)
    best = np.full((layouts, 4, 2), 1e9, np.float32)
    chosen = np.zeros(held.shape, np.int32)
    for trial in range(20):
        key = draw.rand(CROPS)[None, None, None, :] + 0.0 * held
        if trial == 0:
            key = -held + 0.01 * key
        elif trial < 8:
            key = key + 2.0 * (held % QUERIES != 0)
        order = np.argsort(key, axis=-1)
        ordered = np.take_along_axis(held, order, axis=-1)
        begin = np.cumsum(ordered, axis=-1) - ordered
        starts = np.zeros_like(held)
        np.put_along_axis(starts, order, begin, axis=-1)
        cost = window_cost(starts, held, slots)
        better = cost < best
        best = np.where(better, cost, best)
        chosen = np.where(better[..., None], starts, chosen)
    pick = np.argmin(best.max(axis=2), axis=1)
    rows = np.arange(layouts)
    owner, starts = halves[rows, pick, 1], chosen[rows, pick]
    return np.where(owner == 1, starts[:, 1] + slots, starts[:, 0])


@functools.lru_cache(maxsize=None)
def start_tables(devices, units, slots):
    layouts = band_layouts(units)
    rank = np.zeros(1 << (units - 1), np.int32)
    for number, sizes in enumerate(layouts):
        cuts = np.cumsum(sizes)[:-1]
        rank[sum(1 << (int(c) - 1) for c in cuts)] = number
    sizes = np.array(
        [[r * c for r in rows for c in cols] for rows in layouts for cols in layouts], np.int32
    )
    if devices == 2:
        starts = best_starts(sizes, slots)
    else:
        starts = np.zeros(sizes.shape, np.int32)
        for at, row in enumerate(sizes):
            loads = [0] * devices
            for crop in sorted(range(CROPS), key=lambda c: -row[c]):
                device = loads.index(min(loads))
                starts[at, crop] = device * slots + loads[device]
                loads[device] += int(row[crop])
    assert ((starts % slots) + sizes <= slots).all() and starts.max() < 256
    return rank, starts


def packed_tables(devices, units, slots):
    rank, starts = start_tables(devices, units, slots)
    shifts = np.arange(0, 32, 8, dtype=np.int64)
    words = (starts.reshape(-1, 4, 4).astype(np.int64) << shifts).sum(axis=2)
    words = np.where(words >= 1 << 31, words - (1 << 32), words)
    return np.concatenate([rank, words.reshape(-1).astype(np.int32)])


def write_plan(devices, slots, ids, table, slot_tile, slot_crop, starts, ends):
    units = ids.shape[0] // TILE
    count = units * units
    layouts = len(band_layouts(units))

    def code(at):
        bits = 0
        for step in range(units - 1):
            bits = bits + jnp.where(at(step) != at(step + 1), 1 << step, 0)
        return table[bits]

    def row_id(step):
        return ids[TILE * step, 0]

    def col_id(step):
        return ids[0, TILE * step]

    layout = code(row_id) * layouts + code(col_id)
    words = [table[(1 << (units - 1)) + 4 * layout + part] for part in range(4)]
    if devices * slots > count:

        def clear(at, carry):
            slot_tile[at] = -1
            slot_crop[at] = -1
            return carry

        lax.fori_loop(0, devices * slots, clear, 0)
    for crop in range(CROPS):
        start = lax.shift_right_logical(words[crop // 4], jnp.int32(8 * (crop % 4))) & 255
        starts[crop] = start
        ends[crop] = start

    def place(row, carry):
        for col in range(units):
            crop = ids[row * TILE, col * TILE]
            at = ends[crop]
            slot_tile[at] = row * units + col
            slot_crop[at] = crop
            ends[crop] = at + 1
        return carry

    lax.fori_loop(0, units, place, 0)


class Plan:
    def __init__(self, me, slot_tile, slot_crop, slots):
        self.slots = slots
        base = me * slots
        lane = lax.broadcasted_iota(jnp.int32, (1, 128), 1) % slots
        down = lax.broadcasted_iota(jnp.int32, (slots, 1), 0)
        self.tile_row, self.crop_row = jnp.zeros_like(lane), jnp.zeros_like(lane)
        self.tile_col, self.crop_col = jnp.zeros_like(down), jnp.zeros_like(down)
        for slot in range(slots):
            tile, crop = slot_tile[base + slot], slot_crop[base + slot]
            self.tile_row = jnp.where(lane == slot, tile, self.tile_row)
            self.crop_row = jnp.where(lane == slot, crop, self.crop_row)
            self.tile_col = jnp.where(down == slot, tile, self.tile_col)
            self.crop_col = jnp.where(down == slot, crop, self.crop_col)
        self.same = (self.crop_col == self.crop_row[:, 0:slots]).astype(F32)


def group_total(value):
    width = CH // GROUPS
    lane = lax.broadcasted_iota(jnp.int32, (value.shape[0], 128), 1)
    parts = []
    for at in range(0, value.shape[1], 128):
        part = value[:, at : at + 128]
        step = 1
        while step < width:
            up = pltpu.roll(part, 128 - step, 1)
            down = pltpu.roll(part, step, 1)
            part = part + jnp.where((lane & step) == 0, up, down)
            step *= 2
        parts.append(part)
    return jnp.concatenate(parts, axis=1)


def crop_mean(same, value):
    count = jnp.sum(same, axis=1, keepdims=True) * float(TILE * TILE * (CH // GROUPS))
    total = lax.dot_general(same, group_total(value), NN, precision=HIGH, preferred_element_type=F32)
    return total / count


def lanes_of(width):
    return [slice(at, at + 128) for at in range(0, width, 128)]


def slab_sum(pixels, slots, width, term):
    parts = []
    for lanes in lanes_of(width):

        def step(at, total):
            return total + term(at, lanes)

        parts.append(lax.fori_loop(0, pixels, step, jnp.zeros((slots, 128), F32), unroll=8))
    return jnp.concatenate(parts, axis=1)


def slab_stats(pixels, slots, slab, same):
    mean = crop_mean(same, slab_sum(pixels, slots, CH, slab))

    def square(at, lanes):
        centred = slab(at, lanes) - mean[:, lanes]
        return centred * centred

    return mean, lax.rsqrt(crop_mean(same, slab_sum(pixels, slots, CH, square)) + EPS)


def sigmoid(value):
    return 0.5 * jnp.tanh(0.5 * value) + 0.5


def fill_halo(pad, plan):
    slots = plan.slots
    wide = TILE * slots
    tile_c = jnp.concatenate([plan.tile_col] * TILE, axis=0)
    crop_c = jnp.concatenate([plan.crop_col] * TILE, axis=0)
    tile_r = jnp.concatenate([plan.tile_row] * (wide // 128), axis=1)
    crop_r = jnp.concatenate([plan.crop_row] * (wide // 128), axis=1)
    block_c = lax.broadcasted_iota(jnp.int32, (wide, wide), 0) // slots
    block_r = lax.broadcasted_iota(jnp.int32, (wide, wide), 1) // slots
    linked = (crop_c == crop_r) & (tile_c >= 0)

    def near(row_step, col_step):
        return linked & (tile_r == tile_c + (TILE * row_step + col_step))

    def edge(row_step, col_step, source):
        pick = (near(row_step, col_step) & (block_c == block_r)).astype(F32).astype(BF16)
        moved = jnp.dot(pick, source.reshape(wide, CH), preferred_element_type=F32).astype(BF16)
        return moved.reshape(TILE, slots, CH)

    def corner(row_step, col_step, source):
        pick = near(row_step, col_step)[0:slots, 0:slots].astype(F32).astype(BF16)
        return jnp.dot(pick, source, preferred_element_type=F32).astype(BF16)

    low, high, end = 1, TILE, TILE + 1
    pad[0, low:end] = edge(-1, 0, pad[high, low:end])
    pad[end, low:end] = edge(1, 0, pad[low, low:end])
    pad[low:end, 0] = edge(0, -1, pad[low:end, high])
    pad[low:end, end] = edge(0, 1, pad[low:end, low])
    pad[0, 0] = corner(-1, -1, pad[high, high])
    pad[0, end] = corner(-1, 1, pad[high, low])
    pad[end, 0] = corner(1, -1, pad[low, high])
    pad[end, end] = corner(1, 1, pad[low, low])


class WeightLoad:
    def __init__(self, position, pieces, target, sem, columns=None):
        self.copies = []
        views = [(pieces[0], None)]
        if len(pieces) > 1:
            me, core = position[0], position[1]
            half = pieces[0].shape[1]
            views = [(pieces[0], me * half)]
            part = half // (len(pieces) - 1)
            for number, piece in enumerate(pieces[1:]):
                spot = (1 - me) * half
                if len(pieces) == 3:
                    spot = spot + (core ^ number) * part
                if len(piece.shape) == 3:
                    views.append((piece, spot))
                    continue
                for at in range(piece.shape[0]):
                    views.append((piece.at[at], spot + at * piece.shape[2]))
        for at, (piece, spot) in enumerate(views):
            width = piece.shape[1]
            rows = slice(None)
            if spot is not None:
                rows = pl.ds(pl.multiple_of(spot, 32), width)
            if columns is not None:
                piece = piece.at[:, :, columns]
            self.copies.append(pltpu.make_async_copy(piece, target.at[:, rows, :], sem.at[at]))

    def start(self):
        for copy in self.copies:
            copy.start()

    def wait(self):
        for copy in self.copies:
            copy.wait()


def weight_sems(pieces):
    return pltpu.SemaphoreType.DMA((9,))


BLOCK = CH // 16


def store_grad(grad, outs, work, position, unit, first, count, front=True):
    if len(outs) == 1:
        outs[0][unit] = grad.astype(BF16)
        return
    work[...] = grad
    me, core, quad = position[0], position[1], position[2]
    for half, out in enumerate(outs):
        for c in range(2):
            for q in range(4):
                row = (me ^ c) * (CH // 2) + (core ^ half) * (CH // 4) + (quad ^ q) * BLOCK
                part = work[pl.ds(pl.multiple_of(row, BLOCK), BLOCK), :]
                if front:
                    to = ((c * 4 + q) * first + unit) * BLOCK
                else:
                    to = (8 * first + (q * 2 + c) * (count - first) + unit - first) * BLOCK
                out[pl.ds(pl.multiple_of(to, BLOCK), BLOCK), :] = part.astype(BF16)


def store_vectors(vecs, out, me):
    if len(out.shape) == 2:
        out[...] = vecs[...]
    else:
        half = out.shape[2]
        out[0] = vecs[:, pl.ds(pl.multiple_of(me * half, half), half)]
        out[1] = vecs[:, pl.ds(pl.multiple_of((1 - me) * half, half), half)]


def vector_shape(paired):
    return shape((2, 16, CH // 2) if paired else (16, CH), F32)


def grad_shapes(count, paired):
    if paired:
        return [shape((8 * count * BLOCK, CH), BF16)] * 2
    return [shape((count, CH, CH), BF16)]


def conv_rows(pad, weight, row, slots, dims, flipped, count=1):
    total = None
    for tap in range(9):
        down, right = tap // 3, tap % 3
        if flipped:
            down, right = 2 - down, 2 - right
        left = pad[pl.ds(row + down, count), right : right + TILE].reshape(count * TILE * slots, CH)
        part = lax.dot_general(left, weight[tap], dims, preferred_element_type=F32)
        total = part if total is None else total + part
    return total


def load_full(parts, me, dtype, store):
    if len(parts) == 1:
        store(slice(None), parts[0][...].astype(dtype))
    else:
        local = parts[0].shape[-1]
        own = pl.ds(pl.multiple_of(me * local, local), local)
        other = pl.ds(pl.multiple_of((1 - me) * local, local), local)
        store(own, parts[0][...].astype(dtype))
        store(other, parts[1][...].astype(dtype))


def vmem(shape, dtype):
    return pltpu.VMEM(shape, dtype)


def specs(kinds):
    table = {
        "v": pl.BlockSpec(memory_space=pltpu.VMEM),
        "s": pl.BlockSpec(memory_space=pltpu.SMEM),
        "h": pl.BlockSpec(memory_space=pl.ANY),
    }
    return [table[k] for k in kinds]


ROOM = {
    "unpack_output": 18,
    "unpack_input_grad": 18,
    "conv2_weight_grad": 24,
    "conv1_weight_grad": 22,
    "conv2_input_grad": 24,
    "conv1_input_grad": 20,
    "conv2_grads": 16,
    "conv1_grads": 14,
}


def call(body, ins, outs, shapes, scratch, name, flops, moved):
    return pl.pallas_call(
        body,
        in_specs=specs(ins),
        out_specs=tuple(specs(outs)),
        out_shape=tuple(shapes),
        scratch_shapes=list(scratch),
        compiler_params=pltpu.CompilerParams(vmem_limit_bytes=ROOM.get(name, 60) << 20),
        cost_estimate=pl.CostEstimate(
            flops=int(flops), bytes_accessed=int(moved), transcendentals=0
        ),
        name=name,
    )


def shape(dims, dtype):
    return jax.ShapeDtypeStruct(dims, dtype)


def pack_first_kernel(devices, slots, position, ids, table, signal, *rest):
    plan, rest = rest[:4], rest[4:]
    write_plan(devices, slots, ids, table, *plan)
    pack_kernel(True, slots, position, plan[0], signal, *rest)


def pack_kernel(by_pixel, slots, position, slot_tile, signal, *rest):
    outs, (raster, stage) = rest[:-2], rest[-2:]
    local, pixels = signal.shape
    side = int(pixels**0.5)
    chunk = 512
    cols = local // 128
    for at in range(0, pixels, chunk):
        flipped = signal[:, at : at + chunk].astype(F32).T
        for col in range(cols):
            raster[col, at : at + chunk, :] = flipped[:, col * 128 : (col + 1) * 128]
    for number, out in enumerate(outs):

        def step(slot, carry):
            tile = slot_tile[pack_base(position, number, len(outs), slots) + slot]
            keep = tile >= 0
            tile = jnp.maximum(tile, 0)
            start = (tile // TILE) * (TILE * side) + (tile % TILE) * TILE
            for row in range(TILE):
                for col in range(cols):
                    value = raster[col, pl.ds(pl.multiple_of(start + row * side, TILE), TILE), :]
                    value = jnp.where(keep, value, 0.0)
                    if by_pixel:
                        pitch = slots + PITCH
                        to = pl.ds(row * TILE * pitch + slot, TILE, stride=pitch)
                        stage[col, to, :] = value
                    else:
                        at = pl.multiple_of(slot * (TILE * TILE) + row * TILE, TILE)
                        stage[col, pl.ds(at, TILE), :] = value
            return carry

        lax.fori_loop(0, slots, step, 0)
        size = slots if by_pixel else TILE * TILE
        pitch = size + PITCH if by_pixel else size
        for number in range(out.shape[0] // size):
            for col in range(cols):
                span = slice(col * 128, (col + 1) * 128)
                value = stage[col, number * pitch : number * pitch + size, :]
                out[number * size : (number + 1) * size, span] = value.astype(BF16)


def pack_base(position, number, devices, slots):
    return (position[0] ^ number if devices == 2 else number) * slots


def pack_scratch(local, pixels, slots):
    rows = TILE * TILE * (slots + PITCH)
    return [vmem((local // 128, pixels, 128), F32), vmem((local // 128, rows, 128), F32)]


def pack_first(position, ids, signal, devices, slots, name):
    local, pixels = signal.shape
    rows = slots * TILE * TILE
    table = jnp.asarray(packed_tables(devices, ids.shape[0] // TILE, slots))
    result = call(
        functools.partial(pack_first_kernel, devices, slots),
        "sssv",
        "ssss" + "v" * devices,
        [shape((devices * slots,), jnp.int32)] * 2
        + [shape((CROPS,), jnp.int32)] * 2
        + [shape((rows, local), BF16)] * devices,
        pack_scratch(local, pixels, slots),
        name,
        4 << 30,
        6 << 20,
    )(position, ids, table, signal)
    return result[:4], result[4:]


def pack(position, slot_tile, signal, by_pixel, devices, slots, name):
    local, pixels = signal.shape
    rows = slots * TILE * TILE
    return call(
        functools.partial(pack_kernel, by_pixel, slots),
        "ssv",
        "v" * devices,
        [shape((rows, local), BF16)] * devices,
        pack_scratch(local, pixels, slots),
        name,
        40 << 30,
        6 << 20,
    )(position, slot_tile, signal)


def unpack_kernel(by_pixel, slots, position, slot_tile, *rest):
    ins, out, (raster, stage) = rest[:-3], rest[-3], rest[-2:]
    local, pixels = out.shape
    side = int(pixels**0.5)
    chunk = 512
    cols = local // 128
    for number, part in enumerate(ins):
        size = slots if by_pixel else TILE * TILE
        pitch = size + PITCH if by_pixel else size
        for at in range(part.shape[0] // size):
            for col in range(cols):
                span = slice(col * 128, (col + 1) * 128)
                value = part[at * size : (at + 1) * size, span]
                stage[col, at * pitch : at * pitch + size, :] = value.astype(F32)

        def step(slot, carry):
            tile = slot_tile[pack_base(position, number, len(ins), slots) + slot]

            @pl.when(tile >= 0)
            def _():
                start = (tile // TILE) * (TILE * side) + (tile % TILE) * TILE
                for row in range(TILE):
                    to = pl.ds(pl.multiple_of(start + row * side, TILE), TILE)
                    for col in range(cols):
                        if by_pixel:
                            at = pl.ds(row * TILE * pitch + slot, TILE, stride=pitch)
                        else:
                            first = pl.multiple_of(slot * (TILE * TILE) + row * TILE, TILE)
                            at = pl.ds(first, TILE)
                        raster[col, to, :] = stage[col, at, :]

            return carry

        lax.fori_loop(0, slots, step, 0)
    for at in range(0, pixels, chunk):
        for col in range(cols):
            span = slice(col * 128, (col + 1) * 128)
            out[span, at : at + chunk] = raster[col, at : at + chunk, :].T.astype(out.dtype)


def unpack(position, slot_tile, parts, pixels, by_pixel, dtype, slots, name):
    rows, local = parts[0].shape
    return call(
        functools.partial(unpack_kernel, by_pixel, slots),
        "ss" + "v" * len(parts),
        "v",
        [shape((local, pixels), dtype)],
        pack_scratch(local, pixels, slots),
        name,
        4 << 30,
        8 << 20,
    )(position, slot_tile, *parts)[0]


(G1, B1, C1, G2, B2, C2, G3, B3, QB, VB, PB) = range(11)


def norm_swish_pad(slab, mean, inverse, gain, bias, pad, copy=None):
    scaled = inverse * gain
    for lanes in lanes_of(CH):
        centre, factor, offset = mean[:, lanes], scaled[:, lanes], bias[:, lanes]

        def step(row, carry):
            for col in range(TILE):
                value = slab(row * TILE + col, lanes)
                before = (value - centre) * factor + offset
                pad[row + 1, col + 1, :, lanes] = (before * jax.nn.sigmoid(before)).astype(BF16)
                if copy is not None:
                    copy[row * TILE + col, :, lanes] = value.astype(BF16)
            return carry

        lax.fori_loop(0, TILE, step, 0)


def first_kernel(parts, count, position, slot_tile, slot_crop, *rest):
    feature_parts, rest = rest[:parts], rest[parts:]
    par_parts, rest = rest[:parts], rest[parts:]
    pieces, rest = rest[:count], rest[count:]
    (par, feats_hbm, pad1_hbm, hidden_hbm, pad2_hbm, stats1, stats2) = rest[:7]
    feats, rounded, hidden, pad1, pad2, weight, weight_sem, sem = rest[7:]
    pixels, slots, _ = hidden.shape
    load_weight = WeightLoad(position, pieces, weight, weight_sem)
    load_weight.start()

    def put_par(columns, value):
        par[:, columns] = value

    load_full(par_parts, position[0], F32, put_par)

    def put(columns, value):
        feats[:, columns] = value

    load_full(feature_parts, position[0], BF16, put)
    save_feats = pltpu.make_async_copy(feats, feats_hbm, sem.at[1])
    save_feats.start()

    plan = Plan(position[0], slot_tile, slot_crop, slots)

    def slab1(at, lanes):
        return feats[pl.ds(pl.multiple_of(at * slots, slots), slots), lanes].astype(F32)

    mean, inverse = slab_stats(pixels, slots, slab1, plan.same)
    stats1[0], stats1[1] = mean, inverse
    norm_swish_pad(slab1, mean, inverse, par[G1 : G1 + 1, :], par[B1 : B1 + 1, :], pad1)
    fill_halo(pad1, plan)
    save_pad1 = pltpu.make_async_copy(pad1, pad1_hbm, sem.at[2])
    save_pad1.start()
    load_weight.wait()

    def step(row, carry):
        total = conv_rows(pad1, weight, row, slots, NT, False) + par[C1 : C1 + 1, :]
        hidden[pl.ds(row * TILE, TILE)] = total.reshape(TILE, slots, CH)
        return carry

    lax.fori_loop(0, TILE, step, 0)

    def slab2(at, lanes):
        return hidden[at, :, lanes]

    mean, inverse = slab_stats(pixels, slots, slab2, plan.same)
    stats2[0], stats2[1] = mean, inverse
    norm_swish_pad(
        slab2, mean, inverse, par[G2 : G2 + 1, :], par[B2 : B2 + 1, :], pad2, rounded
    )
    save_hidden = pltpu.make_async_copy(rounded, hidden_hbm, sem.at[3])
    save_hidden.start()
    fill_halo(pad2, plan)
    save_pad2 = pltpu.make_async_copy(pad2, pad2_hbm, sem.at[4])
    save_pad2.start()
    save_feats.wait()
    save_pad1.wait()
    save_hidden.wait()
    save_pad2.wait()


def first(position, tables, par_parts, parts, weight, slots):
    pixels = TILE * TILE
    rows = pixels * slots
    pad = (TILE + 2, TILE + 2, slots, CH)
    return call(
        functools.partial(first_kernel, len(parts), len(weight)),
        "sss" + "v" * len(parts) + "v" * len(parts) + "h" * len(weight),
        "vhhhhvv",
        [
            shape((16, CH), F32),
            shape((rows, CH), BF16),
            shape(pad, BF16),
            shape((pixels, slots, CH), BF16),
            shape(pad, BF16),
            shape((2, slots, CH), F32),
            shape((2, slots, CH), F32),
        ],
        [
            vmem((rows, CH), BF16),
            vmem((pixels, slots, CH), BF16),
            vmem((pixels, slots, CH), F32),
            vmem(pad, BF16),
            vmem(pad, BF16),
            vmem((9, CH, CH), BF16),
            weight_sems(weight),
            pltpu.SemaphoreType.DMA((5,)),
        ],
        "conv1_forward",
        2 * rows * CH * CH * 9,
        20 << 20,
    )(position, *tables[:2], *parts, *par_parts, *weight)


def second_kernel(count, position, slot_tile, slot_crop, par, feats, pad_hbm, *rest):
    pieces, rest = rest[:count], rest[count:]
    resid_hbm, normed_hbm, stats3 = rest[:3]
    resid, resid_tile, normed, pad, weight, rows_scr, weight_sem, sem = rest[3:]
    slots = pad.shape[2]
    pixels = TILE * TILE
    load_pad = pltpu.make_async_copy(pad_hbm, pad, sem.at[0])
    load_weight = WeightLoad(position, pieces, weight, weight_sem)
    load_pad.start()
    load_weight.start()
    plan = Plan(position[0], slot_tile, slot_crop, slots)
    same = plan.same
    load_pad.wait()
    load_weight.wait()
    wide = TILE * slots

    def step(row, carry):
        at = pl.ds(pl.multiple_of(row * wide, wide), wide)
        total = conv_rows(pad, weight, row, slots, NT, False) + par[C2 : C2 + 1, :]
        total = total + feats[at, :].astype(F32)
        for col in range(CH // 128):
            for x in range(TILE):
                to = pl.multiple_of((row * TILE + x) * (slots + PITCH), 8)
                part = total[x * slots : (x + 1) * slots, col * 128 : (col + 1) * 128]
                resid[col, pl.ds(to, slots), :] = part
        return carry

    lax.fori_loop(0, TILE, step, 0)

    def slab(at, lanes):
        begin = pl.multiple_of(at * (slots + PITCH), 8)
        return resid[lanes.start // 128, pl.ds(begin, slots), :]

    mean, inverse = slab_stats(pixels, slots, slab, same)
    stats3[0], stats3[1] = mean, inverse
    rows_scr[0], rows_scr[1] = mean, inverse * par[G3 : G3 + 1, :]
    bias = par[B3 : B3 + 1, :]

    def tile_step(slot, carry):
        at = pl.ds(pl.multiple_of(slot * pixels, pixels), pixels)
        centre, factor = rows_scr[0, pl.ds(slot, 1)], rows_scr[1, pl.ds(slot, 1)]
        for col, lanes in enumerate(lanes_of(CH)):
            value = resid[col, pl.ds(slot, pixels, stride=slots + PITCH), :]
            resid_tile[at, lanes] = value.astype(BF16)
            scaled = (value - centre[:, lanes]) * factor[:, lanes]
            normed[at, lanes] = (scaled + bias[:, lanes]).astype(BF16)
        return carry

    lax.fori_loop(0, slots, tile_step, 0, unroll=2)
    save_resid = pltpu.make_async_copy(resid_tile, resid_hbm, sem.at[2])
    save_normed = pltpu.make_async_copy(normed, normed_hbm, sem.at[3])
    save_resid.start()
    save_normed.start()
    save_resid.wait()
    save_normed.wait()


def second(position, tables, par, feats, pad, weight, slots):
    pixels = TILE * TILE
    rows = pixels * slots
    return call(
        functools.partial(second_kernel, len(weight)),
        "sssvvh" + "h" * len(weight),
        "hhv",
        [shape((rows, CH), BF16), shape((rows, CH), BF16), shape((2, slots, CH), F32)],
        [
            vmem((CH // 128, pixels * (slots + PITCH), 128), F32),
            vmem((rows, CH), BF16),
            vmem((rows, CH), BF16),
            vmem(pad.shape, BF16),
            vmem((9, CH, CH), BF16),
            vmem((2, slots, CH), F32),
            weight_sems(weight),
            pltpu.SemaphoreType.DMA((4,)),
        ],
        "conv2_forward",
        2 * rows * CH * CH * 9,
        16 << 20,
    )(position, *tables[:2], par, feats, pad, *weight)


def attention_kernel(parts, outs, count, position, slot_tile, slot_crop, starts, ends, *rest):
    par, normed, resid_hbm, stats3 = rest[:4]
    tangent_parts, rest = rest[4 : 4 + parts], rest[4 + parts :]
    pieces, rest = rest[:count], rest[count:]
    out_hbm, rest = rest[:outs], rest[outs:]
    grads_hbm, rest = rest[:outs], rest[outs:]
    vecs_out, pad = rest[:2]
    (tangent, query, key, value, mixed_grad, mixed, query_grad, key_grad, value_grad) = rest[2:11]
    normed_grad, by_tile, rows_scr, weight, key_crop, work, vecs = rest[11:18]
    scores_scr, prob_grads, sums, weight_sem, sem, resid = rest[18:24]
    grad_outs = rest[24:]
    load_weight = WeightLoad(position, pieces, weight, weight_sem)
    load_weight.start()
    wq, wk, wv, wp = (weight.at[k] for k in range(4))
    rows = normed.shape[0]
    pixels = TILE * TILE
    slots = rows // pixels
    me = position[0]
    base = me * slots
    per_block = QUERIES
    block = per_block * pixels
    plan = Plan(me, slot_tile, slot_crop, slots)
    lane_slot = lax.broadcasted_iota(jnp.int32, (1, rows), 1) // pixels
    crops = jnp.zeros((1, rows), jnp.int32)
    for slot in range(slots):
        crops = jnp.where(lane_slot == slot, slot_crop[base + slot], crops)
    key_crop[...] = crops

    half = CH // outs
    columns = [pl.ds(0, CH)]
    if outs == 2:
        columns = [pl.ds(pl.multiple_of((me ^ k) * half, half), half) for k in range(2)]
    load_tangent = [
        pltpu.make_async_copy(part, tangent.at[:, columns[k]], sem.at[k])
        for k, part in enumerate(tangent_parts)
    ]
    load_resid = pltpu.make_async_copy(resid_hbm, resid, sem.at[2])
    save_out = [
        pltpu.make_async_copy(query.at[:, columns[k]], part, sem.at[3 + k])
        for k, part in enumerate(out_hbm)
    ]
    save_grads = [
        pltpu.make_async_copy(part, grads_hbm[k], sem.at[5 + k])
        for k, part in enumerate(grad_outs)
    ]
    for copy in load_tangent + [load_resid]:
        copy.start()
    load_weight.wait()
    for copy in load_tangent:
        copy.wait()

    def project(at, carry):
        span = pl.ds(pl.multiple_of(at * block, block), block)
        left = normed[span, :]
        total = lax.dot_general(left, wq[...], NT, preferred_element_type=F32)
        query[span, :] = (total + par[QB : QB + 1, :]).astype(BF16)
        key[span, :] = lax.dot_general(left, wk[...], NT, preferred_element_type=F32).astype(BF16)
        total = lax.dot_general(left, wv[...], NT, preferred_element_type=F32)
        value[span, :] = (total + par[VB : VB + 1, :]).astype(BF16)
        mixed_grad[span, :] = jnp.dot(
            tangent[span, :], wp[...], preferred_element_type=F32
        ).astype(BF16)
        key_grad[span, :] = jnp.zeros((block, CH), F32)
        value_grad[span, :] = jnp.zeros((block, CH), F32)
        return carry

    lax.fori_loop(0, rows // block, project, 0)

    def attend_step(at, carry):
        span = pl.ds(pl.multiple_of(at * block, block), block)
        low_crop = slot_crop[base + at * per_block]
        high_crop = slot_crop[base + at * per_block + per_block - 1]
        low = starts[jnp.maximum(low_crop, 0)] - base
        low = jnp.where(low_crop < 0, at * per_block, low) // 2 * 2
        high = jnp.where(high_crop < 0, slots, ends[jnp.maximum(high_crop, 0)] - base)
        count = (high - low + KEYS - 1) // KEYS
        begin = jnp.minimum(low, slots - KEYS * count) * pixels
        down = lax.broadcasted_iota(jnp.int32, (block, 1), 0) // pixels
        own_crop = jnp.zeros((block, 1), jnp.int32)
        for slot in range(per_block):
            own_crop = jnp.where(down == slot, slot_crop[base + at * per_block + slot], own_crop)

        def keys_of(number):
            return pl.ds(pl.multiple_of(begin + number * (KEYS * pixels), 128), KEYS * pixels)

        def score(number, top):
            keys = keys_of(number)
            scores = lax.dot_general(
                query[span, :], key[keys, :], NT, preferred_element_type=F32
            )
            scores = jnp.where(own_crop == key_crop[:, keys], scores * SCALE, -1e30)
            scores_scr[number] = scores
            prob_grads[number] = lax.dot_general(
                mixed_grad[span, :], value[keys, :], NT, preferred_element_type=F32
            )
            return jnp.maximum(top, jnp.max(scores, axis=1, keepdims=True))

        top = lax.fori_loop(0, count, score, jnp.full((block, 1), -1e30, F32))

        def weigh(number, carry):
            total, inner = carry
            exponent = jnp.exp(scores_scr[number] - top)
            scores_scr[number] = exponent
            total += jnp.sum(exponent, axis=1, keepdims=True)
            inner += jnp.sum(exponent * prob_grads[number], axis=1, keepdims=True)
            return total, inner

        zero = jnp.zeros((block, 1), F32)
        total, inner = lax.fori_loop(0, count, weigh, (zero, zero))
        share = 1.0 / total
        inner = inner * share
        sums[...] = jnp.zeros_like(sums)

        def spread_back(number, carry):
            keys = keys_of(number)
            prob = scores_scr[number] * share
            rounded = prob.astype(BF16)
            score_grad = (prob * (prob_grads[number] - inner)).astype(BF16)
            sums[0] += jnp.dot(rounded, value[keys, :], preferred_element_type=F32)
            sums[1] += jnp.dot(score_grad, key[keys, :], preferred_element_type=F32)
            key_grad[keys, :] += lax.dot_general(
                score_grad, query[span, :], TN, preferred_element_type=F32
            )
            value_grad[keys, :] += lax.dot_general(
                rounded, mixed_grad[span, :], TN, preferred_element_type=F32
            )
            return carry

        lax.fori_loop(0, count, spread_back, 0)
        mixed[span, :] = sums[0].astype(BF16)
        query_grad[span, :] = (sums[1] * SCALE).astype(BF16)
        return carry

    lax.fori_loop(0, rows // block, attend_step, 0)

    def back(at, carry):
        query_bias, value_bias, tangent_sum = carry
        span = pl.ds(pl.multiple_of(at * block, block), block)
        dq = query_grad[span, :]
        dk = (key_grad[span, :] * SCALE).astype(BF16)
        dv = value_grad[span, :].astype(BF16)
        key[span, :] = dk
        value[span, :] = dv
        total = jnp.dot(dq, wq[...], preferred_element_type=F32)
        total += jnp.dot(dk, wk[...], preferred_element_type=F32)
        total += jnp.dot(dv, wv[...], preferred_element_type=F32)
        normed_grad[span, :] = total
        result = lax.dot_general(mixed[span, :], wp[...], NT, preferred_element_type=F32)
        result = (result + par[PB : PB + 1, :] + resid[span, :].astype(F32)).astype(BF16)
        query[span, :] = result
        query_bias += jnp.sum(dq.astype(F32), axis=0, keepdims=True)
        value_bias += jnp.sum(dv.astype(F32), axis=0, keepdims=True)
        tangent_sum += jnp.sum(tangent[span, :].astype(F32), axis=0, keepdims=True)
        return query_bias, value_bias, tangent_sum

    load_resid.wait()
    zero = jnp.zeros((1, CH), F32)
    query_bias, value_bias, tangent_sum = lax.fori_loop(
        0, rows // block, back, (zero, zero, zero)
    )
    for copy in save_out:
        copy.start()
    left = normed[...]
    for number, grad in enumerate((query_grad, key, value)):
        total = lax.dot_general(grad[...], left, TN, preferred_element_type=F32)
        store_grad(total, grad_outs, work, position, number, 4, 4)
    total = lax.dot_general(tangent[...], mixed[...], TN, preferred_element_type=F32)
    store_grad(total, grad_outs, work, position, 3, 4, 4)
    for copy in save_grads:
        copy.start()

    def tile_sums(slot, carry):
        span = pl.ds(pl.multiple_of(slot * pixels, pixels), pixels)
        row = pl.ds(slot, 1)
        centre, factor = stats3[0, row], stats3[1, row]
        plains, crosseds = [], []
        for lanes in lanes_of(CH):
            upstream = normed_grad[span, lanes]
            hat = (resid[span, lanes].astype(F32) - centre[:, lanes]) * factor[:, lanes]
            plains.append(jnp.sum(upstream, axis=0, keepdims=True))
            crosseds.append(jnp.sum(upstream * hat, axis=0, keepdims=True))
        rows_scr[0, row] = jnp.concatenate(plains, axis=1)
        rows_scr[1, row] = jnp.concatenate(crosseds, axis=1)
        return carry

    lax.fori_loop(0, slots, tile_sums, 0)
    same = plan.same
    gain = par[G3 : G3 + 1, :]
    plain, crossed = rows_scr[0], rows_scr[1]
    vecs[...] = jnp.zeros_like(vecs)
    vecs[G3 : G3 + 1, :] = jnp.sum(crossed, axis=0, keepdims=True)
    vecs[B3 : B3 + 1, :] = jnp.sum(plain, axis=0, keepdims=True)
    vecs[QB : QB + 1, :] = query_bias
    vecs[VB : VB + 1, :] = value_bias
    vecs[PB : PB + 1, :] = tangent_sum
    rows_scr[0] = crop_mean(same, plain * gain)
    rows_scr[1] = crop_mean(same, crossed * gain)

    def apply(slot, carry):
        span = pl.ds(pl.multiple_of(slot * pixels, pixels), pixels)
        padded = pl.ds(pl.multiple_of(slot * (pixels + PITCH), 8), pixels)
        row = pl.ds(slot, 1)
        centre, factor = stats3[0, row], stats3[1, row]
        slope = factor * gain
        level = factor * rows_scr[0, row]
        tilt = factor * factor * rows_scr[1, row]
        for col, lanes in enumerate(lanes_of(CH)):
            centred = resid[span, lanes].astype(F32) - centre[:, lanes]
            grad = normed_grad[span, lanes] * slope[:, lanes] - level[:, lanes]
            grad = grad - centred * tilt[:, lanes]
            by_tile[col, padded, :] = tangent[span, lanes].astype(F32) + grad
        return carry

    lax.fori_loop(0, slots, apply, 0)

    def spread(row, carry):
        total = carry
        for col in range(TILE):
            at = row * TILE + col
            slab = jnp.concatenate(
                [
                    by_tile[c, pl.ds(at, slots, stride=pixels + PITCH), :] for c in range(CH // 128)
                ],
                axis=1,
            )
            rounded = slab.astype(BF16)
            pad[row + 1, col + 1] = rounded
            total += jnp.sum(rounded.astype(F32), axis=0, keepdims=True)
        return total

    vecs[C2 : C2 + 1, :] = lax.fori_loop(0, TILE, spread, zero)
    store_vectors(vecs, vecs_out, me)
    fill_halo(pad, plan)
    for copy in save_out + save_grads:
        copy.wait()


def attention(position, tables, par, normed, resid, stats3, tangent_parts, weight, slots):
    pixels = TILE * TILE
    rows = pixels * slots
    parts = len(tangent_parts)
    pad = (TILE + 2, TILE + 2, slots, CH)
    if parts == 2:
        out_shapes = [shape((rows, CH // 2), BF16)] * 2
    else:
        out_shapes = [shape((rows, CH), BF16)]
    outs = len(out_shapes)
    result = call(
        functools.partial(attention_kernel, parts, outs, len(weight)),
        "sssssvvhv" + "h" * parts + "h" * len(weight),
        "h" * (2 * outs) + "vv",
        out_shapes
        + grad_shapes(4, outs == 2)
        + [vector_shape(outs == 2), shape(pad, BF16)],
        [vmem((rows, CH), BF16)] * 7
        + [vmem((rows, CH), F32)] * 3
        + [vmem((CH // 128, slots * (pixels + PITCH), 128), F32), vmem((2, slots, CH), F32)]
        + [vmem((4, CH, CH), BF16), vmem((1, rows), jnp.int32), vmem((CH, CH), F32)]
        + [vmem((16, CH), F32)]
        + [vmem((slots // KEYS, QUERIES * pixels, KEYS * pixels), F32)] * 2
        + [vmem((2, QUERIES * pixels, CH), F32)]
        + [weight_sems(weight), pltpu.SemaphoreType.DMA((7,)), vmem((rows, CH), BF16)]
        + [vmem(part.shape, BF16) for part in grad_shapes(4, outs == 2)],
        "attention",
        30 << 30,
        24 << 20,
    )(
        position,
        *tables,
        par,
        normed,
        resid,
        stats3,
        *tangent_parts,
        *weight,
    )
    return result[:outs], result[outs : 2 * outs], result[2 * outs :]


def weight_grad_kernel(paired, first, extra, position, active, grad, *rest):
    outs = 2 if paired else 1
    extras, rest = rest[: outs if extra else 0], rest[outs if extra else 0 :]
    out_parts, (flipped, work, sem) = rest[:outs], rest[outs:]
    copies = []
    for half, part in enumerate(extras):
        for at in range(8):
            source = part.at[pl.ds(at * extra * BLOCK, extra * BLOCK)]
            target = out_parts[half].at[pl.ds(at * first * BLOCK, extra * BLOCK)]
            copies.append(pltpu.make_async_copy(source, target, sem.at[half, at]))
    for copy in copies:
        copy.start()
    slots = active.shape[2]
    wide = TILE * slots
    for row in range(TILE):
        left = grad[row + 1, 1 : TILE + 1].reshape(wide, CH)
        flipped[:, row * wide : (row + 1) * wide] = left.T

    def step(front, tap, carry):
        right = active[pl.ds(tap // 3, TILE), pl.ds(tap % 3, TILE)].reshape(TILE * wide, CH)
        total = jnp.dot(flipped[...], right, preferred_element_type=F32)
        store_grad(total, out_parts, work, position, tap + extra, first, 9 + extra, front)
        return carry

    if first > extra:
        lax.fori_loop(0, first - extra, functools.partial(step, True), 0)
    if first - extra < 9:
        lax.fori_loop(first - extra, 9, functools.partial(step, False), 0)
    for copy in copies:
        copy.wait()


def weight_grad(position, active, grad, paired, slots, name, first=9, extras=()):
    rows = TILE * TILE * slots
    extra = 4 if extras else 0
    shapes = grad_shapes(9 + extra, paired)
    return call(
        functools.partial(weight_grad_kernel, paired, first, extra),
        "svv" + "h" * len(extras),
        "v" * len(shapes),
        shapes,
        [
            vmem((CH, rows), BF16),
            vmem((CH, CH), F32),
            pltpu.SemaphoreType.DMA((2, 8)),
        ],
        name,
        2 * rows * CH * CH * 9,
        12 << 20,
    )(position, active, grad, *extras)


def swish_back(upstream, before):
    gate = sigmoid(before)
    return upstream * (gate + before * gate * (1.0 - gate))


def norm_back_sums(source, upstream, mean, inverse, gain, bias, slots):
    plains, crosseds = [], []
    for lanes in lanes_of(upstream.shape[2]):
        centre, factor = mean[:, lanes], inverse[:, lanes]
        slope, offset = gain[:, lanes], bias[:, lanes]

        def step(at, carry):
            plain, crossed = carry
            hat = (source(at, lanes) - centre) * factor
            grad = swish_back(upstream[at, :, lanes], hat * slope + offset)
            upstream[at, :, lanes] = grad
            return plain + grad, crossed + grad * hat

        zero = jnp.zeros((slots, 128), F32)
        plain, crossed = lax.fori_loop(0, TILE * TILE, step, (zero, zero), unroll=4)
        plains.append(plain)
        crosseds.append(crossed)
    return jnp.concatenate(plains, axis=1), jnp.concatenate(crosseds, axis=1)


def norm_back_apply(source, upstream, mean, inverse, gain, plain, crossed, put):
    for lanes in lanes_of(upstream.shape[2]):
        centre, factor = mean[:, lanes], inverse[:, lanes]
        slope = factor * gain[:, lanes]
        level = factor * plain[:, lanes]
        tilt = factor * factor * crossed[:, lanes]

        def step(at, carry):
            centred = source(at, lanes) - centre
            put(at, lanes, upstream[at, :, lanes] * slope - level - centred * tilt)
            return carry

        lax.fori_loop(0, TILE * TILE, step, 0, unroll=8)


def middle_kernel(count, position, slot_tile, slot_crop, par, stats2, pad_hbm, hidden_hbm, *rest):
    pieces, rest = rest[:count], rest[count:]
    pad_out_hbm, vecs_out = rest[:2]
    pad, weight, hidden, upstream, pad_out, vecs, totals, weight_sem, sem = rest[2:]
    slots = pad.shape[2]
    load_pad = pltpu.make_async_copy(pad_hbm, pad, sem.at[0])
    load_weight = WeightLoad(position, pieces, weight, weight_sem)
    load_hidden = pltpu.make_async_copy(hidden_hbm, hidden, sem.at[2])
    load_pad.start()
    load_weight.start()
    load_hidden.start()
    plan = Plan(position[0], slot_tile, slot_crop, slots)
    same = plan.same
    load_pad.wait()
    load_weight.wait()

    def step(row, carry):
        total = conv_rows(pad, weight, row, slots, NN, True)
        upstream[pl.ds(row * TILE, TILE)] = total.reshape(TILE, slots, CH)
        return carry

    lax.fori_loop(0, TILE, step, 0)
    load_hidden.wait()
    mean, inverse = stats2[0], stats2[1]
    gain, bias = par[G2 : G2 + 1, :], par[B2 : B2 + 1, :]

    def source(at, lanes):
        return hidden[at, :, lanes].astype(F32)

    plain, crossed = norm_back_sums(
        source, upstream, mean, inverse, gain, bias, slots
    )
    vecs[...] = jnp.zeros_like(vecs)
    vecs[G2 : G2 + 1, :] = jnp.sum(crossed, axis=0, keepdims=True)
    vecs[B2 : B2 + 1, :] = jnp.sum(plain, axis=0, keepdims=True)
    plain = crop_mean(same, plain * gain)
    crossed = crop_mean(same, crossed * gain)

    totals[...] = jnp.zeros_like(totals)

    def put(at, lanes, grad):
        rounded = grad.astype(BF16)
        pad_out[at // TILE + 1, at % TILE + 1, :, lanes] = rounded
        totals[:, lanes] += rounded.astype(F32)

    norm_back_apply(source, upstream, mean, inverse, gain, plain, crossed, put)
    vecs[C1 : C1 + 1, :] = jnp.sum(totals[...], axis=0, keepdims=True)
    store_vectors(vecs, vecs_out, position[0])
    fill_halo(pad_out, plan)
    save = pltpu.make_async_copy(pad_out, pad_out_hbm, sem.at[3])
    save.start()
    save.wait()


def middle(position, tables, par, stats2, pad, weight, hidden, slots):
    pixels = TILE * TILE
    rows = pixels * slots
    return call(
        functools.partial(middle_kernel, len(weight)),
        "sssvvhh" + "h" * len(weight),
        "hv",
        [shape(pad.shape, BF16), vector_shape(len(weight) > 1)],
        [
            vmem(pad.shape, BF16),
            vmem((9, CH, CH), BF16),
            vmem((pixels, slots, CH), BF16),
            vmem((pixels, slots, CH), F32),
            vmem(pad.shape, BF16),
            vmem((16, CH), F32),
            vmem((slots, CH), F32),
            weight_sems(weight),
            pltpu.SemaphoreType.DMA((4,)),
        ],
        "conv2_input_grad",
        2 * rows * CH * CH * 9,
        16 << 20,
    )(position, *tables[:2], par, stats2, pad, hidden, *weight)


def last_kernel(
    whose, count, position, slot_tile, slot_crop, par, stats1, vecs2, vecs3, *rest
):
    feats_hbm, pad_hbm, resid_hbm = rest[:3]
    pieces, rest = rest[3 : 3 + count], rest[3 + count :]
    out, vecs, pad, weight, feats, resid, upstream, weight_sem, sem = rest
    slots = pad.shape[2]
    width = upstream.shape[2]
    pixels = TILE * TILE
    me = position[0]
    columns = None
    span = pl.ds(0, width)
    if width < CH:
        columns = span = pl.ds(pl.multiple_of((me ^ whose) * width, width), width)
    load_weight = WeightLoad(position, pieces, weight, weight_sem, columns)
    load_pad = pltpu.make_async_copy(pad_hbm, pad, sem.at[0])
    inner = pl.ds(1, TILE)
    load_resid = pltpu.make_async_copy(resid_hbm.at[inner, inner, :, span], resid, sem.at[1])
    load_feats = pltpu.make_async_copy(feats_hbm.at[:, span], feats, sem.at[2])
    load_pad.start()
    load_weight.start()
    load_feats.start()
    load_resid.start()
    plan = Plan(me, slot_tile, slot_crop, slots)
    same = plan.same
    load_pad.wait()
    load_weight.wait()

    def step(row, carry):
        total = conv_rows(pad, weight, row, slots, NN, True)
        upstream[pl.ds(row * TILE, TILE)] = total.reshape(TILE, slots, width)
        return carry

    lax.fori_loop(0, TILE, step, 0)
    load_feats.wait()
    load_resid.wait()
    mean, inverse = stats1[0, :, span], stats1[1, :, span]
    gain, bias = par[G1 : G1 + 1, span], par[B1 : B1 + 1, span]

    def source(at, lanes):
        return feats[pl.ds(pl.multiple_of(at * slots, slots), slots), lanes].astype(F32)

    plain, crossed = norm_back_sums(source, upstream, mean, inverse, gain, bias, slots)
    vecs[...] = vecs2[...] + vecs3[...] if width == CH else vecs2[whose] + vecs3[whose]
    vecs[G1 : G1 + 1, :] = jnp.sum(crossed, axis=0, keepdims=True)
    vecs[B1 : B1 + 1, :] = jnp.sum(plain, axis=0, keepdims=True)
    plain = crop_mean(same, plain * gain)
    crossed = crop_mean(same, crossed * gain)

    def put(at, lanes, grad):
        rows = pl.ds(pl.multiple_of(at * slots, slots), slots)
        grad = resid[at // TILE, at % TILE, :, lanes].astype(F32) + grad
        out[rows, lanes] = grad.astype(out.dtype)

    norm_back_apply(source, upstream, mean, inverse, gain, plain, crossed, put)


def last(position, tables, par, stats1, vecs, feats, pad, weight, resid_grad, whose, slots):
    pixels = TILE * TILE
    rows = pixels * slots
    width = CH // 2 if len(weight) > 1 else CH
    return call(
        functools.partial(last_kernel, whose, len(weight)),
        "sssvvvvhhh" + "h" * len(weight),
        "vv",
        [
            shape((rows, width), F32 if width < CH and whose == 0 else BF16),
            shape((16, width), F32),
        ],
        [
            vmem(pad.shape, BF16),
            vmem((9, CH, width), BF16),
            vmem((rows, width), BF16),
            vmem((TILE, TILE, slots, width), BF16),
            vmem((pixels, slots, width), F32),
            weight_sems(weight),
            pltpu.SemaphoreType.DMA((3,)),
        ],
        "conv1_input_grad",
        2 * rows * CH * width * 9,
        10 << 20,
    )(position, *tables[:2], par, stats1, *vecs, feats, pad, resid_grad, *weight)


def after(value, *others):
    flat, tree = jax.tree.flatten(value)
    extra = jax.tree.leaves(others)
    held = lax.optimization_barrier(tuple(flat) + tuple(extra))
    return jax.tree.unflatten(tree, list(held[: len(flat)]))


def add(*terms):
    total = terms[0].astype(F32)
    for term in terms[1:]:
        total = total + term.astype(F32)
    return total


def swap(value, axis):
    return lax.ppermute(value, axis, [(0, 1), (1, 0)])


def to_all(value, axes, count):
    return lax.all_to_all(jnp.broadcast_to(value[None], (count,) + value.shape), axes, 0, 0)


QUAD = ("y", "near")


def from_quad(values):
    return [
        lax.ppermute(value, ("near", "y"), [(at, at ^ bits) for at in range(4)])
        for bits, value in zip((2, 1, 3), values)
    ]


def rounded_sum(terms):
    total = terms[0].astype(F32)
    for term in terms[1:]:
        total = total + term.astype(F32)
    return total.astype(BF16)


def vector_rows(vectors):
    rows, width = vectors.shape
    return jnp.pad(vectors.astype(BF16), ((0, BLOCK - rows), (0, CH - width)))


class Reduction:
    def __init__(self, halves, first, count):
        self.stage, self.first, self.count = 0, first, count
        self.state = (halves[0], halves[1], swap(halves[1], "core"))

    def advance(self, *others, vectors=None):
        if others:
            self.state = after(self.state, *others)
        self.stage += 1
        front = self.first * BLOCK
        back = (self.count - self.first) * BLOCK
        state = self.state
        if self.stage == 1:
            mine, _, came = state

            def part(begin, size):
                span = slice(begin, begin + size)
                return rounded_sum([mine[span], came[span]])

            start = 8 * front
            keep = part(0, 4 * front) if front else None, part(start, 2 * back)
            sent_front = part(4 * front, 4 * front) if front else None
            sent_back = [part(start + q * 2 * back, 2 * back) for q in (1, 2, 3)]
            came_front = swap(sent_front, "chan") if front else None
            self.state = keep, (came_front, from_quad(sent_back))
            return sent_front, sent_back
        if self.stage == 2:
            (mine_front, mine_back), (came_front, came_back) = state
            piece = [slice(q * front, (q + 1) * front) for q in range(4)]
            sent_front, keep_front = [], None
            if front:
                terms = [[mine_front[span], came_front[span]] for span in piece]
                keep_front, sent_front = terms[0], [rounded_sum(term) for term in terms[1:]]
            sent_back = rounded_sum([mine_back[back:]] + [value[back:] for value in came_back])
            if vectors is not None:
                sent_back = jnp.concatenate([sent_back, vector_rows(vectors)], axis=0)
            keep_back = [mine_back[:back]] + [value[:back] for value in came_back]
            self.state = keep_front, keep_back, (from_quad(sent_front), swap(sent_back, "chan"))
            return sent_front, sent_back
        if self.stage == 3:
            mine_front, mine_back, (came_front, came_back) = state
            parts = [rounded_sum(mine_front + came_front)] if front else []
            parts.append(rounded_sum(mine_back + [came_back[:back]]))
            if vectors is not None:
                parts.append(rounded_sum([vector_rows(vectors), came_back[back:]]))
            value = jnp.concatenate(parts, axis=0)
            self.state = value, swap(value, "far")
            return value
        if self.stage == 4:
            value = rounded_sum(list(state))
            self.state = [value] + from_quad([value] * 3)
            return value
        if self.stage == 5:
            mine = jnp.concatenate(state, axis=0)
            self.state = mine, swap(mine, "core")
            return mine

    @property
    def pieces(self):
        return list(self.state)


def assemble_kernel(sizes, position, mine, other, *outs):
    units = mine.shape[0] // (4 * BLOCK)
    vectors = None
    for number, part in enumerate((mine, other)):
        for at in range(4):
            row = ((position[1] ^ number) * 4 + (position[2] ^ at)) * BLOCK
            rows = pl.ds(pl.multiple_of(row, BLOCK), BLOCK)
            unit = 0
            for out, size in zip(outs, sizes):
                for index in range(max(size, 1)):
                    begin = (at * units + unit) * BLOCK
                    value = part[begin : begin + BLOCK, :].astype(F32)
                    if size:
                        out[index, rows, :] = value
                    else:
                        out[rows, :] = value
                    unit += 1
            if unit < units:
                begin = (at * units + unit) * BLOCK
                term = part[begin : begin + BLOCK, :].astype(F32)
                vectors = term if vectors is None else vectors + term
    if vectors is not None:
        outs[-1][...] = vectors


def assemble(position, pieces, sizes, vectors, name):
    shapes = [shape(((size,) if size else ()) + (8 * BLOCK, CH), F32) for size in sizes]
    if vectors:
        shapes.append(shape((BLOCK, CH), F32))
    return call(
        functools.partial(assemble_kernel, sizes),
        "svv",
        "v" * len(shapes),
        shapes,
        [],
        name,
        4 << 30,
        6 << 20,
    )(position, *pieces)


def body(
    paired,
    features,
    crop_ids,
    cotangent,
    norm1_gain,
    norm1_bias,
    conv1_weight,
    conv1_bias,
    norm2_gain,
    norm2_bias,
    conv2_weight,
    conv2_bias,
    norm3_gain,
    norm3_bias,
    query_weight,
    query_bias,
    key_weight,
    value_weight,
    value_bias,
    proj_weight,
    proj_bias,
):
    _, local, pixels = features.shape
    devices = lax.axis_size("chan")
    index = lax.axis_index("chan").astype(jnp.int32)
    tiles = pixels // (TILE * TILE)
    slots = tiles if devices == 1 else tiles // 2
    if paired:
        core, down, near = [lax.axis_index(a).astype(jnp.int32) for a in ("core", "y", "near")]
        quad = down * 2 + near
        piece = core * 4 + quad
    else:
        core = quad = jnp.int32(0)
    position = jnp.stack([index, core, quad])

    def exchange(parts):
        if paired:
            return [parts[0], swap(parts[1], "chan")]
        if devices == 2:
            parts = [jnp.where(index == 0, parts[k], parts[1 - k]) for k in range(2)]
        moved = lax.all_to_all(jnp.stack(parts), "chan", 0, 0)
        return [jnp.transpose(moved, (1, 0, 2)).reshape(moved.shape[1], CH)]

    def give_back(parts):
        if paired:
            return [parts[0], swap(parts[1], "chan")]
        whole = parts[0].reshape(parts[0].shape[0], devices, local)
        moved = lax.all_to_all(jnp.transpose(whole, (1, 0, 2)), "chan", 0, 0)
        parts = [moved[at] for at in range(devices)]
        if devices == 2:
            parts = [jnp.where(index == 0, parts[k], parts[1 - k]) for k in range(2)]
        return parts

    lanes = -(-local // 128) * 128

    def widened(signal):
        return jnp.pad(signal, ((0, lanes - local), (0, 0))) if lanes > local else signal

    def narrowed(parts):
        return [part[:, :local] for part in parts] if lanes > local else parts

    def unpack_lanes(parts, by_pixel, dtype, name):
        if lanes > local:
            parts = [jnp.pad(part, ((0, 0), (0, lanes - local))) for part in parts]
        whole = unpack(position, tables[0], parts, pixels, by_pixel, dtype, slots, name)
        return whole[:local]

    def vector_table(norm1_gain):
        return jnp.stack(
            [
                norm1_gain,
                norm1_bias,
                conv1_bias,
                norm2_gain,
                norm2_bias,
                conv2_bias,
                norm3_gain,
                norm3_bias,
                query_bias,
                value_bias,
                proj_bias,
            ]
            + [jnp.zeros_like(proj_bias)] * 5
        )

    small = jnp.stack([query_weight, key_weight, value_weight, proj_weight])
    if paired:
        eighth = local // 8
        part = lax.dynamic_slice_in_dim(conv1_weight, piece * eighth, eighth, 1)
        eighth1 = swap(part, "chan")
        part = lax.dynamic_slice_in_dim(conv2_weight, piece * eighth, eighth, 1)
        eighth2 = swap(part, "chan")
    else:
        par_parts = [lax.all_gather(vector_table(norm1_gain), "chan", axis=1, tiled=True)]
        weight1 = [lax.all_gather(conv1_weight, "chan", axis=1, tiled=True)]
    tables, packed = pack_first(
        position, crop_ids[0], widened(features[0]), devices, slots, "pack_features"
    )
    feature_parts = exchange(narrowed(packed))
    if paired:
        eighth1 = after(eighth1, packed[1])
        mine = to_all(eighth1, QUAD, 4)
        weight1 = [conv1_weight, mine, swap(mine, "core")]
        vectors = vector_table(after(norm1_gain, eighth1))
        par_parts = [vectors, swap(vectors, "chan")]
    packed = pack(
        position, tables[0], widened(cotangent[0]), False, devices, slots, "pack_cotangent"
    )
    packed = list(packed)
    if paired:
        part = lax.dynamic_slice_in_dim(small, core * (local // 2), local // 2, 1)
        eighth2, part = after((eighth2, part), feature_parts[1], weight1[1], packed[1])
        weight2 = [conv2_weight, to_all(eighth2, ("core",) + QUAD, 8)]
        own_small = swap(part, "chan")
    else:
        weight2 = [lax.all_gather(conv2_weight, "chan", axis=1, tiled=True)]
        weight3 = [lax.all_gather(small, "chan", axis=1, tiled=True)]
        tangent_parts = exchange(narrowed(packed))
    par, feats, pad1, hidden, pad2, stats1, stats2 = first(
        position, tables, par_parts, feature_parts, weight1, slots
    )
    if paired:
        own_small, packed[1] = after((own_small, packed[1]), pad2)
        tangent_parts = [packed[0], swap(packed[1], "chan")]
        weight3 = [small, own_small, swap(own_small, "core")]
    resid, normed, stats3 = second(position, tables, par, feats, pad2, weight2, slots)
    if paired:
        weight3 = after(weight3, normed)
    out_parts, small_grads, (vecs3, grad2) = attention(
        position, tables, par, normed, resid, stats3, tangent_parts, weight3, slots
    )
    out_parts = give_back(out_parts)
    if paired:
        resid_grad = grad2
        halves = weight_grad(
            position, pad2, grad2, True, slots, "conv2_weight_grad", 8, small_grads
        )
        chain2 = Reduction(halves, 8, 13)
        grad2 = after(grad2, halves[1])
        grad1, vecs2 = middle(position, tables, par, stats2, grad2, weight2, hidden, slots)
        back = functools.partial(last, position, tables, par, stats1, (vecs2, vecs3), feats)
        sent = chain2.advance(grad1, out_parts[1])
        halves = weight_grad(
            position, pad1, after(grad1, sent), True, slots, "conv1_weight_grad", 0
        )
        sent = chain2.advance(halves[1])
        chain1 = Reduction(after(halves, sent), 0, 9)
        grad1 = after(grad1, sent, halves[1])
        in_other, vecs_other = back(grad1, weight1, resid_grad, 1, slots)
        sent = chain1.advance(in_other, chain2.state), chain2.advance(in_other)
        in_got = swap(after(in_other, sent), "chan")
        grad1 = after(grad1, sent, in_other)
        in_own, vecs_own = back(grad1, weight1, resid_grad, 0, slots)
        sent = chain1.advance(in_own, vectors=vecs_other), chain2.advance(in_own)
        out_parts = after(out_parts, sent, in_own, in_got)
        output = unpack_lanes(out_parts, False, BF16, "unpack_output")
        sent = chain1.advance(output, vectors=vecs_own)
        in_parts = after([in_own, in_got], sent)
        input_grad = unpack_lanes(in_parts, True, F32, "unpack_input_grad")
        sent = chain1.advance(input_grad)
        sent = sent, chain2.advance(sent)
        small_grads = assemble(
            position, after(chain2.pieces, sent), [0, 0, 0, 0, 9], False, "conv2_grads"
        )
        small_grads, weight2_grad = small_grads[:4], small_grads[4]
        chain1.advance(weight2_grad)
        weight1_grad, vecs = assemble(position, chain1.pieces, [9], True, "conv1_grads")
        vecs = vecs[:16, :local]
    else:
        output = unpack_lanes(out_parts, False, BF16, "unpack_output")
        grads2 = weight_grad(position, pad2, grad2, False, slots, "conv2_weight_grad")
        grad1, vecs2 = middle(position, tables, par, stats2, grad2, weight2, hidden, slots)
        grads1 = weight_grad(position, pad1, grad1, False, slots, "conv1_weight_grad")
        in_all, vecs1 = last(
            position, tables, par, stats1, (vecs2, vecs3), feats, grad1, weight1, grad2, 0, slots
        )
        input_grad = unpack_lanes(give_back([in_all]), True, F32, "unpack_input_grad")

        def total(grad, axis):
            part = lax.psum_scatter(grad, "chan", scatter_dimension=axis, tiled=True)
            return lax.psum(part, "dp").astype(F32)

        small_grads, weight2_grad, weight1_grad = [
            total(g[0], 1) for g in (small_grads, grads2, grads1)
        ]
        vecs = total(vecs1, 1)
    gq, gk, gv, gp = small_grads if paired else [small_grads[k] for k in range(4)]
    return (
        output[None],
        input_grad[None],
        vecs[G1],
        vecs[B1],
        weight1_grad,
        vecs[C1],
        vecs[G2],
        vecs[B2],
        weight2_grad,
        vecs[C2],
        vecs[G3],
        vecs[B3],
        gq,
        vecs[QB],
        gk,
        gv,
        vecs[VB],
        gp,
        vecs[PB],
    )


def solution(mesh):
    paired = mesh.shape["dp"] == 16 and mesh.shape["chan"] == 2
    rows = "dp"
    if paired:
        rows = ("far", "near", "y", "core")
        mesh = jax.sharding.Mesh(mesh.devices.reshape((2,) * 5), rows + ("chan",))
    canvas = P(rows, "chan", None)
    vector = P("chan")
    conv = P(None, "chan", None)
    matrix = P("chan", None)
    placed = (
        (canvas, P(rows, None, None), canvas)
        + (vector, vector, conv, vector, vector, vector, conv, vector, vector, vector)
        + (matrix, vector, matrix, matrix, vector, matrix, vector)
    )
    results = (
        (canvas, canvas, vector, vector, conv, vector, vector, vector, conv, vector)
        + (vector, vector, matrix, vector, matrix, matrix, vector, matrix, vector)
    )
    return jax.shard_map(functools.partial(body, paired), mesh=mesh, in_specs=placed, out_specs=results, check_vma=False)
```
